128 devices in a mesh: sub: 16 (over y, x), lam: 8 (over z, core).
Axes of the slice: x: 4, y: 4, z: 4, core: 2. Of those that a mesh axis runs over, the one named last changes fastest.
Arguments:
- edge_field: bfloat16 [8, 65536, 128], P('lam', 'sub'), may hold values from -6 to 6
- coupling: float32 [8, 65536], P('lam', 'sub'), may hold values from 0.3 to 3
- owner_map: int32 [8, 65536, 1], P('lam', 'sub'), may hold values from 0 to 127; in each aligned block of 4096 rows (0 to 4095, 4096 to 8191, ..., all dimensions but the last counted through in order) at most 48 rows name the same one
- in_plane: bfloat16 [128, 128], replicated, may hold values from -0.5 to 0.5
- profile_op: bfloat16 [128, 128, 128], P(('sub', 'lam')), may hold values from -0.5 to 0.5
Outputs:
- field_next: float32 [8, 65536, 128], P('lam', 'sub')
The draws below stay inside these ranges and needn't reach their ends.
Inputs may be any that keep to these rules, and one draw needn't show every extreme that they name: `owner_map`: within the 4096 elements of one device no owner is named more than 48 times, a bound that some block reaches.
All inputs are finite; a program needn't handle non-finite values.
Results may differ from the reference program's by a relative error of at most 0.0018.
Values may be sent and summed in bfloat16 or wider, within the bound.
No kernel may reach another device: no remote copies, remote signals or barrier semaphores. Data moves between devices by JAX's collectives and lax.ppermute only.
A program may use at most 64 MiB of HBM per device.

```python
import math
import jax
import jax.numpy as jnp
import numpy as np
from jax import lax

PTS = 64
VALS = 128
ELEM_DEV = 4096
CAP = 48
STACKS = 8
CHAIN = 65536
DEVICES = 128


def shard_levels(key, shape, shards, least, largest):
    gain = 1.0
    for dim, parts in shards:
        heights = jax.random.uniform(jax.random.fold_in(jax.random.fold_in(key, 6), dim), (parts,), jnp.float32, least / len(shards), largest / len(shards))
        gain = gain * jnp.repeat(jnp.exp(heights), shape[dim] // parts).reshape((-1,) + (1,) * (len(shape) - 1 - dim))
    return gain


def assign_block(key, own, number, rows, amount, top, bound, skew):
    sequence = jax.random.permutation(key, amount)
    packed, ordinary = load_shares(amount, rows * top, bound, skew, True), load_shares(amount, rows * top, bound, skew, False)
    places = jnp.arange(amount)

    def named(sizes, offset_by):
        used = int((sizes > 0).sum())
        fixed = max(1, used // 4)
        passed = fixed + (places - fixed + offset_by * (used - fixed)) % max(1, amount - fixed)
        return jnp.zeros((amount,), jnp.int32).at[sequence[jnp.where(places < fixed, places, passed)]].set(jnp.asarray(sizes, jnp.int32))

    sizes = jnp.where(number % 4 == 0, named(packed, number // 4), named(ordinary, number - number // 4 - 1))
    mixed = jax.random.permutation(jax.random.fold_in(own, 3), amount)
    giver, receiver = mixed[0:amount // 2 * 2:2], mixed[1:amount // 2 * 2:2]
    margin = jnp.minimum(sizes[giver] - 1, bound - sizes[receiver]) // 2
    margin = jnp.where((giver == sequence[0]) | (receiver == sequence[0]) | (sizes[receiver] == 0), 0, jnp.maximum(margin, 0))
    passed = jax.random.randint(jax.random.fold_in(own, 4), (amount // 2,), 0, 1 << 20) % (margin + 1)
    sizes = sizes.at[giver].add(-passed).at[receiver].add(passed)
    labels = jnp.searchsorted(jnp.cumsum(sizes), jnp.arange(rows * top), side="right").astype(jnp.int32)
    listing = labels.reshape(top, rows).T
    listing = listing[jax.random.permutation(jax.random.fold_in(own, 1), rows)]
    offset_by = jax.random.randint(jax.random.fold_in(own, 2), (rows, 1), 0, top)
    return jnp.take_along_axis(listing, (jnp.arange(top)[None, :] + offset_by) % top, axis=1)


def load_shares(amount, total, reach, skew, full):
    weights = [(1 << 20) // math.isqrt(grade ** skew) + 1 for grade in range(1, amount + 1)]
    largest = reach if full else min(reach, max(-(-total // amount), total * weights[0] // sum(weights)))
    least = 1 if total - largest >= amount - 1 else 0
    counts, rest = [largest] + [least] * (amount - 1), total - largest - least * (amount - 1)
    while rest > 0:
        candidates = [i for i in range(1, amount) if counts[i] < largest] or [i for i in range(1, amount) if counts[i] < reach]
        mass, remaining = sum([weights[i] for i in candidates]), rest
        for i in candidates:
            more = min(reach - counts[i], max(1, remaining * weights[i] // mass), rest)
            counts[i] = counts[i] + more
            rest = rest - more
    return np.array(counts)


def scatter_about(key, shape, deviation, bound, shards=(), kind=jnp.bfloat16):
    result = deviation * jax.random.normal(key, shape, jnp.float32)
    if shards:
        result = result * shard_levels(key, shape, shards, -0.22, 0.18)
    return jnp.clip(result, -bound, bound).astype(kind)


def setup_inputs(seed: int = 0) -> dict:
    arg_keys = jax.random.split(jax.random.key(seed), 6)
    edge_field = scatter_about(arg_keys[0], (STACKS, CHAIN, VALS), 1.0, 6.0, ((0, 8), (1, 16)))
    coupling = jnp.clip(jnp.exp(math.log(3.0) - 2.3025851 * jax.random.uniform(arg_keys[1], (STACKS, CHAIN), jnp.float32) ** shard_levels(arg_keys[1], (STACKS, CHAIN), ((0, 8), (1, 16)), -0.2, 0.2)), 0.3, 3.0)
    owner_map_keys = jax.random.split(jax.random.fold_in(arg_keys[2], 1), STACKS * CHAIN // ELEM_DEV)
    owner_map_turns = jax.random.permutation(jax.random.fold_in(arg_keys[2], 3), STACKS * CHAIN // ELEM_DEV)
    owner_map = jax.vmap(lambda own, number: assign_block(jax.random.fold_in(arg_keys[2], 2), own, number, ELEM_DEV, DEVICES, 1, CAP, 2))(owner_map_keys, owner_map_turns).reshape((STACKS, CHAIN, 1))
    in_plane = scatter_about(arg_keys[3], (VALS, VALS), VALS ** -0.5, 0.5)
    profile_op = scatter_about(arg_keys[4], (DEVICES, VALS, VALS), VALS ** -0.5, 0.5, ((0, 128),))
    return dict(edge_field=edge_field, coupling=coupling, owner_map=owner_map, in_plane=in_plane, profile_op=profile_op)


step_size = 0.25


def profile_response(response_raw):
    real_part = response_raw[:, :PTS]
    imag_part = response_raw[:, PTS:]
    magnitude = real_part * real_part + imag_part * imag_part
    reluct = 1.0 + 4.0 * magnitude / (1.0 + magnitude)
    return (response_raw * jnp.concatenate([reluct, reluct], axis=1)).astype(jnp.bfloat16)


def reference(edge_field, coupling, owner_map, in_plane, profile_op):
    element_rows = edge_field.reshape(-1, VALS)
    owner_ids = owner_map.reshape(-1).astype(jnp.int32)
    total_rows = element_rows.shape[0]
    ordering = jnp.argsort(owner_ids, stable=True).astype(jnp.int32)
    sorted_owner = owner_ids[ordering]
    owner_counts = jnp.bincount(owner_ids, length=DEVICES).astype(jnp.int32)
    owner_starts = (jnp.cumsum(owner_counts) - owner_counts).astype(jnp.int32)
    block_rows = DEVICES * CAP
    padded_rows = jnp.concatenate([element_rows[ordering], jnp.zeros((block_rows, VALS), element_rows.dtype)], axis=0)

    def per_owner(owner_idx):
        owner_block = lax.dynamic_slice_in_dim(padded_rows, owner_starts[owner_idx], block_rows, 0)
        response_raw = jnp.dot(owner_block, profile_op[owner_idx], preferred_element_type=jnp.float32)
        return profile_response(response_raw)

    blocks = lax.map(per_owner, jnp.arange(DEVICES, dtype=jnp.int32))
    positions = (jnp.arange(total_rows, dtype=jnp.int32) - owner_starts[sorted_owner]).astype(jnp.int32)
    sorted_effect = blocks[sorted_owner, positions]
    effective = jnp.zeros_like(sorted_effect).at[ordering].set(sorted_effect)
    effective = effective.reshape(STACKS, CHAIN, VALS)
    padded_field = jnp.pad(edge_field, ((0, 0), (1, 1), (0, 0)))
    projected = jnp.dot(padded_field.reshape(-1, VALS), in_plane, preferred_element_type=jnp.float32)
    projected = projected.reshape(STACKS, CHAIN + 2, VALS)
    stiffness = coupling[:, :, None] * (2.0 * projected[:, 1:-1] - projected[:, :-2] - projected[:, 2:])
    return edge_field.astype(jnp.float32) - step_size * (stiffness + effective.astype(jnp.float32))
```

```python
import functools

import jax
import jax.numpy as jnp
import numpy as np
from jax import lax
from jax.experimental import pallas as pl
from jax.experimental.pallas import tpu as pltpu
from jax.sharding import PartitionSpec as P

step_size = 0.25
axes_all = ("sub", "lam")
owners = 128
cap = 48
rows = 4096
vals = 128
slots = owners * cap
chunk = 256
offsets = np.array([0, -1, 1, 2])
vmem_bytes = 40 * 1024 * 1024


def params():
    return pltpu.CompilerParams(vmem_limit_bytes=vmem_bytes)


def device(y, x, z, c):
    return ((y % 4) * 4 + (x % 4)) * 8 + (z % 4) * 2 + (c % 2)


def shifted(value, step, axes):
    pairs = []
    for y in range(4):
        for x in range(4):
            for z in range(4):
                for c in range(2):
                    place = dict(y=y, x=x, z=z, c=c)
                    place[axes[c]] += step
                    pairs.append((device(y, x, z, c), device(**place)))
    return lax.ppermute(value, axes_all, pairs)


def core_swap(value):
    pairs = [(d, d ^ 1) for d in range(owners)]
    return lax.ppermute(value, axes_all, pairs)


def around(value, axes):
    return [value] + [shifted(value, step, axes) for step in (1, -1, 2)]


def gather_operators(block):
    near = jnp.concatenate(around(block, "zz"), axis=0)
    plane = jnp.concatenate(around(near, "xy"), axis=0)
    parts = around(plane, "yx")
    return [(part, core_swap(part)) for part in parts]


def slot_owners():
    sub, lam = lax.axis_index("sub"), lax.axis_index("lam")
    y, x, z, c = sub // 4, sub % 4, lam // 2, lam % 2
    index = np.arange(owners)
    third, group = index // 32, (index // 16) % 2
    second, first = (index // 4) % 4, index % 4
    core = jnp.asarray(group, jnp.int32) ^ c
    by_second = jnp.asarray(offsets[second], jnp.int32)
    by_third = jnp.asarray(offsets[third], jnp.int32)
    even = core == 0
    dx = jnp.where(even, by_second, by_third)
    dy = jnp.where(even, by_third, by_second)
    dz = jnp.asarray(offsets[first], jnp.int32)
    return (((y + dy + 4) % 4) * 4 + (x + dx + 4) % 4) * 8 + ((z + dz + 4) % 4) * 2 + core


def rank_kernel(owner_ref, table_ref, slot_ref):
    table = table_ref[...]
    row = lax.broadcasted_iota(jnp.int32, (chunk, chunk + owners), 0)
    col = lax.broadcasted_iota(jnp.int32, (chunk, chunk + owners), 1)
    earlier = jnp.where((row < col) | (col >= chunk), 1.0, 0.0).astype(jnp.bfloat16)
    start = cap * lax.broadcasted_iota(jnp.int32, (owners, owners), 0).astype(jnp.float32)
    for j in range(rows // chunk):
        hit = table == owner_ref[j : j + 1, :]
        count = jnp.dot(
            jnp.where(hit, 1.0, 0.0).astype(jnp.bfloat16), earlier, preferred_element_type=jnp.float32
        )
        place = count[:, :chunk] + jnp.concatenate([start, start], axis=1)
        slot = jnp.sum(jnp.where(hit, place, 0.0), axis=0, keepdims=True)
        slot_ref[j : j + 1, :] = slot.astype(jnp.int32)
        start = start + count[:, chunk:]


def rank(owner, table):
    return pl.pallas_call(
        rank_kernel,
        out_shape=jax.ShapeDtypeStruct((rows // chunk, chunk), jnp.int32),
        compiler_params=params(),
        cost_estimate=pl.CostEstimate(flops=2 * 128 * 4096 * 384, bytes_accessed=100000, transcendentals=0),
    )(owner, table)


def sort_kernel(slot_ref, field_ref, sorted_ref, wide, placed):
    wide[...] = field_ref[...].astype(jnp.float32)

    def body(i, carry):
        first = pl.multiple_of(i * 32, 32)
        for j in range(32):
            placed[pl.ds(slot_ref[first + j], 1), :] = wide[pl.ds(first + j, 1), :]
        return carry

    lax.fori_loop(0, rows // 32, body, 0)
    sorted_ref[...] = placed[...].astype(jnp.bfloat16)


def sort_rows(slot, field):
    return pl.pallas_call(
        sort_kernel,
        in_specs=[pl.BlockSpec(memory_space=pltpu.SMEM), pl.BlockSpec(memory_space=pltpu.VMEM)],
        out_shape=jax.ShapeDtypeStruct((slots, vals), jnp.bfloat16),
        scratch_shapes=[pltpu.VMEM((rows, vals), jnp.float32), pltpu.VMEM((slots, vals), jnp.float32)],
        compiler_params=params(),
        cost_estimate=pl.CostEstimate(flops=0, bytes_accessed=20000000, transcendentals=0),
    )(slot, field)


def stencil_kernel(field_ref, halo_ref, coupling_ref, plane_ref, base_ref, projected):
    plane = plane_ref[...]
    ends = jnp.dot(halo_ref[...], plane, preferred_element_type=jnp.float32)
    projected[0:8, :] = ends[0:8]
    projected[rows + 8 : rows + 16, :] = ends[8:16]
    for j in range(rows // 512):
        projected[8 + j * 512 : 8 + (j + 1) * 512, :] = jnp.dot(
            field_ref[j * 512 : (j + 1) * 512, :], plane, preferred_element_type=jnp.float32
        )
    for j in range(rows // vals):
        lo = j * vals
        weight = jnp.broadcast_to(coupling_ref[j : j + 1, :], (vals, vals)).T
        here = projected[lo + 8 : lo + 8 + vals, :]
        before = projected[lo + 7 : lo + 7 + vals, :]
        after = projected[lo + 9 : lo + 9 + vals, :]
        field = field_ref[lo : lo + vals, :].astype(jnp.float32)
        base_ref[lo : lo + vals, :] = field - step_size * (weight * (2.0 * here - before - after))


def stencil(field, halo, coupling, plane):
    return pl.pallas_call(
        stencil_kernel,
        out_shape=jax.ShapeDtypeStruct((rows, vals), jnp.float32),
        scratch_shapes=[pltpu.VMEM((rows + 16, vals), jnp.float32)],
        compiler_params=params(),
        cost_estimate=pl.CostEstimate(flops=2 * 4096 * 128 * 128, bytes_accessed=10000000, transcendentals=0),
    )(field, halo, coupling, plane)


def respond(block, operator):
    response = jnp.dot(block, operator, preferred_element_type=jnp.float32)
    square = response * response
    magnitude = square + pltpu.roll(square, vals // 2, 1)
    reluct = 5.0 - 4.0 / (1.0 + magnitude)
    return reluct * response


def effect_kernel(*refs):
    sorted_ref, near_ref, far_ref = refs[:3]
    effect_ref = refs[-1]
    for g, operator_ref in enumerate((near_ref, far_ref)):
        for k in range(16):
            lo = (g * 16 + k) * cap
            effect_ref[lo : lo + cap, :] = respond(
                sorted_ref[lo : lo + cap, :], operator_ref[k * vals : (k + 1) * vals, :]
            )


def effects(sorted_rows, near, far, number, previous):
    block = 32 * cap
    whole = pl.BlockSpec((16 * vals, vals), lambda i: (0, 0))
    specs = [pl.BlockSpec((block, vals), lambda i: (number, 0)), whole, whole]
    operands = [sorted_rows, near, far]
    if previous is not None:
        specs.append(pl.BlockSpec(memory_space=pl.ANY))
        operands.append(previous)
    return pl.pallas_call(
        effect_kernel,
        grid=(1,),
        in_specs=specs,
        out_specs=pl.BlockSpec((block, vals), lambda i: (number, 0)),
        out_shape=jax.ShapeDtypeStruct((slots, vals), jnp.float32),
        input_output_aliases={} if previous is None else {3: 0},
        compiler_params=params(),
        cost_estimate=pl.CostEstimate(
            flops=2 * block * 128 * 128, bytes_accessed=4000000, transcendentals=0
        ),
    )(*operands)


def combine_kernel(slot_ref, effect_ref, base_ref, out_ref):
    top = pl.program_id(0) * 512

    def body(i, carry):
        first = pl.multiple_of(i * 32, 32)
        for j in range(32):
            effect = effect_ref[pl.ds(slot_ref[top + first + j], 1), :]
            out_ref[pl.ds(first + j, 1), :] = base_ref[pl.ds(first + j, 1), :] - step_size * effect
        return carry

    lax.fori_loop(0, 512 // 32, body, 0)


def combine(slot, effect, base):
    part = pl.BlockSpec((512, vals), lambda i: (i, 0))
    return pl.pallas_call(
        combine_kernel,
        grid=(rows // 512,),
        in_specs=[
            pl.BlockSpec(memory_space=pltpu.SMEM),
            pl.BlockSpec((slots, vals), lambda i: (0, 0)),
            part,
        ],
        out_specs=part,
        out_shape=jax.ShapeDtypeStruct((rows, vals), jnp.float32),
        compiler_params=params(),
        cost_estimate=pl.CostEstimate(flops=4096 * 128, bytes_accessed=10000000, transcendentals=0),
    )(slot, effect, base)


def halo_rows(field):
    ends = lax.axis_size("sub") - 1
    before = lax.ppermute(field[rows - 16 :], "sub", [(i, i + 1) for i in range(ends)])
    after = lax.ppermute(field[:16], "sub", [(i + 1, i) for i in range(ends)])
    return jnp.concatenate([before[8:], after[:8]], axis=0)


def per_device(edge_field, coupling, owner_map, in_plane, profile_op):
    field = edge_field[0]
    parts = gather_operators(profile_op[0])
    table = slot_owners()[:, None]
    slot = rank(owner_map.reshape(rows // chunk, chunk), table).reshape(rows)
    sorted_rows = sort_rows(slot, field)
    base = stencil(field, halo_rows(field), coupling.reshape(rows // vals, vals), in_plane)
    effect = None
    for number, (near, far) in enumerate(parts):
        effect = effects(sorted_rows, near, far, number, effect)
    return combine(slot, effect, base)[None]


def solution(mesh):
    placed = (
        P("lam", "sub", None),
        P("lam", "sub"),
        P("lam", "sub", None),
        P(),
        P(("sub", "lam"), None, None),
    )
    return jax.shard_map(
        per_device, mesh=mesh, in_specs=placed, out_specs=P("lam", "sub", None), check_vma=False
    )
```

```python
import functools

import jax
import jax.numpy as jnp
import numpy as np
from jax import lax
from jax.experimental import pallas as pl
from jax.experimental.pallas import tpu as pltpu
from jax.sharding import PartitionSpec as P

step_size = 0.25
axes_all = ("sub", "lam")
owners = 128
cap = 48
rows = 4096
vals = 128
slots = owners * cap
chunk = 256
offsets = np.array([0, 2, -1, 1])
vmem_bytes = 40 * 1024 * 1024


def params():
    return pltpu.CompilerParams(vmem_limit_bytes=vmem_bytes)


def device(y, x, z, c):
    return ((y % 4) * 4 + (x % 4)) * 8 + (z % 4) * 2 + (c % 2)


def shifted(value, step, axes):
    pairs = []
    for y in range(4):
        for x in range(4):
            for z in range(4):
                for c in range(2):
                    place = dict(y=y, x=x, z=z, c=c)
                    place[axes[c]] += step
                    pairs.append((device(y, x, z, c), device(**place)))
    return lax.ppermute(value, axes_all, pairs)


def core_swap(value):
    pairs = [(d, d ^ 1) for d in range(owners)]
    return lax.ppermute(value, axes_all, pairs)


def around(value, axes):
    return [value] + [shifted(value, step, axes) for step in (2, 1, -1)]


def slot_owners():
    sub, lam = lax.axis_index("sub"), lax.axis_index("lam")
    y, x, z, c = sub // 4, sub % 4, lam // 2, lam % 2
    index = np.arange(owners)
    third, group = index // 32, (index // 16) % 2
    second, first = (index // 4) % 4, index % 4
    core = jnp.asarray(group, jnp.int32) ^ c
    by_second = jnp.asarray(offsets[second], jnp.int32)
    by_third = jnp.asarray(offsets[third], jnp.int32)
    even = core == 0
    dx = jnp.where(even, by_second, by_third)
    dy = jnp.where(even, by_third, by_second)
    dz = jnp.asarray(offsets[first], jnp.int32)
    return (((y + dy + 4) % 4) * 4 + (x + dx + 4) % 4) * 8 + ((z + dz + 4) % 4) * 2 + core


def rank_kernel(owner_ref, table_ref, slot_ref):
    table = table_ref[...]
    row = lax.broadcasted_iota(jnp.int32, (chunk, chunk + owners), 0)
    col = lax.broadcasted_iota(jnp.int32, (chunk, chunk + owners), 1)
    earlier = jnp.where((row < col) | (col >= chunk), 1.0, 0.0).astype(jnp.bfloat16)
    start = cap * lax.broadcasted_iota(jnp.int32, (owners, owners), 0).astype(jnp.float32)
    for j in range(rows // chunk):
        hit = table == owner_ref[j : j + 1, :]
        count = jnp.dot(
            jnp.where(hit, 1.0, 0.0).astype(jnp.bfloat16), earlier, preferred_element_type=jnp.float32
        )
        place = count[:, :chunk] + jnp.concatenate([start, start], axis=1)
        slot = jnp.sum(jnp.where(hit, place, 0.0), axis=0, keepdims=True)
        slot_ref[j : j + 1, :] = slot.astype(jnp.int32)
        start = start + count[:, chunk:]


def rank(owner, table):
    return pl.pallas_call(
        rank_kernel,
        out_shape=jax.ShapeDtypeStruct((rows // chunk, chunk), jnp.int32),
        compiler_params=params(),
        cost_estimate=pl.CostEstimate(flops=2 * 128 * 4096 * 384, bytes_accessed=100000, transcendentals=0),
    )(owner, table)


def sort_kernel(slot_ref, field_ref, sorted_ref, wide, placed):
    wide[...] = field_ref[...].astype(jnp.float32)

    def body(i, carry):
        first = pl.multiple_of(i * 32, 32)
        for j in range(32):
            placed[pl.ds(slot_ref[first + j], 1), :] = wide[pl.ds(first + j, 1), :]
        return carry

    lax.fori_loop(0, rows // 32, body, 0)
    sorted_ref[...] = placed[...].astype(jnp.bfloat16)


def sort_rows(slot, field):
    return pl.pallas_call(
        sort_kernel,
        in_specs=[pl.BlockSpec(memory_space=pltpu.SMEM), pl.BlockSpec(memory_space=pltpu.VMEM)],
        out_shape=jax.ShapeDtypeStruct((slots, vals), jnp.bfloat16),
        scratch_shapes=[pltpu.VMEM((rows, vals), jnp.float32), pltpu.VMEM((slots, vals), jnp.float32)],
        compiler_params=params(),
        cost_estimate=pl.CostEstimate(flops=0, bytes_accessed=20000000, transcendentals=0),
    )(slot, field)


def stencil_kernel(field_ref, halo_ref, coupling_ref, plane_ref, base_ref, projected):
    plane = plane_ref[...]
    ends = jnp.dot(halo_ref[...], plane, preferred_element_type=jnp.float32)
    projected[0:8, :] = ends[0:8]
    projected[rows + 8 : rows + 16, :] = ends[8:16]
    for j in range(rows // 512):
        projected[8 + j * 512 : 8 + (j + 1) * 512, :] = jnp.dot(
            field_ref[j * 512 : (j + 1) * 512, :], plane, preferred_element_type=jnp.float32
        )
    for j in range(rows // vals):
        lo = j * vals
        weight = jnp.broadcast_to(coupling_ref[j : j + 1, :], (vals, vals)).T
        here = projected[lo + 8 : lo + 8 + vals, :]
        before = projected[lo + 7 : lo + 7 + vals, :]
        after = projected[lo + 9 : lo + 9 + vals, :]
        field = field_ref[lo : lo + vals, :].astype(jnp.float32)
        base_ref[lo : lo + vals, :] = field - step_size * (weight * (2.0 * here - before - after))


def stencil(field, halo, coupling, plane):
    return pl.pallas_call(
        stencil_kernel,
        out_shape=jax.ShapeDtypeStruct((rows, vals), jnp.float32),
        scratch_shapes=[pltpu.VMEM((rows + 16, vals), jnp.float32)],
        compiler_params=params(),
        cost_estimate=pl.CostEstimate(flops=1000, bytes_accessed=1000, transcendentals=0),
    )(field, halo, coupling, plane)


def respond(block, operator):
    response = jnp.dot(block, operator, preferred_element_type=jnp.float32)
    square = response * response
    magnitude = square + pltpu.roll(square, vals // 2, 1)
    reluct = 5.0 - 4.0 / (1.0 + magnitude)
    return reluct * response


def effect_block(sorted_ref, operator_ref, effect_ref, block):
    for k in range(16):
        lo = (block * 16 + k) * cap
        effect_ref[lo : lo + cap, :] = respond(
            sorted_ref[lo : lo + cap, :], operator_ref[k * vals : (k + 1) * vals, :]
        )


def effect_kernel(blocks, *refs):
    sorted_ref, effect_ref = refs[0], refs[-1]
    for block, operator_ref in zip(blocks, refs[1:]):
        effect_block(sorted_ref, operator_ref, effect_ref, block)


in_vmem = pl.BlockSpec(memory_space=pltpu.VMEM)


def effects(sorted_rows, operators, blocks, previous):
    operands = [sorted_rows, *operators]
    if previous is not None:
        operands.append(previous)
    return pl.pallas_call(
        functools.partial(effect_kernel, blocks),
        in_specs=[in_vmem] * len(operands),
        out_specs=in_vmem,
        out_shape=jax.ShapeDtypeStruct((slots, vals), jnp.float32),
        input_output_aliases={} if previous is None else {len(operands) - 1: 0},
        compiler_params=params(),
        cost_estimate=pl.CostEstimate(flops=1000, bytes_accessed=1000, transcendentals=0),
    )(*operands)


part_rows = 512


def final_kernel(blocks, slot_ref, base_ref, sorted_ref, *refs):
    operators, (_, out_ref, effect_ref, result, sent) = refs[:-5], refs[-5:]
    for block, operator_ref in zip(blocks, operators):
        effect_block(sorted_ref, operator_ref, effect_ref, block)

    def copy(part):
        span = pl.ds(pl.multiple_of(part * part_rows, part_rows), part_rows)
        return pltpu.make_async_copy(result.at[span], out_ref.at[span], sent.at[part])

    for part in range(rows // part_rows):

        def body(i, carry):
            first = pl.multiple_of(part * part_rows + i * 32, 32)
            for j in range(32):
                effect = effect_ref[pl.ds(slot_ref[first + j], 1), :]
                row = pl.ds(first + j, 1)
                result[row, :] = base_ref[row, :] - step_size * effect
            return carry

        lax.fori_loop(0, part_rows // 32, body, 0)
        copy(part).start()
    for part in range(rows // part_rows):
        copy(part).wait()


def finish(slot, base, sorted_rows, operators, blocks, previous):
    operands = [slot, base, sorted_rows, *operators, previous]
    return pl.pallas_call(
        functools.partial(final_kernel, blocks),
        in_specs=[pl.BlockSpec(memory_space=pltpu.SMEM)] + [in_vmem] * (len(operands) - 1),
        out_specs=[pl.BlockSpec(memory_space=pl.ANY), in_vmem],
        out_shape=[
            jax.ShapeDtypeStruct((rows, vals), jnp.float32),
            jax.ShapeDtypeStruct((slots, vals), jnp.float32),
        ],
        input_output_aliases={len(operands) - 1: 1},
        scratch_shapes=[
            pltpu.VMEM((rows, vals), jnp.float32),
            pltpu.SemaphoreType.DMA((rows // part_rows,)),
        ],
        compiler_params=params(),
        cost_estimate=pl.CostEstimate(flops=4096 * 128, bytes_accessed=10000000, transcendentals=0),
    )(*operands)[0]


def halo_rows(field):
    ends = lax.axis_size("sub") - 1
    before = lax.ppermute(field[rows - 16 :], "sub", [(i, i + 1) for i in range(ends)])
    after = lax.ppermute(field[:16], "sub", [(i + 1, i) for i in range(ends)])
    return jnp.concatenate([before[8:], after[:8]], axis=0)


def per_device(edge_field, coupling, owner_map, in_plane, profile_op):
    field = edge_field[0]
    tied = lax.optimization_barrier
    near = jnp.concatenate(around(profile_op[0], "zz"), axis=0)
    table = slot_owners()[:, None]
    slot = rank(owner_map.reshape(rows // chunk, chunk), table).reshape(rows)
    near, slot = tied((near, slot))
    plane = jnp.concatenate(around(near, "xy"), axis=0)
    sorted_rows = sort_rows(slot, field)
    plane, sorted_rows = tied((plane, sorted_rows))
    own, *others = around(plane, "yx")
    effect = effects(sorted_rows, [own, core_swap(own)], (0, 1), None)
    base = stencil(field, halo_rows(field), coupling.reshape(rows // vals, vals), in_plane)
    *others, effect, base = tied((*others, effect, base))
    effect = effects(sorted_rows, others, (2, 4, 6), effect)
    far = [core_swap(part) for part in others]
    return finish(slot, base, sorted_rows, far, (3, 5, 7), effect)[None]


def solution(mesh):
    placed = (
        P("lam", "sub", None),
        P("lam", "sub"),
        P("lam", "sub", None),
        P(),
        P(("sub", "lam"), None, None),
    )
    return jax.shard_map(
        per_device, mesh=mesh, in_specs=placed, out_specs=P("lam", "sub", None), check_vma=False
    )
```

```python
import functools

import jax
import jax.numpy as jnp
import numpy as np
from jax import lax
from jax.experimental import pallas as pl
from jax.experimental.pallas import tpu as pltpu
from jax.sharding import PartitionSpec as P

step_size = 0.25
axes_all = ("sub", "lam")
owners = 128
cap = 48
rows = 4096
vals = 128
slots = owners * cap
chunk = 256
unroll = 128
group = 4 * vals
stride = group + 16
offsets = np.array([0, 2, -1, 1])
vmem_bytes = 20 * 1024 * 1024


in_vmem = pl.BlockSpec(memory_space=pltpu.VMEM)


def params():
    return pltpu.CompilerParams(vmem_limit_bytes=vmem_bytes)


def device(y, x, z, c):
    return ((y % 4) * 4 + (x % 4)) * 8 + (z % 4) * 2 + (c % 2)


def shifted(value, step, axes):
    pairs = []
    for y in range(4):
        for x in range(4):
            for z in range(4):
                for c in range(2):
                    place = dict(y=y, x=x, z=z, c=c)
                    place[axes[c]] += step
                    pairs.append((device(y, x, z, c), device(**place)))
    return lax.ppermute(value, axes_all, pairs)


def core_swap(value):
    pairs = [(d, d ^ 1) for d in range(owners)]
    return lax.ppermute(value, axes_all, pairs)


def swap_pieces(value):
    return [core_swap(value[i : i + group]) for i in range(0, value.shape[0], stride)]


def around(value, axes):
    return [value] + [shifted(value, step, axes) for step in (2, 1, -1)]


def slot_owners():
    sub, lam = lax.axis_index("sub"), lax.axis_index("lam")
    y, x, z, c = sub // 4, sub % 4, lam // 2, lam % 2
    index = np.arange(owners)
    third, group = index // 32, (index // 16) % 2
    second, first = (index // 4) % 4, index % 4
    core = jnp.asarray(group, jnp.int32) ^ c
    by_second = jnp.asarray(offsets[second], jnp.int32)
    by_third = jnp.asarray(offsets[third], jnp.int32)
    even = core == 0
    dx = jnp.where(even, by_second, by_third)
    dy = jnp.where(even, by_third, by_second)
    dz = jnp.asarray(offsets[first], jnp.int32)
    return (((y + dy + 4) % 4) * 4 + (x + dx + 4) % 4) * 8 + ((z + dz + 4) % 4) * 2 + core


def rank_kernel(owner_ref, table_ref, slot_ref):
    table = table_ref[...]
    row = lax.broadcasted_iota(jnp.int32, (chunk, chunk + owners), 0)
    col = lax.broadcasted_iota(jnp.int32, (chunk, chunk + owners), 1)
    earlier = jnp.where((row < col) | (col >= chunk), 1.0, 0.0).astype(jnp.bfloat16)
    start = cap * lax.broadcasted_iota(jnp.int32, (owners, owners), 0).astype(jnp.float32)
    for j in range(rows // chunk):
        hit = table == owner_ref[j : j + 1, :]
        count = jnp.dot(
            jnp.where(hit, 1.0, 0.0).astype(jnp.bfloat16), earlier, preferred_element_type=jnp.float32
        )
        place = count[:, :chunk] + jnp.concatenate([start, start], axis=1)
        slot = jnp.sum(jnp.where(hit, place, 0.0), axis=0, keepdims=True)
        slot_ref[j : j + 1, :] = slot.astype(jnp.int32)
        start = start + count[:, chunk:]


def rank(owner, table):
    return pl.pallas_call(
        rank_kernel,
        out_shape=jax.ShapeDtypeStruct((rows // chunk, chunk), jnp.int32),
        compiler_params=params(),
        cost_estimate=pl.CostEstimate(flops=2 * 128 * 4096 * 384, bytes_accessed=100000, transcendentals=0),
    )(owner, table)


def sort_kernel(slot_ref, field_ref, sorted_ref, wide, placed):
    wide[...] = field_ref[...].astype(jnp.float32)

    def body(i, carry):
        first = pl.multiple_of(i * unroll, unroll)
        for j in range(unroll):
            placed[pl.ds(slot_ref[first + j], 1), :] = wide[pl.ds(first + j, 1), :]
        return carry

    lax.fori_loop(0, rows // unroll, body, 0)
    sorted_ref[...] = placed[...].astype(jnp.bfloat16)


def sort_rows(slot, field):
    return pl.pallas_call(
        sort_kernel,
        in_specs=[pl.BlockSpec(memory_space=pltpu.SMEM), pl.BlockSpec(memory_space=pltpu.VMEM)],
        out_shape=jax.ShapeDtypeStruct((slots, vals), jnp.bfloat16),
        scratch_shapes=[pltpu.VMEM((rows, vals), jnp.float32), pltpu.VMEM((slots, vals), jnp.float32)],
        compiler_params=params(),
        cost_estimate=pl.CostEstimate(flops=0, bytes_accessed=20000000, transcendentals=0),
    )(slot, field)


def halo_choice():
    sub, lam = lax.axis_index("sub"), lax.axis_index("lam")
    x, inner = sub % 4, jnp.where(lam % 2 == 0, 0, 2)
    before = jnp.where(sub == 0, 3, jnp.where(x == 0, 1, inner))
    after = jnp.where(sub == 15, 3, jnp.where(x == 3, 1, inner))
    return jnp.stack([before, after]).astype(jnp.int32)


def halo(choice, own_ref, next_ref, label):
    def ends(ref, second):
        top = second * stride + group
        return ref[top : top + 16, :].astype(jnp.float32)

    nothing = jnp.zeros((16, vals), jnp.float32)
    across = jnp.where(choice == 2, ends(next_ref, 0), nothing)
    corner = jnp.where(choice == 1, ends(next_ref, label), across)
    return jnp.where(choice == 0, ends(own_ref, label), corner).astype(jnp.bfloat16)


def stencil_kernel(
    choice_ref, field_ref, own_ref, before_ref, after_ref, coupling_ref, plane_ref, base_ref, projected
):
    plane = plane_ref[...]
    before = halo(choice_ref[0], own_ref, before_ref, 2)
    after = halo(choice_ref[1], own_ref, after_ref, 3)
    projected[0:8, :] = jnp.dot(before, plane, preferred_element_type=jnp.float32)[8:16]
    projected[rows + 8 : rows + 16, :] = jnp.dot(after, plane, preferred_element_type=jnp.float32)[0:8]
    for j in range(rows // 512):
        projected[8 + j * 512 : 8 + (j + 1) * 512, :] = jnp.dot(
            field_ref[j * 512 : (j + 1) * 512, :], plane, preferred_element_type=jnp.float32
        )
    for j in range(rows // vals):
        lo = j * vals
        weight = jnp.broadcast_to(coupling_ref[j : j + 1, :], (vals, vals)).T
        here = projected[lo + 8 : lo + 8 + vals, :]
        before = projected[lo + 7 : lo + 7 + vals, :]
        after = projected[lo + 9 : lo + 9 + vals, :]
        field = field_ref[lo : lo + vals, :].astype(jnp.float32)
        base_ref[lo : lo + vals, :] = field - step_size * (weight * (2.0 * here - before - after))


def stencil(field, own, before, after, coupling, plane):
    return pl.pallas_call(
        stencil_kernel,
        in_specs=[pl.BlockSpec(memory_space=pltpu.SMEM)] + [in_vmem] * 6,
        out_specs=in_vmem,
        out_shape=jax.ShapeDtypeStruct((rows, vals), jnp.float32),
        scratch_shapes=[pltpu.VMEM((rows + 16, vals), jnp.float32)],
        compiler_params=params(),
        cost_estimate=pl.CostEstimate(flops=1000, bytes_accessed=1000, transcendentals=0),
    )(halo_choice(), field, own, before, after, coupling, plane)


def respond(block, operator):
    response = jnp.dot(block, operator, preferred_element_type=jnp.float32)
    square = response * response
    magnitude = square + pltpu.roll(square, vals // 2, 1)
    reluct = 5.0 - 4.0 / (1.0 + magnitude)
    return reluct * response


def effect_blocks(sorted_ref, operators, effect_ref, blocks):
    tiles = [
        (ref, top + k * vals)
        for ref in operators
        for top in range(0, ref.shape[0], stride)
        for k in range(group // vals)
    ]
    for number, (operator_ref, top) in enumerate(tiles[: 16 * len(blocks)]):
        lo = (blocks[number // 16] * 16 + number % 16) * cap
        effect_ref[lo : lo + cap, :] = respond(
            sorted_ref[lo : lo + cap, :], operator_ref[top : top + vals, :]
        )


def effect_kernel(blocks, *refs):
    effect_blocks(refs[0], refs[1:], refs[-1], blocks)


def effects(sorted_rows, operators, blocks, previous):
    operands = [sorted_rows, *operators]
    if previous is not None:
        operands.append(previous)
    return pl.pallas_call(
        functools.partial(effect_kernel, blocks),
        in_specs=[in_vmem] * len(operands),
        out_specs=in_vmem,
        out_shape=jax.ShapeDtypeStruct((slots, vals), jnp.float32),
        input_output_aliases={} if previous is None else {len(operands) - 1: 0},
        compiler_params=params(),
        cost_estimate=pl.CostEstimate(flops=1000, bytes_accessed=1000, transcendentals=0),
    )(*operands)


part_rows = 512


def final_kernel(blocks, slot_ref, base_ref, sorted_ref, *refs):
    operators, (_, out_ref, effect_ref, result, sent) = refs[:-5], refs[-5:]
    effect_blocks(sorted_ref, operators, effect_ref, blocks)

    def copy(part):
        span = pl.ds(pl.multiple_of(part * part_rows, part_rows), part_rows)
        return pltpu.make_async_copy(result.at[span], out_ref.at[span], sent.at[part])

    for part in range(rows // part_rows):

        def body(i, carry):
            first = pl.multiple_of(part * part_rows + i * unroll, unroll)
            for j in range(unroll):
                effect = effect_ref[pl.ds(slot_ref[first + j], 1), :]
                row = pl.ds(first + j, 1)
                result[row, :] = base_ref[row, :] - step_size * effect
            return carry

        lax.fori_loop(0, part_rows // unroll, body, 0)
        copy(part).start()
    for part in range(rows // part_rows):
        copy(part).wait()


def finish(slot, base, sorted_rows, operators, blocks, previous):
    operands = [slot, base, sorted_rows, *operators, previous]
    return pl.pallas_call(
        functools.partial(final_kernel, blocks),
        in_specs=[pl.BlockSpec(memory_space=pltpu.SMEM)] + [in_vmem] * (len(operands) - 1),
        out_specs=[pl.BlockSpec(memory_space=pl.ANY), in_vmem],
        out_shape=[
            jax.ShapeDtypeStruct((rows, vals), jnp.float32),
            jax.ShapeDtypeStruct((slots, vals), jnp.float32),
        ],
        input_output_aliases={len(operands) - 1: 1},
        scratch_shapes=[
            pltpu.VMEM((rows, vals), jnp.float32),
            pltpu.SemaphoreType.DMA((rows // part_rows,)),
        ],
        compiler_params=params(),
        cost_estimate=pl.CostEstimate(flops=4096 * 128, bytes_accessed=10000000, transcendentals=0),
    )(*operands)[0]


def per_device(edge_field, coupling, owner_map, in_plane, profile_op):
    field = edge_field[0]
    tied = lax.optimization_barrier
    ends = jnp.concatenate([field[:8], field[rows - 8 :]], axis=0)
    near = jnp.concatenate([*around(profile_op[0], "zz"), ends], axis=0)
    table = slot_owners()[:, None]
    slot = rank(owner_map.reshape(rows // chunk, chunk), table).reshape(rows)
    near, slot = tied((near, slot))
    plane = jnp.concatenate(around(near, "xy"), axis=0)
    sorted_rows = sort_rows(slot, field)
    plane, sorted_rows = tied((plane, sorted_rows))
    own, across, plus, minus = around(plane, "yx")
    effect = effects(sorted_rows, [own, *swap_pieces(own)], (0, 1), None)
    minus, plus, effect = tied((minus, plus, effect))
    effect = effects(sorted_rows, [plus, minus], (4, 6), effect)
    base = stencil(field, own, plus, minus, coupling.reshape(rows // vals, vals), in_plane)
    effect = effects(sorted_rows, [*swap_pieces(plus), *swap_pieces(minus)], (5, 7), effect)
    across, effect, base = tied((across, effect, base))
    return finish(slot, base, sorted_rows, [across, *swap_pieces(across)], (2, 3), effect)[None]


def solution(mesh):
    placed = (
        P("lam", "sub", None),
        P("lam", "sub"),
        P("lam", "sub", None),
        P(),
        P(("sub", "lam"), None, None),
    )
    return jax.shard_map(
        per_device, mesh=mesh, in_specs=placed, out_specs=P("lam", "sub", None), check_vma=False
    )
```

```python
import functools

import jax
import jax.numpy as jnp
from jax import lax
from jax.experimental import pallas as pl
from jax.experimental.pallas import tpu as pltpu
from jax.sharding import PartitionSpec as P

step_size = 0.25
axes_all = ("sub", "lam")
owners = 128
cap = 48
rows = 4096
vals = 128
slots = owners * cap
chunk = 256
unroll = 128
group = 4 * vals
stride = group + 16
vmem_bytes = 20 * 1024 * 1024


in_vmem = pl.BlockSpec(memory_space=pltpu.VMEM)


def params():
    return pltpu.CompilerParams(vmem_limit_bytes=vmem_bytes)


def device(y, x, z, c):
    return ((y % 4) * 4 + (x % 4)) * 8 + (z % 4) * 2 + (c % 2)


def shifted(value, step, axes):
    pairs = []
    for y in range(4):
        for x in range(4):
            for z in range(4):
                for c in range(2):
                    place = dict(y=y, x=x, z=z, c=c)
                    place[axes[c]] += step
                    pairs.append((device(y, x, z, c), device(**place)))
    return lax.ppermute(value, axes_all, pairs)


def core_swap(value):
    pairs = [(d, d ^ 1) for d in range(owners)]
    return lax.ppermute(value, axes_all, pairs)


def swap_pieces(value):
    return [core_swap(value[i : i + group]) for i in range(0, value.shape[0], stride)]


def around(value, axes):
    return [value] + [shifted(value, step, axes) for step in (2, 1, -1)]


def offset(index):
    return jnp.where(index == 1, 2, jnp.where(index == 2, 3, jnp.where(index == 3, 1, 0)))


def slot_owners():
    sub, lam = lax.axis_index("sub"), lax.axis_index("lam")
    y, x, z, c = sub // 4, sub % 4, lam // 2, lam % 2
    index = lax.broadcasted_iota(jnp.int32, (owners, chunk), 0)
    third, side = index >> 5, (index >> 4) & 1
    second, first = (index >> 2) & 3, index & 3
    core = side ^ c
    dx = jnp.where(core == 0, offset(second), offset(third))
    dy = jnp.where(core == 0, offset(third), offset(second))
    return ((((y + dy) & 3) << 2) + ((x + dx) & 3)) * 8 + ((z + offset(first)) & 3) * 2 + core


def rank_kernel(owner_ref, slot_ref):
    table = slot_owners()
    row = lax.broadcasted_iota(jnp.int32, (chunk, chunk + owners), 0)
    col = lax.broadcasted_iota(jnp.int32, (chunk, chunk + owners), 1)
    earlier = jnp.where((row < col) | (col >= chunk), 1.0, 0.0).astype(jnp.bfloat16)
    start = cap * lax.broadcasted_iota(jnp.int32, (owners, owners), 0).astype(jnp.float32)
    for j in range(0, rows, chunk):
        hit = table == owner_ref[:, j : j + chunk]
        count = jnp.dot(
            jnp.where(hit, 1.0, 0.0).astype(jnp.bfloat16), earlier, preferred_element_type=jnp.float32
        )
        place = count[:, :chunk] + jnp.concatenate([start, start], axis=1)
        slot = jnp.sum(jnp.where(hit, place, 0.0), axis=0, keepdims=True)
        slot_ref[:, j : j + chunk] = slot.astype(jnp.int32)
        start = start + count[:, chunk:]


def rank(owner):
    return pl.pallas_call(
        rank_kernel,
        out_shape=jax.ShapeDtypeStruct((1, rows), jnp.int32),
        compiler_params=params(),
        cost_estimate=pl.CostEstimate(flops=2 * 128 * 4096 * 384, bytes_accessed=100000, transcendentals=0),
    )(owner)


def sort_kernel(slot_ref, field_ref, sorted_ref, wide, placed):
    wide[...] = field_ref[...].astype(jnp.float32)

    def body(i, carry):
        first = pl.multiple_of(i * unroll, unroll)
        for j in range(unroll):
            placed[pl.ds(slot_ref[first + j], 1), :] = wide[pl.ds(first + j, 1), :]
        return carry

    lax.fori_loop(0, rows // unroll, body, 0)
    sorted_ref[...] = placed[...].astype(jnp.bfloat16)


def sort_rows(slot, field):
    return pl.pallas_call(
        sort_kernel,
        in_specs=[pl.BlockSpec(memory_space=pltpu.SMEM), pl.BlockSpec(memory_space=pltpu.VMEM)],
        out_shape=jax.ShapeDtypeStruct((slots, vals), jnp.bfloat16),
        scratch_shapes=[pltpu.VMEM((rows, vals), jnp.float32), pltpu.VMEM((slots, vals), jnp.float32)],
        compiler_params=params(),
        cost_estimate=pl.CostEstimate(flops=0, bytes_accessed=20000000, transcendentals=0),
    )(slot, field)


def halo(choice, own_ref, next_ref, label):
    def ends(ref, second):
        top = second * stride + group
        return ref[top : top + 16, :].astype(jnp.float32)

    nothing = jnp.zeros((16, vals), jnp.float32)
    across = jnp.where(choice == 2, ends(next_ref, 0), nothing)
    corner = jnp.where(choice == 1, ends(next_ref, label), across)
    return jnp.where(choice == 0, ends(own_ref, label), corner).astype(jnp.bfloat16)


def stencil_kernel(
    field_ref, own_ref, before_ref, after_ref, coupling_ref, plane_ref, base_ref, projected
):
    plane = plane_ref[...]
    sub, lam = lax.axis_index("sub"), lax.axis_index("lam")
    x, inner = sub % 4, jnp.where(lam % 2 == 0, 0, 2)
    choice = jnp.where(sub == 0, 3, jnp.where(x == 0, 1, inner))
    before = halo(choice, own_ref, before_ref, 2)
    choice = jnp.where(sub == 15, 3, jnp.where(x == 3, 1, inner))
    after = halo(choice, own_ref, after_ref, 3)
    projected[0:8, :] = jnp.dot(before, plane, preferred_element_type=jnp.float32)[8:16]
    projected[rows + 8 : rows + 16, :] = jnp.dot(after, plane, preferred_element_type=jnp.float32)[0:8]
    for j in range(rows // 512):
        projected[8 + j * 512 : 8 + (j + 1) * 512, :] = jnp.dot(
            field_ref[j * 512 : (j + 1) * 512, :], plane, preferred_element_type=jnp.float32
        )
    for j in range(rows // vals):
        lo = j * vals
        weight = jnp.broadcast_to(coupling_ref[j : j + 1, :], (vals, vals)).T
        here = projected[lo + 8 : lo + 8 + vals, :]
        before = projected[lo + 7 : lo + 7 + vals, :]
        after = projected[lo + 9 : lo + 9 + vals, :]
        field = field_ref[lo : lo + vals, :].astype(jnp.float32)
        base_ref[lo : lo + vals, :] = field - step_size * (weight * (2.0 * here - before - after))


def stencil(field, own, before, after, coupling, plane):
    return pl.pallas_call(
        stencil_kernel,
        in_specs=[in_vmem] * 6,
        out_specs=in_vmem,
        out_shape=jax.ShapeDtypeStruct((rows, vals), jnp.float32),
        scratch_shapes=[pltpu.VMEM((rows + 16, vals), jnp.float32)],
        compiler_params=params(),
        cost_estimate=pl.CostEstimate(flops=1000, bytes_accessed=1000, transcendentals=0),
    )(field, own, before, after, coupling, plane)


def respond(block, operator):
    response = jnp.dot(block, operator, preferred_element_type=jnp.float32)
    square = response * response
    magnitude = square + pltpu.roll(square, vals // 2, 1)
    reluct = 5.0 - 4.0 / (1.0 + magnitude)
    return reluct * response


def effect_blocks(sorted_ref, operators, effect_ref, blocks):
    tiles = [
        (ref, top + k * vals)
        for ref in operators
        for top in range(0, ref.shape[0], stride)
        for k in range(group // vals)
    ]
    for number, (operator_ref, top) in enumerate(tiles[: 16 * len(blocks)]):
        lo = (blocks[number // 16] * 16 + number % 16) * cap
        effect_ref[lo : lo + cap, :] = respond(
            sorted_ref[lo : lo + cap, :], operator_ref[top : top + vals, :]
        )


def effect_kernel(blocks, *refs):
    effect_blocks(refs[0], refs[1:], refs[-1], blocks)


def effects(sorted_rows, operators, blocks, previous):
    operands = [sorted_rows, *operators]
    if previous is not None:
        operands.append(previous)
    return pl.pallas_call(
        functools.partial(effect_kernel, blocks),
        in_specs=[in_vmem] * len(operands),
        out_specs=in_vmem,
        out_shape=jax.ShapeDtypeStruct((slots, vals), jnp.float32),
        input_output_aliases={} if previous is None else {len(operands) - 1: 0},
        compiler_params=params(),
        cost_estimate=pl.CostEstimate(flops=1000, bytes_accessed=1000, transcendentals=0),
    )(*operands)


part_rows = 512


def final_kernel(blocks, slot_ref, base_ref, sorted_ref, *refs):
    operators, (_, out_ref, effect_ref, result, sent) = refs[:-5], refs[-5:]
    effect_blocks(sorted_ref, operators, effect_ref, blocks)

    def copy(part):
        span = pl.ds(pl.multiple_of(part * part_rows, part_rows), part_rows)
        return pltpu.make_async_copy(result.at[span], out_ref.at[span], sent.at[part])

    for part in range(rows // part_rows):

        def body(i, carry):
            first = pl.multiple_of(part * part_rows + i * unroll, unroll)
            for j in range(unroll):
                effect = effect_ref[pl.ds(slot_ref[first + j], 1), :]
                row = pl.ds(first + j, 1)
                result[row, :] = base_ref[row, :] - step_size * effect
            return carry

        lax.fori_loop(0, part_rows // unroll, body, 0)
        copy(part).start()
    for part in range(rows // part_rows):
        copy(part).wait()


def finish(slot, base, sorted_rows, operators, blocks, previous):
    operands = [slot, base, sorted_rows, *operators, previous]
    return pl.pallas_call(
        functools.partial(final_kernel, blocks),
        in_specs=[pl.BlockSpec(memory_space=pltpu.SMEM)] + [in_vmem] * (len(operands) - 1),
        out_specs=[pl.BlockSpec(memory_space=pl.ANY), in_vmem],
        out_shape=[
            jax.ShapeDtypeStruct((rows, vals), jnp.float32),
            jax.ShapeDtypeStruct((slots, vals), jnp.float32),
        ],
        input_output_aliases={len(operands) - 1: 1},
        scratch_shapes=[
            pltpu.VMEM((rows, vals), jnp.float32),
            pltpu.SemaphoreType.DMA((rows // part_rows,)),
        ],
        compiler_params=params(),
        cost_estimate=pl.CostEstimate(flops=4096 * 128, bytes_accessed=10000000, transcendentals=0),
    )(*operands)[0]


def per_device(edge_field, coupling, owner_map, in_plane, profile_op):
    field = edge_field[0]
    tied = lax.optimization_barrier
    ends = jnp.concatenate([field[:8], field[rows - 8 :]], axis=0)
    near = jnp.concatenate([*around(profile_op[0], "zz"), ends], axis=0)
    slot = rank(owner_map.transpose(0, 2, 1)[0]).reshape(rows)
    near, slot = tied((near, slot))
    plane = jnp.concatenate(around(near, "xy"), axis=0)
    sorted_rows = sort_rows(slot, field)
    plane, sorted_rows = tied((plane, sorted_rows))
    own, across, plus, minus = around(plane, "yx")
    effect = effects(sorted_rows, [own, *swap_pieces(own)], (0, 1), None)
    minus, plus, effect = tied((minus, plus, effect))
    effect = effects(sorted_rows, [plus, minus], (4, 6), effect)
    base = stencil(field, own, plus, minus, coupling.reshape(rows // vals, vals), in_plane)
    effect = effects(sorted_rows, [*swap_pieces(plus), *swap_pieces(minus)], (5, 7), effect)
    across, effect, base = tied((across, effect, base))
    return finish(slot, base, sorted_rows, [across, *swap_pieces(across)], (2, 3), effect)[None]


def solution(mesh):
    placed = (
        P("lam", "sub", None),
        P("lam", "sub"),
        P("lam", "sub", None),
        P(),
        P(("sub", "lam"), None, None),
    )
    return jax.shard_map(
        per_device, mesh=mesh, in_specs=placed, out_specs=P("lam", "sub", None), check_vma=False
    )
```

```python
import functools

import jax
import jax.numpy as jnp
from jax import lax
from jax.experimental import pallas as pl
from jax.experimental.pallas import tpu as pltpu
from jax.sharding import PartitionSpec as P

step_size = 0.25
axes_all = ("sub", "lam")
owners = 128
cap = 48
rows = 4096
vals = 128
slots = owners * cap
chunk = 256
unroll = 128
group = 4 * vals
stride = group + 16
vmem_bytes = 20 * 1024 * 1024


in_vmem = pl.BlockSpec(memory_space=pltpu.VMEM)


def params():
    return pltpu.CompilerParams(vmem_limit_bytes=vmem_bytes)


def device(y, x, z, c):
    return ((y % 4) * 4 + (x % 4)) * 8 + (z % 4) * 2 + (c % 2)


def shifted(value, moves):
    pairs = []
    for y in range(4):
        for x in range(4):
            for z in range(4):
                for c in range(2):
                    dy, dx, dz = moves[c]
                    pairs.append((device(y, x, z, c), device(y + dy, x + dx, z + dz, c)))
    return lax.ppermute(value, axes_all, pairs)


def scaled(moves, step):
    return [tuple(step * part for part in move) for move in moves]


def core_swap(value):
    pairs = [(d, d ^ 1) for d in range(owners)]
    return lax.ppermute(value, axes_all, pairs)


def swap_pieces(value):
    return [core_swap(value[i : i + group]) for i in range(0, value.shape[0], stride)]


first_moves = [(2, 0, 1), (0, 2, 1)]
second_moves = [(0, 1, 0), (1, 0, 0)]
third_moves = [(1, 0, 0), (0, 1, 0)]
side_moves = [(0, 0, 1), (0, 0, -1)]


def around(value, moves):
    return [value] + [shifted(value, scaled(moves, step)) for step in (2, 1, -1)]


def offset(index):
    return jnp.where(index == 1, 2, jnp.where(index == 2, 3, jnp.where(index == 3, 1, 0)))


def slot_owners():
    sub, lam = lax.axis_index("sub"), lax.axis_index("lam")
    y, x, z, c = sub // 4, sub % 4, lam // 2, lam % 2
    index = lax.broadcasted_iota(jnp.int32, (owners, chunk), 0)
    third, side = index >> 5, (index >> 4) & 1
    second, first = (index >> 2) & 3, index & 3
    core = side ^ c
    turn = offset(first)
    along = 2 * turn + jnp.where(third == 2, 3, jnp.where(third == 3, 1, 0))
    up = turn + jnp.where(third == 1, jnp.where(core == 0, 3, 1), 0)
    dx = jnp.where(core == 0, offset(second), along)
    dy = jnp.where(core == 0, along, offset(second))
    return ((((y + dy) & 3) << 2) + ((x + dx) & 3)) * 8 + ((z + up) & 3) * 2 + core


def rank_kernel(owner_ref, slot_ref):
    table = slot_owners()
    row = lax.broadcasted_iota(jnp.int32, (chunk, chunk + owners), 0)
    col = lax.broadcasted_iota(jnp.int32, (chunk, chunk + owners), 1)
    earlier = jnp.where((row < col) | (col >= chunk), 1.0, 0.0).astype(jnp.bfloat16)
    start = cap * lax.broadcasted_iota(jnp.int32, (owners, owners), 0).astype(jnp.float32)
    for j in range(0, rows, chunk):
        hit = table == owner_ref[:, j : j + chunk]
        count = jnp.dot(
            jnp.where(hit, 1.0, 0.0).astype(jnp.bfloat16), earlier, preferred_element_type=jnp.float32
        )
        place = count[:, :chunk] + jnp.concatenate([start, start], axis=1)
        slot = jnp.sum(jnp.where(hit, place, 0.0), axis=0, keepdims=True)
        slot_ref[:, j : j + chunk] = slot.astype(jnp.int32)
        start = start + count[:, chunk:]


def rank(owner):
    return pl.pallas_call(
        rank_kernel,
        out_shape=jax.ShapeDtypeStruct((1, rows), jnp.int32),
        compiler_params=params(),
        cost_estimate=pl.CostEstimate(flops=2 * 128 * 4096 * 384, bytes_accessed=100000, transcendentals=0),
    )(owner)


def sort_kernel(slot_ref, field_ref, sorted_ref, wide, placed):
    wide[...] = field_ref[...].astype(jnp.float32)

    def body(i, carry):
        first = pl.multiple_of(i * unroll, unroll)
        for j in range(unroll):
            placed[pl.ds(slot_ref[first + j], 1), :] = wide[pl.ds(first + j, 1), :]
        return carry

    lax.fori_loop(0, rows // unroll, body, 0)
    sorted_ref[...] = placed[...].astype(jnp.bfloat16)


def sort_rows(slot, field):
    return pl.pallas_call(
        sort_kernel,
        in_specs=[pl.BlockSpec(memory_space=pltpu.SMEM), pl.BlockSpec(memory_space=pltpu.VMEM)],
        out_shape=jax.ShapeDtypeStruct((slots, vals), jnp.bfloat16),
        scratch_shapes=[pltpu.VMEM((rows, vals), jnp.float32), pltpu.VMEM((slots, vals), jnp.float32)],
        compiler_params=params(),
        cost_estimate=pl.CostEstimate(flops=0, bytes_accessed=20000000, transcendentals=0),
    )(slot, field)


def halo(choice, own_ref, next_ref, label):
    def ends(ref, second):
        top = second * stride + group
        return ref[top : top + 16, :].astype(jnp.float32)

    nothing = jnp.zeros((16, vals), jnp.float32)
    across = jnp.where(choice == 2, ends(next_ref, 0), nothing)
    corner = jnp.where(choice == 1, ends(next_ref, label), across)
    return jnp.where(choice == 0, ends(own_ref, label), corner).astype(jnp.bfloat16)


def stencil_kernel(
    field_ref, own_ref, before_ref, after_ref, coupling_ref, plane_ref, base_ref, projected
):
    plane = plane_ref[...]
    sub, lam = lax.axis_index("sub"), lax.axis_index("lam")
    x, inner = sub % 4, jnp.where(lam % 2 == 0, 0, 2)
    choice = jnp.where(sub == 0, 3, jnp.where(x == 0, 1, inner))
    before = halo(choice, own_ref, before_ref, 2)
    choice = jnp.where(sub == 15, 3, jnp.where(x == 3, 1, inner))
    after = halo(choice, own_ref, after_ref, 3)
    projected[0:8, :] = jnp.dot(before, plane, preferred_element_type=jnp.float32)[8:16]
    projected[rows + 8 : rows + 16, :] = jnp.dot(after, plane, preferred_element_type=jnp.float32)[0:8]
    for j in range(rows // 512):
        projected[8 + j * 512 : 8 + (j + 1) * 512, :] = jnp.dot(
            field_ref[j * 512 : (j + 1) * 512, :], plane, preferred_element_type=jnp.float32
        )
    for j in range(rows // vals):
        lo = j * vals
        weight = jnp.broadcast_to(coupling_ref[j : j + 1, :], (vals, vals)).T
        here = projected[lo + 8 : lo + 8 + vals, :]
        before = projected[lo + 7 : lo + 7 + vals, :]
        after = projected[lo + 9 : lo + 9 + vals, :]
        field = field_ref[lo : lo + vals, :].astype(jnp.float32)
        base_ref[lo : lo + vals, :] = field - step_size * (weight * (2.0 * here - before - after))


def stencil(field, own, before, after, coupling, plane):
    return pl.pallas_call(
        stencil_kernel,
        in_specs=[in_vmem] * 6,
        out_specs=in_vmem,
        out_shape=jax.ShapeDtypeStruct((rows, vals), jnp.float32),
        scratch_shapes=[pltpu.VMEM((rows + 16, vals), jnp.float32)],
        compiler_params=params(),
        cost_estimate=pl.CostEstimate(flops=1000, bytes_accessed=1000, transcendentals=0),
    )(field, own, before, after, coupling, plane)


def respond(block, operator):
    response = jnp.dot(block, operator, preferred_element_type=jnp.float32)
    square = response * response
    magnitude = square + pltpu.roll(square, vals // 2, 1)
    reluct = 5.0 - 4.0 / (1.0 + magnitude)
    return reluct * response


def effect_blocks(sorted_ref, operators, effect_ref, blocks):
    tiles = [
        (ref, top + k * vals)
        for ref in operators
        for top in range(0, ref.shape[0], stride)
        for k in range(group // vals)
    ]
    for number, (operator_ref, top) in enumerate(tiles[: 16 * len(blocks)]):
        lo = (blocks[number // 16] * 16 + number % 16) * cap
        effect_ref[lo : lo + cap, :] = respond(
            sorted_ref[lo : lo + cap, :], operator_ref[top : top + vals, :]
        )


def effect_kernel(blocks, *refs):
    effect_blocks(refs[0], refs[1:], refs[-1], blocks)


def effects(sorted_rows, operators, blocks, previous):
    operands = [sorted_rows, *operators]
    if previous is not None:
        operands.append(previous)
    return pl.pallas_call(
        functools.partial(effect_kernel, blocks),
        in_specs=[in_vmem] * len(operands),
        out_specs=in_vmem,
        out_shape=jax.ShapeDtypeStruct((slots, vals), jnp.float32),
        input_output_aliases={} if previous is None else {len(operands) - 1: 0},
        compiler_params=params(),
        cost_estimate=pl.CostEstimate(flops=1000, bytes_accessed=1000, transcendentals=0),
    )(*operands)


part_rows = 512


def final_kernel(blocks, slot_ref, base_ref, sorted_ref, *refs):
    operators, (_, out_ref, effect_ref, result, sent) = refs[:-5], refs[-5:]
    effect_blocks(sorted_ref, operators, effect_ref, blocks)

    def copy(part):
        span = pl.ds(pl.multiple_of(part * part_rows, part_rows), part_rows)
        return pltpu.make_async_copy(result.at[span], out_ref.at[span], sent.at[part])

    for part in range(rows // part_rows):

        def body(i, carry):
            first = pl.multiple_of(part * part_rows + i * unroll, unroll)
            for j in range(unroll):
                effect = effect_ref[pl.ds(slot_ref[first + j], 1), :]
                row = pl.ds(first + j, 1)
                result[row, :] = base_ref[row, :] - step_size * effect
            return carry

        lax.fori_loop(0, part_rows // unroll, body, 0)
        copy(part).start()
    for part in range(rows // part_rows):
        copy(part).wait()


def finish(slot, base, sorted_rows, operators, blocks, previous):
    operands = [slot, base, sorted_rows, *operators, previous]
    return pl.pallas_call(
        functools.partial(final_kernel, blocks),
        in_specs=[pl.BlockSpec(memory_space=pltpu.SMEM)] + [in_vmem] * (len(operands) - 1),
        out_specs=[pl.BlockSpec(memory_space=pl.ANY), in_vmem],
        out_shape=[
            jax.ShapeDtypeStruct((rows, vals), jnp.float32),
            jax.ShapeDtypeStruct((slots, vals), jnp.float32),
        ],
        input_output_aliases={len(operands) - 1: 1},
        scratch_shapes=[
            pltpu.VMEM((rows, vals), jnp.float32),
            pltpu.SemaphoreType.DMA((rows // part_rows,)),
        ],
        compiler_params=params(),
        cost_estimate=pl.CostEstimate(flops=4096 * 128, bytes_accessed=10000000, transcendentals=0),
    )(*operands)[0]


def per_device(edge_field, coupling, owner_map, in_plane, profile_op):
    field = edge_field[0]
    tied = lax.optimization_barrier
    ends = jnp.concatenate([field[:8], field[rows - 8 :]], axis=0)
    near = jnp.concatenate([*around(profile_op[0], first_moves), ends], axis=0)
    slot = rank(owner_map.transpose(0, 2, 1)[0]).reshape(rows)
    near, slot = tied((near, slot))
    plane = jnp.concatenate(around(near, second_moves), axis=0)
    sorted_rows = sort_rows(slot, field)
    plane, sorted_rows = tied((plane, sorted_rows))
    own, plus, minus = plane, shifted(plane, third_moves), shifted(plane, scaled(third_moves, -1))
    across = shifted(plane, side_moves)
    effect = effects(sorted_rows, [own, *swap_pieces(own)], (0, 1), None)
    minus, plus, effect = tied((minus, plus, effect))
    effect = effects(sorted_rows, [plus, minus], (4, 6), effect)
    base = stencil(field, own, plus, minus, coupling.reshape(rows // vals, vals), in_plane)
    effect = effects(sorted_rows, [*swap_pieces(plus), *swap_pieces(minus)], (5, 7), effect)
    across, effect, base = tied((across, effect, base))
    return finish(slot, base, sorted_rows, [across, *swap_pieces(across)], (2, 3), effect)[None]


def solution(mesh):
    placed = (
        P("lam", "sub", None),
        P("lam", "sub"),
        P("lam", "sub", None),
        P(),
        P(("sub", "lam"), None, None),
    )
    return jax.shard_map(
        per_device, mesh=mesh, in_specs=placed, out_specs=P("lam", "sub", None), check_vma=False
    )
```

```python
import functools

import jax
import jax.numpy as jnp
from jax import lax
from jax.experimental import pallas as pl
from jax.experimental.pallas import tpu as pltpu
from jax.sharding import PartitionSpec as P

step_size = 0.25
axes_all = ("sub", "lam")
owners = 128
cap = 48
rows = 4096
vals = 128
slots = owners * cap
half = slots // 2
block = 16 * cap
chunk = 256
unroll = 128
group = 4 * vals
stride = group + 16
vmem_bytes = 20 * 1024 * 1024


in_vmem = pl.BlockSpec(memory_space=pltpu.VMEM)


def params():
    return pltpu.CompilerParams(vmem_limit_bytes=vmem_bytes)


def device(y, x, z, c):
    return ((y % 4) * 4 + (x % 4)) * 8 + (z % 4) * 2 + (c % 2)


def shifted(value, moves):
    pairs = []
    for y in range(4):
        for x in range(4):
            for z in range(4):
                for c in range(2):
                    dy, dx, dz = moves[c]
                    pairs.append((device(y, x, z, c), device(y + dy, x + dx, z + dz, c)))
    return lax.ppermute(value, axes_all, pairs)


def scaled(moves, step):
    return [tuple(step * part for part in move) for move in moves]


def core_swap(value):
    pairs = [(d, d ^ 1) for d in range(owners)]
    return lax.ppermute(value, axes_all, pairs)


first_moves = [(2, 0, 1), (0, 2, 1)]
second_moves = [(0, 1, 0), (1, 0, 0)]
third_moves = [(1, 0, 0), (0, 1, 0)]
side_moves = [(0, 0, 1), (0, 0, -1)]


def around(value, moves):
    return [value] + [shifted(value, scaled(moves, step)) for step in (2, 1, -1)]


def offset(index):
    return jnp.where(index == 1, 2, jnp.where(index == 2, 3, jnp.where(index == 3, 1, 0)))


def slot_owners():
    sub, lam = lax.axis_index("sub"), lax.axis_index("lam")
    y, x, z, c = sub // 4, sub % 4, lam // 2, lam % 2
    index = lax.broadcasted_iota(jnp.int32, (owners, chunk), 0)
    side, third = index >> 6, (index >> 4) & 3
    second, first = (index >> 2) & 3, index & 3
    core = side ^ c
    turn = offset(first)
    along = 2 * turn + jnp.where(third == 2, 3, jnp.where(third == 3, 1, 0))
    up = turn + jnp.where(third == 1, jnp.where(core == 0, 3, 1), 0)
    dx = jnp.where(core == 0, offset(second), along)
    dy = jnp.where(core == 0, along, offset(second))
    return ((((y + dy) & 3) << 2) + ((x + dx) & 3)) * 8 + ((z + up) & 3) * 2 + core


def rank_kernel(owner_ref, slot_ref):
    table = slot_owners()
    row = lax.broadcasted_iota(jnp.int32, (chunk, chunk + owners), 0)
    col = lax.broadcasted_iota(jnp.int32, (chunk, chunk + owners), 1)
    earlier = jnp.where((row < col) | (col >= chunk), 1.0, 0.0).astype(jnp.bfloat16)
    start = cap * lax.broadcasted_iota(jnp.int32, (owners, owners), 0).astype(jnp.float32)
    for j in range(0, rows, chunk):
        hit = table == owner_ref[:, j : j + chunk]
        count = jnp.dot(
            jnp.where(hit, 1.0, 0.0).astype(jnp.bfloat16), earlier, preferred_element_type=jnp.float32
        )
        place = count[:, :chunk] + jnp.concatenate([start, start], axis=1)
        slot = jnp.sum(jnp.where(hit, place, 0.0), axis=0, keepdims=True)
        slot_ref[:, j : j + chunk] = slot.astype(jnp.int32)
        start = start + count[:, chunk:]


def rank(owner):
    return pl.pallas_call(
        rank_kernel,
        out_shape=jax.ShapeDtypeStruct((1, rows), jnp.int32),
        compiler_params=params(),
        cost_estimate=pl.CostEstimate(flops=2 * 128 * 4096 * 384, bytes_accessed=100000, transcendentals=0),
    )(owner)


def sort_kernel(slot_ref, field_ref, near_ref, far_ref, wide, placed):
    wide[...] = field_ref[...].astype(jnp.float32)

    def body(i, carry):
        first = pl.multiple_of(i * unroll, unroll)
        for j in range(unroll):
            placed[pl.ds(slot_ref[first + j], 1), :] = wide[pl.ds(first + j, 1), :]
        return carry

    lax.fori_loop(0, rows // unroll, body, 0)
    near_ref[...] = placed[:half].astype(jnp.bfloat16)
    far_ref[...] = placed[half:].astype(jnp.bfloat16)


def sort_rows(slot, field):
    return pl.pallas_call(
        sort_kernel,
        in_specs=[pl.BlockSpec(memory_space=pltpu.SMEM), in_vmem],
        out_specs=[in_vmem, in_vmem],
        out_shape=[jax.ShapeDtypeStruct((half, vals), jnp.bfloat16)] * 2,
        scratch_shapes=[pltpu.VMEM((rows, vals), jnp.float32), pltpu.VMEM((slots, vals), jnp.float32)],
        compiler_params=params(),
        cost_estimate=pl.CostEstimate(flops=0, bytes_accessed=20000000, transcendentals=0),
    )(slot, field)


def halo(choice, own_ref, next_ref, label):
    def ends(ref, second):
        top = second * stride + group
        return ref[top : top + 16, :].astype(jnp.float32)

    nothing = jnp.zeros((16, vals), jnp.float32)
    across = jnp.where(choice == 2, ends(next_ref, 0), nothing)
    corner = jnp.where(choice == 1, ends(next_ref, label), across)
    return jnp.where(choice == 0, ends(own_ref, label), corner).astype(jnp.bfloat16)


def stencil_kernel(
    field_ref, own_ref, before_ref, after_ref, coupling_ref, plane_ref, base_ref, projected
):
    plane = plane_ref[...]
    sub, lam = lax.axis_index("sub"), lax.axis_index("lam")
    x, inner = sub % 4, jnp.where(lam % 2 == 0, 0, 2)
    choice = jnp.where(sub == 0, 3, jnp.where(x == 0, 1, inner))
    before = halo(choice, own_ref, before_ref, 2)
    choice = jnp.where(sub == 15, 3, jnp.where(x == 3, 1, inner))
    after = halo(choice, own_ref, after_ref, 3)
    projected[0:8, :] = jnp.dot(before, plane, preferred_element_type=jnp.float32)[8:16]
    projected[rows + 8 : rows + 16, :] = jnp.dot(after, plane, preferred_element_type=jnp.float32)[0:8]
    for j in range(rows // 512):
        projected[8 + j * 512 : 8 + (j + 1) * 512, :] = jnp.dot(
            field_ref[j * 512 : (j + 1) * 512, :], plane, preferred_element_type=jnp.float32
        )
    for j in range(rows // vals):
        lo = j * vals
        weight = jnp.broadcast_to(coupling_ref[j : j + 1, :], (vals, vals)).T
        here = projected[lo + 8 : lo + 8 + vals, :]
        before = projected[lo + 7 : lo + 7 + vals, :]
        after = projected[lo + 9 : lo + 9 + vals, :]
        field = field_ref[lo : lo + vals, :].astype(jnp.float32)
        base_ref[lo : lo + vals, :] = field - step_size * (weight * (2.0 * here - before - after))


def stencil(field, own, before, after, coupling, plane):
    return pl.pallas_call(
        stencil_kernel,
        in_specs=[in_vmem] * 6,
        out_specs=in_vmem,
        out_shape=jax.ShapeDtypeStruct((rows, vals), jnp.float32),
        scratch_shapes=[pltpu.VMEM((rows + 16, vals), jnp.float32)],
        compiler_params=params(),
        cost_estimate=pl.CostEstimate(flops=1000, bytes_accessed=1000, transcendentals=0),
    )(field, own, before, after, coupling, plane)


def respond(block, operator):
    response = jnp.dot(block, operator, preferred_element_type=jnp.float32)
    square = response * response
    magnitude = square + pltpu.roll(square, vals // 2, 1)
    reluct = 5.0 - 4.0 / (1.0 + magnitude)
    return reluct * response


def effect_kernel(thirds, near_ref, guest_ref, *refs):
    operators, (effect_ref, reply_ref) = refs[: len(thirds)], refs[-2:]
    for number, (third, operator_ref) in enumerate(zip(thirds, operators)):
        for k in range(16):
            top = k // 4 * stride + k % 4 * vals
            operator = operator_ref[top : top + vals, :]
            lo, out = third * block + k * cap, number * block + k * cap
            effect_ref[lo : lo + cap, :] = respond(near_ref[lo : lo + cap, :], operator)
            reply_ref[out : out + cap, :] = respond(guest_ref[lo : lo + cap, :], operator).astype(
                jnp.bfloat16
            )


def effects(near, guest, operators, thirds, previous):
    operands = [near, guest, *operators]
    if previous is not None:
        operands.append(previous)
    return pl.pallas_call(
        functools.partial(effect_kernel, thirds),
        in_specs=[in_vmem] * len(operands),
        out_specs=[in_vmem, in_vmem],
        out_shape=[
            jax.ShapeDtypeStruct((slots, vals), jnp.float32),
            jax.ShapeDtypeStruct((len(thirds) * block, vals), jnp.bfloat16),
        ],
        input_output_aliases={} if previous is None else {len(operands) - 1: 0},
        compiler_params=params(),
        cost_estimate=pl.CostEstimate(flops=1000, bytes_accessed=1000, transcendentals=0),
    )(*operands)


part_rows = 512


def final_kernel(slot_ref, base_ref, own_ref, pair_ref, side_ref, _, out_ref, effect_ref, result, sent):
    for returned_ref, third in ((own_ref, 0), (pair_ref, 2), (side_ref, 1)):
        lo = half + third * block
        effect_ref[lo : lo + returned_ref.shape[0], :] = returned_ref[...].astype(jnp.float32)

    def copy(part):
        span = pl.ds(pl.multiple_of(part * part_rows, part_rows), part_rows)
        return pltpu.make_async_copy(result.at[span], out_ref.at[span], sent.at[part])

    for part in range(rows // part_rows):

        def body(i, carry):
            first = pl.multiple_of(part * part_rows + i * unroll, unroll)
            for j in range(unroll):
                effect = effect_ref[pl.ds(slot_ref[first + j], 1), :]
                row = pl.ds(first + j, 1)
                result[row, :] = base_ref[row, :] - step_size * effect
            return carry

        lax.fori_loop(0, part_rows // unroll, body, 0)
        copy(part).start()
    for part in range(rows // part_rows):
        copy(part).wait()


def finish(slot, base, returned, effect):
    operands = [slot, base, *returned, effect]
    return pl.pallas_call(
        final_kernel,
        in_specs=[pl.BlockSpec(memory_space=pltpu.SMEM)] + [in_vmem] * (len(operands) - 1),
        out_specs=[pl.BlockSpec(memory_space=pl.ANY), in_vmem],
        out_shape=[
            jax.ShapeDtypeStruct((rows, vals), jnp.float32),
            jax.ShapeDtypeStruct((slots, vals), jnp.float32),
        ],
        input_output_aliases={len(operands) - 1: 1},
        scratch_shapes=[
            pltpu.VMEM((rows, vals), jnp.float32),
            pltpu.SemaphoreType.DMA((rows // part_rows,)),
        ],
        compiler_params=params(),
        cost_estimate=pl.CostEstimate(flops=4096 * 128, bytes_accessed=10000000, transcendentals=0),
    )(*operands)[0]


def per_device(edge_field, coupling, owner_map, in_plane, profile_op):
    field = edge_field[0]
    tied = lax.optimization_barrier
    ends = jnp.concatenate([field[:8], field[rows - 8 :]], axis=0)
    near = jnp.concatenate([*around(profile_op[0], first_moves), ends], axis=0)
    slot = rank(owner_map.transpose(0, 2, 1)[0]).reshape(rows)
    near, slot = tied((near, slot))
    plane = jnp.concatenate(around(near, second_moves), axis=0)
    near_rows, far_rows = sort_rows(slot, field)
    plane, near_rows, far_rows = tied((plane, near_rows, far_rows))
    plus, minus = shifted(plane, third_moves), shifted(plane, scaled(third_moves, -1))
    side = shifted(plane, side_moves)
    guest = core_swap(far_rows)
    effect, reply = effects(near_rows, guest, [plane], (0,), None)
    returned = [core_swap(reply)]
    minus, plus, effect = tied((minus, plus, effect))
    effect, reply = effects(near_rows, guest, [plus, minus], (2, 3), effect)
    returned.append(core_swap(reply))
    base = stencil(field, plane, plus, minus, coupling.reshape(rows // vals, vals), in_plane)
    side, effect, base = tied((side, effect, base))
    effect, reply = effects(near_rows, guest, [side], (1,), effect)
    returned.append(core_swap(reply))
    return finish(slot, base, returned, effect)[None]


def solution(mesh):
    placed = (
        P("lam", "sub", None),
        P("lam", "sub"),
        P("lam", "sub", None),
        P(),
        P(("sub", "lam"), None, None),
    )
    return jax.shard_map(
        per_device, mesh=mesh, in_specs=placed, out_specs=P("lam", "sub", None), check_vma=False
    )
```

```python
import functools

import jax
import jax.numpy as jnp
from jax import lax
from jax.experimental import pallas as pl
from jax.experimental.pallas import tpu as pltpu
from jax.sharding import PartitionSpec as P

step_size = 0.25
axes_all = ("sub", "lam")
owners = 128
cap = 48
rows = 4096
vals = 128
slots = owners * cap
half = slots // 2
block = 16 * cap
chunk = 256
unroll = 128
group = 4 * vals
stride = group + 16
vmem_bytes = 20 * 1024 * 1024


in_vmem = pl.BlockSpec(memory_space=pltpu.VMEM)


def params():
    return pltpu.CompilerParams(vmem_limit_bytes=vmem_bytes)


def device(y, x, z, c):
    return ((y % 4) * 4 + (x % 4)) * 8 + (z % 4) * 2 + (c % 2)


def shifted(value, moves):
    pairs = []
    for y in range(4):
        for x in range(4):
            for z in range(4):
                for c in range(2):
                    dy, dx, dz = moves[c]
                    pairs.append((device(y, x, z, c), device(y + dy, x + dx, z + dz, c)))
    return lax.ppermute(value, axes_all, pairs)


def scaled(moves, step):
    return [tuple(step * part for part in move) for move in moves]


def core_swap(value):
    pairs = [(d, d ^ 1) for d in range(owners)]
    return lax.ppermute(value, axes_all, pairs)


first_moves = [(2, 0, 1), (0, 2, 1)]
second_moves = [(0, 1, 0), (1, 0, 0)]
third_moves = [(1, 0, 0), (0, 1, 0)]
side_moves = [(0, 0, 1), (0, 0, -1)]


def around(value, moves):
    return [value] + [shifted(value, scaled(moves, step)) for step in (2, 1, -1)]


def offset(index):
    return jnp.where(index == 1, 2, jnp.where(index == 2, 3, jnp.where(index == 3, 1, 0)))


def slot_owners():
    sub, lam = lax.axis_index("sub"), lax.axis_index("lam")
    y, x, z, c = sub // 4, sub % 4, lam // 2, lam % 2
    index = lax.broadcasted_iota(jnp.int32, (owners, chunk), 0)
    side, third = index >> 6, (index >> 4) & 3
    second, first = (index >> 2) & 3, index & 3
    core = side ^ c
    turn = offset(first)
    along = 2 * turn + jnp.where(third == 2, 3, jnp.where(third == 3, 1, 0))
    up = turn + jnp.where(third == 1, jnp.where(core == 0, 3, 1), 0)
    dx = jnp.where(core == 0, offset(second), along)
    dy = jnp.where(core == 0, along, offset(second))
    return ((((y + dy) & 3) << 2) + ((x + dx) & 3)) * 8 + ((z + up) & 3) * 2 + core


def rank_kernel(owner_ref, slot_ref):
    table = slot_owners()
    row = lax.broadcasted_iota(jnp.int32, (chunk, chunk + owners), 0)
    col = lax.broadcasted_iota(jnp.int32, (chunk, chunk + owners), 1)
    earlier = jnp.where((row < col) | (col >= chunk), 1.0, 0.0).astype(jnp.bfloat16)
    start = cap * lax.broadcasted_iota(jnp.int32, (owners, owners), 0).astype(jnp.float32)
    for j in range(0, rows, chunk):
        hit = table == owner_ref[:, j : j + chunk]
        count = jnp.dot(
            jnp.where(hit, 1.0, 0.0).astype(jnp.bfloat16), earlier, preferred_element_type=jnp.float32
        )
        place = count[:, :chunk] + jnp.concatenate([start, start], axis=1)
        slot = jnp.sum(jnp.where(hit, place, 0.0), axis=0, keepdims=True)
        slot_ref[:, j : j + chunk] = slot.astype(jnp.int32)
        start = start + count[:, chunk:]


def rank(owner):
    return pl.pallas_call(
        rank_kernel,
        out_shape=jax.ShapeDtypeStruct((1, rows), jnp.int32),
        compiler_params=params(),
        cost_estimate=pl.CostEstimate(flops=2 * 128 * 4096 * 384, bytes_accessed=100000, transcendentals=0),
    )(owner)


def sort_kernel(slot_ref, field_ref, near_ref, far_ref, wide, placed):
    wide[...] = field_ref[...].astype(jnp.float32)

    def body(i, carry):
        first = pl.multiple_of(i * unroll, unroll)
        for j in range(unroll):
            placed[pl.ds(slot_ref[first + j], 1), :] = wide[pl.ds(first + j, 1), :]
        return carry

    lax.fori_loop(0, rows // unroll, body, 0)
    near_ref[...] = placed[:half].astype(jnp.bfloat16)
    far_ref[...] = placed[half:].astype(jnp.bfloat16)


def sort_rows(slot, field):
    return pl.pallas_call(
        sort_kernel,
        in_specs=[pl.BlockSpec(memory_space=pltpu.SMEM), in_vmem],
        out_specs=[in_vmem, in_vmem],
        out_shape=[jax.ShapeDtypeStruct((half, vals), jnp.bfloat16)] * 2,
        scratch_shapes=[pltpu.VMEM((rows, vals), jnp.float32), pltpu.VMEM((slots, vals), jnp.float32)],
        compiler_params=params(),
        cost_estimate=pl.CostEstimate(flops=0, bytes_accessed=20000000, transcendentals=0),
    )(slot, field)


def halo(choice, own_ref, next_ref, label):
    def ends(ref, second):
        top = second * stride + group
        return ref[top : top + 16, :].astype(jnp.float32)

    nothing = jnp.zeros((16, vals), jnp.float32)
    across = jnp.where(choice == 2, ends(next_ref, 0), nothing)
    corner = jnp.where(choice == 1, ends(next_ref, label), across)
    return jnp.where(choice == 0, ends(own_ref, label), corner).astype(jnp.bfloat16)


def stencil_kernel(
    field_ref, own_ref, before_ref, after_ref, coupling_ref, plane_ref, base_ref, projected
):
    plane = plane_ref[...]
    sub, lam = lax.axis_index("sub"), lax.axis_index("lam")
    x, inner = sub % 4, jnp.where(lam % 2 == 0, 0, 2)
    choice = jnp.where(sub == 0, 3, jnp.where(x == 0, 1, inner))
    before = halo(choice, own_ref, before_ref, 2)
    choice = jnp.where(sub == 15, 3, jnp.where(x == 3, 1, inner))
    after = halo(choice, own_ref, after_ref, 3)
    projected[0:8, :] = jnp.dot(before, plane, preferred_element_type=jnp.float32)[8:16]
    projected[rows + 8 : rows + 16, :] = jnp.dot(after, plane, preferred_element_type=jnp.float32)[0:8]
    for j in range(rows // 512):
        projected[8 + j * 512 : 8 + (j + 1) * 512, :] = jnp.dot(
            field_ref[j * 512 : (j + 1) * 512, :], plane, preferred_element_type=jnp.float32
        )
    for j in range(rows // vals):
        lo = j * vals
        weight = jnp.broadcast_to(coupling_ref[j : j + 1, :], (vals, vals)).T
        here = projected[lo + 8 : lo + 8 + vals, :]
        before = projected[lo + 7 : lo + 7 + vals, :]
        after = projected[lo + 9 : lo + 9 + vals, :]
        field = field_ref[lo : lo + vals, :].astype(jnp.float32)
        base_ref[lo : lo + vals, :] = field - step_size * (weight * (2.0 * here - before - after))


def stencil(field, own, before, after, coupling, plane):
    return pl.pallas_call(
        stencil_kernel,
        in_specs=[in_vmem] * 6,
        out_specs=in_vmem,
        out_shape=jax.ShapeDtypeStruct((rows, vals), jnp.float32),
        scratch_shapes=[pltpu.VMEM((rows + 16, vals), jnp.float32)],
        compiler_params=params(),
        cost_estimate=pl.CostEstimate(flops=1000, bytes_accessed=1000, transcendentals=0),
    )(field, own, before, after, coupling, plane)


def respond(block, operator):
    response = jnp.dot(block, operator, preferred_element_type=jnp.float32)
    square = response * response
    magnitude = square + pltpu.roll(square, vals // 2, 1)
    reluct = 5.0 - 4.0 / (1.0 + magnitude)
    return reluct * response


def effect_kernel(thirds, places, rows_ref, *refs):
    operators, out_ref = refs[: len(thirds)], refs[-1]
    for third, place, operator_ref in zip(thirds, places, operators):
        for k in range(16):
            top = k // 4 * stride + k % 4 * vals
            lo, out = third * block + k * cap, place * block + k * cap
            effect = respond(rows_ref[lo : lo + cap, :], operator_ref[top : top + vals, :])
            out_ref[out : out + cap, :] = effect.astype(out_ref.dtype)


def effect_call(operands, thirds, places, shape, dtype, aliases):
    return pl.pallas_call(
        functools.partial(effect_kernel, thirds, places),
        in_specs=[in_vmem] * len(operands),
        out_specs=in_vmem,
        out_shape=jax.ShapeDtypeStruct((shape, vals), dtype),
        input_output_aliases=aliases,
        compiler_params=params(),
        cost_estimate=pl.CostEstimate(flops=1000, bytes_accessed=1000, transcendentals=0),
    )(*operands)


def replies(guest, operators, thirds):
    count = len(thirds)
    return effect_call([guest, *operators], thirds, range(count), count * block, jnp.bfloat16, {})


def effects(near, operators, thirds, previous):
    operands = [near, *operators]
    aliases = {}
    if previous is not None:
        aliases = {len(operands): 0}
        operands.append(previous)
    return effect_call(operands, thirds, thirds, slots, jnp.float32, aliases)


part_tops = (0, 1024, 2048, 3072, 3584, 3840, rows)


def final_kernel(slot_ref, base_ref, own_ref, pair_ref, side_ref, _, out_ref, effect_ref, result, sent):
    for returned_ref, third in ((own_ref, 0), (pair_ref, 2), (side_ref, 1)):
        lo = half + third * block
        effect_ref[lo : lo + returned_ref.shape[0], :] = returned_ref[...].astype(jnp.float32)

    copies = []
    for number, (top, end) in enumerate(zip(part_tops, part_tops[1:])):

        def body(i, carry):
            first = pl.multiple_of(top + i * unroll, unroll)
            for j in range(unroll):
                effect = effect_ref[pl.ds(slot_ref[first + j], 1), :]
                row = pl.ds(first + j, 1)
                result[row, :] = base_ref[row, :] - step_size * effect
            return carry

        lax.fori_loop(0, (end - top) // unroll, body, 0)
        span = slice(top, end)
        copies.append(pltpu.make_async_copy(result.at[span], out_ref.at[span], sent.at[number]))
        copies[-1].start()
    for copy in copies:
        copy.wait()


def finish(slot, base, returned, effect):
    operands = [slot, base, *returned, effect]
    return pl.pallas_call(
        final_kernel,
        in_specs=[pl.BlockSpec(memory_space=pltpu.SMEM)] + [in_vmem] * (len(operands) - 1),
        out_specs=[pl.BlockSpec(memory_space=pl.ANY), in_vmem],
        out_shape=[
            jax.ShapeDtypeStruct((rows, vals), jnp.float32),
            jax.ShapeDtypeStruct((slots, vals), jnp.float32),
        ],
        input_output_aliases={len(operands) - 1: 1},
        scratch_shapes=[
            pltpu.VMEM((rows, vals), jnp.float32),
            pltpu.SemaphoreType.DMA((len(part_tops) - 1,)),
        ],
        compiler_params=params(),
        cost_estimate=pl.CostEstimate(flops=4096 * 128, bytes_accessed=10000000, transcendentals=0),
    )(*operands)[0]


def per_device(edge_field, coupling, owner_map, in_plane, profile_op):
    field = edge_field[0]
    tied = lax.optimization_barrier
    ends = jnp.concatenate([field[:8], field[rows - 8 :]], axis=0)
    near = jnp.concatenate([*around(profile_op[0], first_moves), ends], axis=0)
    slot = rank(owner_map.transpose(0, 2, 1)[0]).reshape(rows)
    near, slot = tied((near, slot))
    plane = jnp.concatenate(around(near, second_moves), axis=0)
    near_rows, far_rows = sort_rows(slot, field)
    plane, near_rows, far_rows = tied((plane, near_rows, far_rows))
    plus, minus = shifted(plane, third_moves), shifted(plane, scaled(third_moves, -1))
    side = shifted(plane, side_moves)
    guest = core_swap(far_rows)
    reply = replies(guest, [plane], (0,))
    effect = effects(near_rows, [plane], (0,), None)
    minus, plus, effect, reply = tied((minus, plus, effect, reply))
    returned = [core_swap(reply)]
    returned.append(core_swap(replies(guest, [plus, minus], (2, 3))))
    returned.append(core_swap(replies(guest, [side], (1,))))
    effect = effects(near_rows, [side, plus, minus], (1, 2, 3), effect)
    base = stencil(field, plane, plus, minus, coupling.reshape(rows // vals, vals), in_plane)
    return finish(slot, base, returned, effect)[None]


def solution(mesh):
    placed = (
        P("lam", "sub", None),
        P("lam", "sub"),
        P("lam", "sub", None),
        P(),
        P(("sub", "lam"), None, None),
    )
    return jax.shard_map(
        per_device, mesh=mesh, in_specs=placed, out_specs=P("lam", "sub", None), check_vma=False
    )
```

```python
import functools

import jax
import jax.numpy as jnp
from jax import lax
from jax.experimental import pallas as pl
from jax.experimental.pallas import tpu as pltpu
from jax.sharding import PartitionSpec as P

step_size = 0.25
axes_all = ("sub", "lam")
owners = 128
cap = 48
rows = 4096
vals = 128
slots = owners * cap
half = slots // 2
block = 16 * cap
chunk = 256
unroll = 128
long_unroll = 256
group = 4 * vals
stride = group + 16
vmem_bytes = 20 * 1024 * 1024


in_vmem = pl.BlockSpec(memory_space=pltpu.VMEM)


def params():
    return pltpu.CompilerParams(vmem_limit_bytes=vmem_bytes)


def device(y, x, z, c):
    return ((y % 4) * 4 + (x % 4)) * 8 + (z % 4) * 2 + (c % 2)


def shifted(value, moves):
    pairs = []
    for y in range(4):
        for x in range(4):
            for z in range(4):
                for c in range(2):
                    dy, dx, dz = moves[c]
                    pairs.append((device(y, x, z, c), device(y + dy, x + dx, z + dz, c)))
    return lax.ppermute(value, axes_all, pairs)


def scaled(moves, step):
    return [tuple(step * part for part in move) for move in moves]


def core_swap(value):
    pairs = [(d, d ^ 1) for d in range(owners)]
    return lax.ppermute(value, axes_all, pairs)


first_moves = [(2, 0, 1), (0, 2, 1)]
second_moves = [(0, 1, 0), (1, 0, 0)]
third_moves = [(1, 0, 0), (0, 1, 0)]
side_moves = [(0, 0, 1), (0, 0, -1)]


def around(value, moves):
    return [value] + [shifted(value, scaled(moves, step)) for step in (2, 1, -1)]


def offset(index):
    return jnp.where(index == 1, 2, jnp.where(index == 2, 3, jnp.where(index == 3, 1, 0)))


def slot_owners():
    sub, lam = lax.axis_index("sub"), lax.axis_index("lam")
    y, x, z, c = sub // 4, sub % 4, lam // 2, lam % 2
    index = lax.broadcasted_iota(jnp.int32, (owners, chunk), 0)
    side, third = index >> 6, (index >> 4) & 3
    second, first = (index >> 2) & 3, index & 3
    core = side ^ c
    turn = offset(first)
    along = 2 * turn + jnp.where(third == 2, 3, jnp.where(third == 3, 1, 0))
    up = turn + jnp.where(third == 1, jnp.where(core == 0, 3, 1), 0)
    dx = jnp.where(core == 0, offset(second), along)
    dy = jnp.where(core == 0, along, offset(second))
    return ((((y + dy) & 3) << 2) + ((x + dx) & 3)) * 8 + ((z + up) & 3) * 2 + core


def rank_kernel(owner_ref, slot_ref):
    table = slot_owners()
    row = lax.broadcasted_iota(jnp.int32, (chunk, chunk + owners), 0)
    col = lax.broadcasted_iota(jnp.int32, (chunk, chunk + owners), 1)
    earlier = jnp.where((row < col) | (col >= chunk), 1.0, 0.0).astype(jnp.bfloat16)
    start = cap * lax.broadcasted_iota(jnp.int32, (owners, owners), 0).astype(jnp.float32)
    for j in range(0, rows, chunk):
        hit = table == owner_ref[:, j : j + chunk]
        count = jnp.dot(
            jnp.where(hit, 1.0, 0.0).astype(jnp.bfloat16), earlier, preferred_element_type=jnp.float32
        )
        place = count[:, :chunk] + jnp.concatenate([start, start], axis=1)
        slot = jnp.sum(jnp.where(hit, place, 0.0), axis=0, keepdims=True)
        slot_ref[:, j : j + chunk] = slot.astype(jnp.int32)
        start = start + count[:, chunk:]


def rank(owner):
    return pl.pallas_call(
        rank_kernel,
        out_shape=jax.ShapeDtypeStruct((1, rows), jnp.int32),
        compiler_params=params(),
        cost_estimate=pl.CostEstimate(flops=2 * 128 * 4096 * 384, bytes_accessed=100000, transcendentals=0),
    )(owner)


def sort_kernel(slot_ref, field_ref, near_ref, own_ref, side_ref, pair_ref, wide, placed):
    wide[...] = field_ref[...].astype(jnp.float32)

    def body(i, carry):
        first = pl.multiple_of(i * unroll, unroll)
        for j in range(unroll):
            placed[pl.ds(slot_ref[first + j], 1), :] = wide[pl.ds(first + j, 1), :]
        return carry

    lax.fori_loop(0, rows // unroll, body, 0)
    near_ref[...] = placed[:half].astype(jnp.bfloat16)
    own_ref[...] = placed[half : half + block].astype(jnp.bfloat16)
    side_ref[...] = placed[half + block : half + 2 * block].astype(jnp.bfloat16)
    pair_ref[...] = placed[half + 2 * block :].astype(jnp.bfloat16)


def sort_rows(slot, field):
    return pl.pallas_call(
        sort_kernel,
        in_specs=[pl.BlockSpec(memory_space=pltpu.SMEM), in_vmem],
        out_specs=[in_vmem] * 4,
        out_shape=[
            jax.ShapeDtypeStruct((count * block, vals), jnp.bfloat16) for count in (4, 1, 1, 2)
        ],
        scratch_shapes=[pltpu.VMEM((rows, vals), jnp.float32), pltpu.VMEM((slots, vals), jnp.float32)],
        compiler_params=params(),
        cost_estimate=pl.CostEstimate(flops=0, bytes_accessed=20000000, transcendentals=0),
    )(slot, field)


def halo(choice, own_ref, next_ref, label):
    def ends(ref, second):
        top = second * stride + group
        return ref[top : top + 16, :].astype(jnp.float32)

    nothing = jnp.zeros((16, vals), jnp.float32)
    across = jnp.where(choice == 2, ends(next_ref, 0), nothing)
    corner = jnp.where(choice == 1, ends(next_ref, label), across)
    return jnp.where(choice == 0, ends(own_ref, label), corner).astype(jnp.bfloat16)


def ends_kernel(own_ref, before_ref, after_ref, coupling_ref, plane_ref, out_ref):
    plane = plane_ref[...]
    sub, lam = lax.axis_index("sub"), lax.axis_index("lam")
    x, inner = sub % 4, jnp.where(lam % 2 == 0, 0, 2)
    choice = jnp.where(sub == 0, 3, jnp.where(x == 0, 1, inner))
    before = halo(choice, own_ref, before_ref, 2)
    choice = jnp.where(sub == 15, 3, jnp.where(x == 3, 1, inner))
    after = halo(choice, own_ref, after_ref, 3)
    before = jnp.dot(before, plane, preferred_element_type=jnp.float32)[15:16]
    after = jnp.dot(after, plane, preferred_element_type=jnp.float32)[0:1]
    out_ref[0:1, :] = step_size * coupling_ref[0:1, 0:1] * before
    out_ref[1:2, :] = step_size * coupling_ref[31:32, 127:128] * after


def end_terms(own, before, after, coupling, plane):
    return pl.pallas_call(
        ends_kernel,
        in_specs=[in_vmem] * 5,
        out_specs=in_vmem,
        out_shape=jax.ShapeDtypeStruct((8, vals), jnp.float32),
        compiler_params=params(),
        cost_estimate=pl.CostEstimate(flops=1000, bytes_accessed=1000, transcendentals=0),
    )(own, before, after, coupling, plane)


def stencil_kernel(field_ref, coupling_ref, plane_ref, base_ref, projected):
    plane = plane_ref[...]
    projected[0:8, :] = jnp.zeros((8, vals), jnp.float32)
    projected[rows + 8 : rows + 16, :] = jnp.zeros((8, vals), jnp.float32)
    for j in range(rows // 512):
        projected[8 + j * 512 : 8 + (j + 1) * 512, :] = jnp.dot(
            field_ref[j * 512 : (j + 1) * 512, :], plane, preferred_element_type=jnp.float32
        )
    for j in range(rows // vals):
        lo = j * vals
        weight = jnp.broadcast_to(coupling_ref[j : j + 1, :], (vals, vals)).T
        here = projected[lo + 8 : lo + 8 + vals, :]
        before = projected[lo + 7 : lo + 7 + vals, :]
        after = projected[lo + 9 : lo + 9 + vals, :]
        field = field_ref[lo : lo + vals, :].astype(jnp.float32)
        base_ref[lo : lo + vals, :] = field - step_size * (weight * (2.0 * here - before - after))


def stencil(field, coupling, plane):
    return pl.pallas_call(
        stencil_kernel,
        in_specs=[in_vmem] * 3,
        out_specs=in_vmem,
        out_shape=jax.ShapeDtypeStruct((rows, vals), jnp.float32),
        scratch_shapes=[pltpu.VMEM((rows + 16, vals), jnp.float32)],
        compiler_params=params(),
        cost_estimate=pl.CostEstimate(flops=1000, bytes_accessed=1000, transcendentals=0),
    )(field, coupling, plane)


def respond(block, operator):
    response = jnp.dot(block, operator, preferred_element_type=jnp.float32)
    square = response * response
    magnitude = square + pltpu.roll(square, vals // 2, 1)
    reluct = 5.0 - 4.0 / (1.0 + magnitude)
    return reluct * response


def effect_kernel(sources, places, rows_ref, *refs):
    operators, out_ref = refs[: len(sources)], refs[-1]
    for source, place, operator_ref in zip(sources, places, operators):
        for k in range(16):
            top = k // 4 * stride + k % 4 * vals
            lo, out = source * block + k * cap, place * block + k * cap
            effect = respond(rows_ref[lo : lo + cap, :], operator_ref[top : top + vals, :])
            out_ref[out : out + cap, :] = effect.astype(out_ref.dtype)


def effect_call(operands, sources, places, shape, dtype, aliases):
    return pl.pallas_call(
        functools.partial(effect_kernel, sources, places),
        in_specs=[in_vmem] * len(operands),
        out_specs=in_vmem,
        out_shape=jax.ShapeDtypeStruct((shape, vals), dtype),
        input_output_aliases=aliases,
        compiler_params=params(),
        cost_estimate=pl.CostEstimate(flops=1000, bytes_accessed=1000, transcendentals=0),
    )(*operands)


def replies(guest, operators, sources):
    count = len(sources)
    return effect_call([guest, *operators], sources, range(count), count * block, jnp.bfloat16, {})


def effects(near, operators, thirds, previous):
    operands = [near, *operators]
    aliases = {}
    if previous is not None:
        aliases = {len(operands): 0}
        operands.append(previous)
    return effect_call(operands, thirds, thirds, slots, jnp.float32, aliases)


part_tops = (0, 1024, 2048, 3072, 3584, 3840, rows)


def final_kernel(
    slot_ref, base_ref, ends_ref, own_ref, pair_ref, side_ref, _, out_ref, effect_ref, result, sent
):
    for returned_ref, third in ((own_ref, 0), (pair_ref, 2), (side_ref, 1)):
        lo = half + third * block
        effect_ref[lo : lo + returned_ref.shape[0], :] = returned_ref[...].astype(jnp.float32)

    copies = []
    for number, (top, end) in enumerate(zip(part_tops, part_tops[1:])):

        def body(i, carry):
            first = pl.multiple_of(top + i * long_unroll, long_unroll)
            for j in range(long_unroll):
                effect = effect_ref[pl.ds(slot_ref[first + j], 1), :]
                row = pl.ds(first + j, 1)
                result[row, :] = base_ref[row, :] - step_size * effect
            return carry

        lax.fori_loop(0, (end - top) // long_unroll, body, 0)
        if top == 0:
            result[0:1, :] = result[0:1, :] + ends_ref[0:1, :]
        if end == rows:
            result[rows - 1 : rows, :] = result[rows - 1 : rows, :] + ends_ref[1:2, :]
        span = slice(top, end)
        copies.append(pltpu.make_async_copy(result.at[span], out_ref.at[span], sent.at[number]))
        copies[-1].start()
    for copy in copies:
        copy.wait()


def finish(slot, base, ends, returned, effect):
    operands = [slot, base, ends, *returned, effect]
    return pl.pallas_call(
        final_kernel,
        in_specs=[pl.BlockSpec(memory_space=pltpu.SMEM)] + [in_vmem] * (len(operands) - 1),
        out_specs=[pl.BlockSpec(memory_space=pl.ANY), in_vmem],
        out_shape=[
            jax.ShapeDtypeStruct((rows, vals), jnp.float32),
            jax.ShapeDtypeStruct((slots, vals), jnp.float32),
        ],
        input_output_aliases={len(operands) - 1: 1},
        scratch_shapes=[
            pltpu.VMEM((rows, vals), jnp.float32),
            pltpu.SemaphoreType.DMA((len(part_tops) - 1,)),
        ],
        compiler_params=params(),
        cost_estimate=pl.CostEstimate(flops=4096 * 128, bytes_accessed=10000000, transcendentals=0),
    )(*operands)[0]


def per_device(edge_field, coupling, owner_map, in_plane, profile_op):
    field = edge_field[0]
    tied = lax.optimization_barrier
    tips = jnp.concatenate([field[:8], field[rows - 8 :]], axis=0)
    near = jnp.concatenate([*around(profile_op[0], first_moves), tips], axis=0)
    slot = rank(owner_map.transpose(0, 2, 1)[0]).reshape(rows)
    near, slot = tied((near, slot))
    plane = jnp.concatenate(around(near, second_moves), axis=0)
    near_rows, *far_rows = sort_rows(slot, field)
    plane, near_rows, *far_rows = tied((plane, near_rows, *far_rows))
    plus, minus = shifted(plane, third_moves), shifted(plane, scaled(third_moves, -1))
    side = shifted(plane, side_moves)
    own_guest, side_guest, pair_guest = [core_swap(part) for part in far_rows]
    weights = coupling.reshape(rows // vals, vals)
    base = stencil(field, weights, in_plane)
    reply = core_swap(replies(own_guest, [plane], (0,)))
    effect = effects(near_rows, [plane], (0,), None)
    minus, plus, effect, reply, base = tied((minus, plus, effect, reply, base))
    returned = [reply]
    returned.append(core_swap(replies(pair_guest, [plus, minus], (0, 1))))
    returned.append(core_swap(replies(side_guest, [side], (0,))))
    effect = effects(near_rows, [side, plus, minus], (1, 2, 3), effect)
    ends = end_terms(plane, plus, minus, weights, in_plane)
    return finish(slot, base, ends, returned, effect)[None]


def solution(mesh):
    placed = (
        P("lam", "sub", None),
        P("lam", "sub"),
        P("lam", "sub", None),
        P(),
        P(("sub", "lam"), None, None),
    )
    return jax.shard_map(
        per_device, mesh=mesh, in_specs=placed, out_specs=P("lam", "sub", None), check_vma=False
    )
```

```python
import functools

import jax
import jax.numpy as jnp
from jax import lax
from jax.experimental import pallas as pl
from jax.experimental.pallas import tpu as pltpu
from jax.sharding import PartitionSpec as P

step_size = 0.25
axes_all = ("sub", "lam")
owners = 128
cap = 48
rows = 4096
vals = 128
slots = owners * cap
half = slots // 2
block = 16 * cap
chunk = 256
unroll = 128
long_unroll = 256
group = 4 * vals
stride = group + 16
vmem_bytes = 20 * 1024 * 1024


in_vmem = pl.BlockSpec(memory_space=pltpu.VMEM)


def params():
    return pltpu.CompilerParams(vmem_limit_bytes=vmem_bytes)


def device(y, x, z, c):
    return ((y % 4) * 4 + (x % 4)) * 8 + (z % 4) * 2 + (c % 2)


def shifted(value, moves):
    pairs = []
    for y in range(4):
        for x in range(4):
            for z in range(4):
                for c in range(2):
                    dy, dx, dz = moves[c]
                    pairs.append((device(y, x, z, c), device(y + dy, x + dx, z + dz, c)))
    return lax.ppermute(value, axes_all, pairs)


def scaled(moves, step):
    return [tuple(step * part for part in move) for move in moves]


def core_swap(value):
    pairs = [(d, d ^ 1) for d in range(owners)]
    return lax.ppermute(value, axes_all, pairs)


first_moves = [(2, 0, 1), (0, 2, 1)]
second_moves = [(0, 1, 0), (1, 0, 0)]
third_moves = [(1, 0, 0), (0, 1, 0)]
side_moves = [(0, 0, 1), (0, 0, -1)]


def around(value, moves):
    return [value] + [shifted(value, scaled(moves, step)) for step in (2, 1, -1)]


def offset(index):
    return jnp.where(index == 1, 2, jnp.where(index == 2, 3, jnp.where(index == 3, 1, 0)))


def slot_owners():
    sub, lam = lax.axis_index("sub"), lax.axis_index("lam")
    y, x, z, c = sub // 4, sub % 4, lam // 2, lam % 2
    index = lax.broadcasted_iota(jnp.int32, (owners, chunk), 0)
    side, third = index >> 6, (index >> 4) & 3
    second, first = (index >> 2) & 3, index & 3
    core = side ^ c
    turn = offset(first)
    along = 2 * turn + jnp.where(third == 2, 3, jnp.where(third == 3, 1, 0))
    up = turn + jnp.where(third == 1, jnp.where(core == 0, 3, 1), 0)
    dx = jnp.where(core == 0, offset(second), along)
    dy = jnp.where(core == 0, along, offset(second))
    return ((((y + dy) & 3) << 2) + ((x + dx) & 3)) * 8 + ((z + up) & 3) * 2 + core


def rank_kernel(owner_ref, slot_ref):
    table = slot_owners()
    row = lax.broadcasted_iota(jnp.int32, (chunk, chunk + owners), 0)
    col = lax.broadcasted_iota(jnp.int32, (chunk, chunk + owners), 1)
    earlier = jnp.where((row < col) | (col >= chunk), 1.0, 0.0).astype(jnp.bfloat16)
    start = cap * lax.broadcasted_iota(jnp.int32, (owners, owners), 0).astype(jnp.float32)
    for j in range(0, rows, chunk):
        hit = table == owner_ref[:, j : j + chunk]
        count = jnp.dot(
            jnp.where(hit, 1.0, 0.0).astype(jnp.bfloat16), earlier, preferred_element_type=jnp.float32
        )
        place = count[:, :chunk] + jnp.concatenate([start, start], axis=1)
        slot = jnp.sum(jnp.where(hit, place, 0.0), axis=0, keepdims=True)
        slot_ref[:, j : j + chunk] = slot.astype(jnp.int32)
        start = start + count[:, chunk:]


def rank(owner):
    return pl.pallas_call(
        rank_kernel,
        out_shape=jax.ShapeDtypeStruct((1, rows), jnp.int32),
        compiler_params=params(),
        cost_estimate=pl.CostEstimate(flops=2 * 128 * 4096 * 384, bytes_accessed=100000, transcendentals=0),
    )(owner)


def sort_kernel(slot_ref, field_ref, near_ref, own_ref, side_ref, plus_ref, minus_ref, wide, placed):
    wide[...] = field_ref[...].astype(jnp.float32)

    def body(i, carry):
        first = pl.multiple_of(i * unroll, unroll)
        for j in range(unroll):
            placed[pl.ds(slot_ref[first + j], 1), :] = wide[pl.ds(first + j, 1), :]
        return carry

    lax.fori_loop(0, rows // unroll, body, 0)
    near_ref[...] = placed[:half].astype(jnp.bfloat16)
    for third, far_ref in enumerate((own_ref, side_ref, plus_ref, minus_ref)):
        lo = half + third * block
        far_ref[...] = placed[lo : lo + block].astype(jnp.bfloat16)


def sort_rows(slot, field):
    return pl.pallas_call(
        sort_kernel,
        in_specs=[pl.BlockSpec(memory_space=pltpu.SMEM), in_vmem],
        out_specs=[in_vmem] * 5,
        out_shape=[
            jax.ShapeDtypeStruct((count * block, vals), jnp.bfloat16) for count in (4, 1, 1, 1, 1)
        ],
        scratch_shapes=[pltpu.VMEM((rows, vals), jnp.float32), pltpu.VMEM((slots, vals), jnp.float32)],
        compiler_params=params(),
        cost_estimate=pl.CostEstimate(flops=0, bytes_accessed=20000000, transcendentals=0),
    )(slot, field)


def halo(choice, own_ref, next_ref, label):
    def ends(ref, second):
        top = second * stride + group
        return ref[top : top + 16, :].astype(jnp.float32)

    nothing = jnp.zeros((16, vals), jnp.float32)
    across = jnp.where(choice == 2, ends(next_ref, 0), nothing)
    corner = jnp.where(choice == 1, ends(next_ref, label), across)
    return jnp.where(choice == 0, ends(own_ref, label), corner).astype(jnp.bfloat16)


def ends_kernel(own_ref, before_ref, after_ref, coupling_ref, plane_ref, out_ref):
    plane = plane_ref[...]
    sub, lam = lax.axis_index("sub"), lax.axis_index("lam")
    x, inner = sub % 4, jnp.where(lam % 2 == 0, 0, 2)
    choice = jnp.where(sub == 0, 3, jnp.where(x == 0, 1, inner))
    before = halo(choice, own_ref, before_ref, 2)
    choice = jnp.where(sub == 15, 3, jnp.where(x == 3, 1, inner))
    after = halo(choice, own_ref, after_ref, 3)
    before = jnp.dot(before, plane, preferred_element_type=jnp.float32)[15:16]
    after = jnp.dot(after, plane, preferred_element_type=jnp.float32)[0:1]
    out_ref[0:1, :] = step_size * coupling_ref[0:1, 0:1] * before
    out_ref[1:2, :] = step_size * coupling_ref[31:32, 127:128] * after


def end_terms(own, before, after, coupling, plane):
    return pl.pallas_call(
        ends_kernel,
        in_specs=[in_vmem] * 5,
        out_specs=in_vmem,
        out_shape=jax.ShapeDtypeStruct((8, vals), jnp.float32),
        compiler_params=params(),
        cost_estimate=pl.CostEstimate(flops=1000, bytes_accessed=1000, transcendentals=0),
    )(own, before, after, coupling, plane)


def stencil_kernel(field_ref, coupling_ref, plane_ref, base_ref, projected):
    plane = plane_ref[...]
    projected[0:8, :] = jnp.zeros((8, vals), jnp.float32)
    projected[rows + 8 : rows + 16, :] = jnp.zeros((8, vals), jnp.float32)
    for j in range(rows // 512):
        projected[8 + j * 512 : 8 + (j + 1) * 512, :] = jnp.dot(
            field_ref[j * 512 : (j + 1) * 512, :], plane, preferred_element_type=jnp.float32
        )
    for j in range(rows // vals):
        lo = j * vals
        weight = jnp.broadcast_to(coupling_ref[j : j + 1, :], (vals, vals)).T
        here = projected[lo + 8 : lo + 8 + vals, :]
        before = projected[lo + 7 : lo + 7 + vals, :]
        after = projected[lo + 9 : lo + 9 + vals, :]
        field = field_ref[lo : lo + vals, :].astype(jnp.float32)
        base_ref[lo : lo + vals, :] = field - step_size * (weight * (2.0 * here - before - after))


def stencil(field, coupling, plane):
    return pl.pallas_call(
        stencil_kernel,
        in_specs=[in_vmem] * 3,
        out_specs=in_vmem,
        out_shape=jax.ShapeDtypeStruct((rows, vals), jnp.float32),
        scratch_shapes=[pltpu.VMEM((rows + 16, vals), jnp.float32)],
        compiler_params=params(),
        cost_estimate=pl.CostEstimate(flops=1000, bytes_accessed=1000, transcendentals=0),
    )(field, coupling, plane)


def respond(block, operator):
    response = jnp.dot(block, operator, preferred_element_type=jnp.float32)
    square = response * response
    magnitude = square + pltpu.roll(square, vals // 2, 1)
    reluct = 5.0 - 4.0 / (1.0 + magnitude)
    return reluct * response


def effect_kernel(sources, places, *refs):
    operators, out_ref = refs[: len(sources)], refs[-1]
    for (number, source), place, operator_ref in zip(sources, places, operators):
        rows_ref = refs[len(sources) + number]
        for k in range(16):
            top = k // 4 * stride + k % 4 * vals
            lo, out = source * block + k * cap, place * block + k * cap
            effect = respond(rows_ref[lo : lo + cap, :], operator_ref[top : top + vals, :])
            out_ref[out : out + cap, :] = effect.astype(out_ref.dtype)


def effect_call(operands, sources, places, shape, dtype, aliases):
    return pl.pallas_call(
        functools.partial(effect_kernel, sources, places),
        in_specs=[in_vmem] * len(operands),
        out_specs=in_vmem,
        out_shape=jax.ShapeDtypeStruct((shape, vals), dtype),
        input_output_aliases=aliases,
        compiler_params=params(),
        cost_estimate=pl.CostEstimate(flops=1000, bytes_accessed=1000, transcendentals=0),
    )(*operands)


def replies(operators, guests):
    count = len(guests)
    sources = [(number, 0) for number in range(count)]
    return effect_call([*operators, *guests], sources, range(count), count * block, jnp.bfloat16, {})


def effects(near, operators, thirds, previous):
    operands = [*operators, near]
    aliases = {}
    if previous is not None:
        aliases = {len(operands): 0}
        operands.append(previous)
    sources = [(0, third) for third in thirds]
    return effect_call(operands, sources, thirds, slots, jnp.float32, aliases)


part_tops = (0, 1024, 2048, 3072, 3584, 3840, rows)


def final_kernel(
    slot_ref, base_ref, ends_ref, own_ref, pair_ref, side_ref, _, out_ref, effect_ref, result, sent
):
    for returned_ref, first, third in ((own_ref, 0, 0), (pair_ref, 0, 2), (pair_ref, 1, 3), (side_ref, 0, 1)):
        lo, top = half + third * block, first * block
        effect_ref[lo : lo + block, :] = returned_ref[top : top + block, :].astype(jnp.float32)

    copies = []
    for number, (top, end) in enumerate(zip(part_tops, part_tops[1:])):

        def body(i, carry):
            first = pl.multiple_of(top + i * long_unroll, long_unroll)
            for j in range(long_unroll):
                effect = effect_ref[pl.ds(slot_ref[first + j], 1), :]
                row = pl.ds(first + j, 1)
                result[row, :] = base_ref[row, :] - step_size * effect
            return carry

        lax.fori_loop(0, (end - top) // long_unroll, body, 0)
        if top == 0:
            result[0:1, :] = result[0:1, :] + ends_ref[0:1, :]
        if end == rows:
            result[rows - 1 : rows, :] = result[rows - 1 : rows, :] + ends_ref[1:2, :]
        span = slice(top, end)
        copies.append(pltpu.make_async_copy(result.at[span], out_ref.at[span], sent.at[number]))
        copies[-1].start()
    for copy in copies:
        copy.wait()


def finish(slot, base, ends, returned, effect):
    operands = [slot, base, ends, *returned, effect]
    return pl.pallas_call(
        final_kernel,
        in_specs=[pl.BlockSpec(memory_space=pltpu.SMEM)] + [in_vmem] * (len(operands) - 1),
        out_specs=[pl.BlockSpec(memory_space=pl.ANY), in_vmem],
        out_shape=[
            jax.ShapeDtypeStruct((rows, vals), jnp.float32),
            jax.ShapeDtypeStruct((slots, vals), jnp.float32),
        ],
        input_output_aliases={len(operands) - 1: 1},
        scratch_shapes=[
            pltpu.VMEM((rows, vals), jnp.float32),
            pltpu.SemaphoreType.DMA((len(part_tops) - 1,)),
        ],
        compiler_params=params(),
        cost_estimate=pl.CostEstimate(flops=4096 * 128, bytes_accessed=10000000, transcendentals=0),
    )(*operands)[0]


def per_device(edge_field, coupling, owner_map, in_plane, profile_op):
    field = edge_field[0]
    tied = lax.optimization_barrier
    tips = jnp.concatenate([field[:8], field[rows - 8 :]], axis=0)
    near = jnp.concatenate([*around(profile_op[0], first_moves), tips], axis=0)
    slot = rank(owner_map.transpose(0, 2, 1)[0]).reshape(rows)
    near, slot = tied((near, slot))
    plane = jnp.concatenate(around(near, second_moves), axis=0)
    near_rows, *far_rows = sort_rows(slot, field)
    plane, near_rows, *far_rows = tied((plane, near_rows, *far_rows))
    plus, minus = shifted(plane, third_moves), shifted(plane, scaled(third_moves, -1))
    side = shifted(plane, side_moves)
    own_guest, side_guest, *pair_guests = [core_swap(part) for part in far_rows]
    weights = coupling.reshape(rows // vals, vals)
    base = stencil(field, weights, in_plane)
    effect = effects(near_rows, [plane], (0,), None)
    reply = replies([plane], [own_guest])
    minus, plus, effect, base, reply = tied((minus, plus, effect, base, reply))
    returned = [core_swap(reply)]
    returned.append(core_swap(replies([plus, minus], pair_guests)))
    returned.append(core_swap(replies([side], [side_guest])))
    effect = effects(near_rows, [side, plus, minus], (1, 2, 3), effect)
    ends = end_terms(plane, plus, minus, weights, in_plane)
    return finish(slot, base, ends, returned, effect)[None]


def solution(mesh):
    placed = (
        P("lam", "sub", None),
        P("lam", "sub"),
        P("lam", "sub", None),
        P(),
        P(("sub", "lam"), None, None),
    )
    return jax.shard_map(
        per_device, mesh=mesh, in_specs=placed, out_specs=P("lam", "sub", None), check_vma=False
    )
```

```python
import functools

import jax
import jax.numpy as jnp
from jax import lax
from jax.experimental import pallas as pl
from jax.experimental.pallas import tpu as pltpu
from jax.sharding import PartitionSpec as P

step_size = 0.25
axes_all = ("sub", "lam")
owners = 128
cap = 48
rows = 4096
vals = 128
slots = owners * cap
half = slots // 2
block = 16 * cap
chunk = 256
unroll = 128
long_unroll = 256
group = 4 * vals
stride = group + 16
vmem_bytes = 20 * 1024 * 1024


in_vmem = pl.BlockSpec(memory_space=pltpu.VMEM)


def params():
    return pltpu.CompilerParams(vmem_limit_bytes=vmem_bytes)


def device(y, x, z, c):
    return ((y % 4) * 4 + (x % 4)) * 8 + (z % 4) * 2 + (c % 2)


def shifted(value, moves):
    pairs = []
    for y in range(4):
        for x in range(4):
            for z in range(4):
                for c in range(2):
                    dy, dx, dz = moves[c]
                    pairs.append((device(y, x, z, c), device(y + dy, x + dx, z + dz, c)))
    return lax.ppermute(value, axes_all, pairs)


def scaled(moves, step):
    return [tuple(step * part for part in move) for move in moves]


def core_swap(value):
    pairs = [(d, d ^ 1) for d in range(owners)]
    return lax.ppermute(value, axes_all, pairs)


first_moves = [(2, 0, 1), (0, 2, 1)]
second_moves = [(0, 1, 0), (1, 0, 0)]
third_moves = [(1, 0, 0), (0, 1, 0)]
side_moves = [(0, 0, 1), (0, 0, -1)]


def around(value, moves):
    return [value] + [shifted(value, scaled(moves, step)) for step in (-1, 1, 2)]


def offset(index):
    return jnp.where(index == 1, 1, jnp.where(index == 2, 3, jnp.where(index == 3, 2, 0)))


def slot_owners():
    sub, lam = lax.axis_index("sub"), lax.axis_index("lam")
    y, x, z, c = sub // 4, sub % 4, lam // 2, lam % 2
    index = lax.broadcasted_iota(jnp.int32, (owners, chunk), 0)
    side, third = index >> 6, (index >> 4) & 3
    second, first = (index >> 2) & 3, index & 3
    core = side ^ c
    turn = offset(first)
    along = 2 * turn + jnp.where(third == 2, 3, jnp.where(third == 3, 1, 0))
    up = turn + jnp.where(third == 1, jnp.where(core == 0, 3, 1), 0)
    dx = jnp.where(core == 0, offset(second), along)
    dy = jnp.where(core == 0, along, offset(second))
    return ((((y + dy) & 3) << 2) + ((x + dx) & 3)) * 8 + ((z + up) & 3) * 2 + core


def rank_kernel(owner_ref, slot_ref):
    table = slot_owners()
    row = lax.broadcasted_iota(jnp.int32, (chunk, chunk + owners), 0)
    col = lax.broadcasted_iota(jnp.int32, (chunk, chunk + owners), 1)
    earlier = jnp.where((row < col) | (col >= chunk), 1.0, 0.0).astype(jnp.bfloat16)
    start = cap * lax.broadcasted_iota(jnp.int32, (owners, owners), 0).astype(jnp.float32)
    for j in range(0, rows, chunk):
        hit = table == owner_ref[:, j : j + chunk]
        count = jnp.dot(
            jnp.where(hit, 1.0, 0.0).astype(jnp.bfloat16), earlier, preferred_element_type=jnp.float32
        )
        place = count[:, :chunk] + jnp.concatenate([start, start], axis=1)
        slot = jnp.sum(jnp.where(hit, place, 0.0), axis=0, keepdims=True)
        slot_ref[:, j : j + chunk] = slot.astype(jnp.int32)
        start = start + count[:, chunk:]


def rank(owner):
    return pl.pallas_call(
        rank_kernel,
        out_shape=jax.ShapeDtypeStruct((1, rows), jnp.int32),
        compiler_params=params(),
        cost_estimate=pl.CostEstimate(flops=2 * 128 * 4096 * 384, bytes_accessed=100000, transcendentals=0),
    )(owner)


def sort_kernel(slot_ref, field_ref, near_ref, own_ref, side_ref, pair_ref, wide, placed):
    wide[...] = field_ref[...].astype(jnp.float32)

    def body(i, carry):
        first = pl.multiple_of(i * unroll, unroll)
        for j in range(unroll):
            placed[pl.ds(slot_ref[first + j], 1), :] = wide[pl.ds(first + j, 1), :]
        return carry

    lax.fori_loop(0, rows // unroll, body, 0)
    near_ref[...] = placed[:half].astype(jnp.bfloat16)
    own_ref[...] = placed[half : half + block].astype(jnp.bfloat16)
    side_ref[...] = placed[half + block : half + 2 * block].astype(jnp.bfloat16)
    pair_ref[...] = placed[half + 2 * block :].astype(jnp.bfloat16)


def sort_rows(slot, field):
    return pl.pallas_call(
        sort_kernel,
        in_specs=[pl.BlockSpec(memory_space=pltpu.SMEM), in_vmem],
        out_specs=[in_vmem] * 4,
        out_shape=[
            jax.ShapeDtypeStruct((count * block, vals), jnp.bfloat16) for count in (4, 1, 1, 2)
        ],
        scratch_shapes=[pltpu.VMEM((rows, vals), jnp.float32), pltpu.VMEM((slots, vals), jnp.float32)],
        compiler_params=params(),
        cost_estimate=pl.CostEstimate(flops=0, bytes_accessed=20000000, transcendentals=0),
    )(slot, field)


def halo(choice, own_ref, next_ref, label):
    def ends(ref, second):
        top = second * stride + group
        return ref[top : top + 16, :].astype(jnp.float32)

    nothing = jnp.zeros((16, vals), jnp.float32)
    across = jnp.where(choice == 2, ends(next_ref, 0), nothing)
    corner = jnp.where(choice == 1, ends(next_ref, label), across)
    return jnp.where(choice == 0, ends(own_ref, label), corner).astype(jnp.bfloat16)


def ends_kernel(own_ref, before_ref, after_ref, coupling_ref, plane_ref, out_ref):
    plane = plane_ref[...]
    sub, lam = lax.axis_index("sub"), lax.axis_index("lam")
    x, inner = sub % 4, jnp.where(lam % 2 == 0, 0, 2)
    choice = jnp.where(sub == 0, 3, jnp.where(x == 0, 1, inner))
    before = halo(choice, own_ref, before_ref, 2)
    choice = jnp.where(sub == 15, 3, jnp.where(x == 3, 1, inner))
    after = halo(choice, own_ref, after_ref, 1)
    before = jnp.dot(before, plane, preferred_element_type=jnp.float32)[15:16]
    after = jnp.dot(after, plane, preferred_element_type=jnp.float32)[0:1]
    out_ref[0:1, :] = step_size * coupling_ref[0:1, 0:1] * before
    out_ref[1:2, :] = step_size * coupling_ref[31:32, 127:128] * after


def end_terms(own, before, after, coupling, plane):
    return pl.pallas_call(
        ends_kernel,
        in_specs=[in_vmem] * 5,
        out_specs=in_vmem,
        out_shape=jax.ShapeDtypeStruct((8, vals), jnp.float32),
        compiler_params=params(),
        cost_estimate=pl.CostEstimate(flops=1000, bytes_accessed=1000, transcendentals=0),
    )(own, before, after, coupling, plane)


def stencil_kernel(field_ref, coupling_ref, plane_ref, base_ref, projected):
    plane = plane_ref[...]
    projected[0:8, :] = jnp.zeros((8, vals), jnp.float32)
    projected[rows + 8 : rows + 16, :] = jnp.zeros((8, vals), jnp.float32)
    for j in range(rows // 512):
        projected[8 + j * 512 : 8 + (j + 1) * 512, :] = jnp.dot(
            field_ref[j * 512 : (j + 1) * 512, :], plane, preferred_element_type=jnp.float32
        )
    for j in range(rows // vals):
        lo = j * vals
        weight = jnp.broadcast_to(coupling_ref[j : j + 1, :], (vals, vals)).T
        here = projected[lo + 8 : lo + 8 + vals, :]
        before = projected[lo + 7 : lo + 7 + vals, :]
        after = projected[lo + 9 : lo + 9 + vals, :]
        field = field_ref[lo : lo + vals, :].astype(jnp.float32)
        base_ref[lo : lo + vals, :] = field - step_size * (weight * (2.0 * here - before - after))


def stencil(field, coupling, plane):
    return pl.pallas_call(
        stencil_kernel,
        in_specs=[in_vmem] * 3,
        out_specs=in_vmem,
        out_shape=jax.ShapeDtypeStruct((rows, vals), jnp.float32),
        scratch_shapes=[pltpu.VMEM((rows + 16, vals), jnp.float32)],
        compiler_params=params(),
        cost_estimate=pl.CostEstimate(flops=1000, bytes_accessed=1000, transcendentals=0),
    )(field, coupling, plane)


def respond(block, operator):
    response = jnp.dot(block, operator, preferred_element_type=jnp.float32)
    square = response * response
    magnitude = square + pltpu.roll(square, vals // 2, 1)
    reluct = 5.0 - 4.0 / (1.0 + magnitude)
    return reluct * response


def effect_kernel(sources, places, rows_ref, *refs):
    operators, out_ref = refs[: len(sources)], refs[-1]
    for source, place, operator_ref in zip(sources, places, operators):
        for k in range(16):
            top = k // 4 * stride + k % 4 * vals
            lo, out = source * block + k * cap, place * block + k * cap
            effect = respond(rows_ref[lo : lo + cap, :], operator_ref[top : top + vals, :])
            out_ref[out : out + cap, :] = effect.astype(out_ref.dtype)


def effect_call(operands, sources, places, shape, dtype, aliases):
    return pl.pallas_call(
        functools.partial(effect_kernel, sources, places),
        in_specs=[in_vmem] * len(operands),
        out_specs=in_vmem,
        out_shape=jax.ShapeDtypeStruct((shape, vals), dtype),
        input_output_aliases=aliases,
        compiler_params=params(),
        cost_estimate=pl.CostEstimate(flops=1000, bytes_accessed=1000, transcendentals=0),
    )(*operands)


def replies(guest, operators, sources):
    count = len(sources)
    return effect_call([guest, *operators], sources, range(count), count * block, jnp.bfloat16, {})


def effects(near, operators, thirds, previous):
    operands = [near, *operators]
    aliases = {}
    if previous is not None:
        aliases = {len(operands): 0}
        operands.append(previous)
    return effect_call(operands, thirds, thirds, slots, jnp.float32, aliases)


part_tops = (0, 1024, 2048, 3072, 3584, 3840, rows)


def final_kernel(
    slot_ref, base_ref, ends_ref, own_ref, pair_ref, side_ref, _, out_ref, effect_ref, result, sent
):
    for returned_ref, third in ((own_ref, 0), (pair_ref, 2), (side_ref, 1)):
        lo = half + third * block
        effect_ref[lo : lo + returned_ref.shape[0], :] = returned_ref[...].astype(jnp.float32)

    copies = []
    for number, (top, end) in enumerate(zip(part_tops, part_tops[1:])):

        def body(i, carry):
            first = pl.multiple_of(top + i * long_unroll, long_unroll)
            for j in range(long_unroll):
                effect = effect_ref[pl.ds(slot_ref[first + j], 1), :]
                row = pl.ds(first + j, 1)
                result[row, :] = base_ref[row, :] - step_size * effect
            return carry

        lax.fori_loop(0, (end - top) // long_unroll, body, 0)
        if top == 0:
            result[0:1, :] = result[0:1, :] + ends_ref[0:1, :]
        if end == rows:
            result[rows - 1 : rows, :] = result[rows - 1 : rows, :] + ends_ref[1:2, :]
        span = slice(top, end)
        copies.append(pltpu.make_async_copy(result.at[span], out_ref.at[span], sent.at[number]))
        copies[-1].start()
    for copy in copies:
        copy.wait()


def finish(slot, base, ends, returned, effect):
    operands = [slot, base, ends, *returned, effect]
    return pl.pallas_call(
        final_kernel,
        in_specs=[pl.BlockSpec(memory_space=pltpu.SMEM)] + [in_vmem] * (len(operands) - 1),
        out_specs=[pl.BlockSpec(memory_space=pl.ANY), in_vmem],
        out_shape=[
            jax.ShapeDtypeStruct((rows, vals), jnp.float32),
            jax.ShapeDtypeStruct((slots, vals), jnp.float32),
        ],
        input_output_aliases={len(operands) - 1: 1},
        scratch_shapes=[
            pltpu.VMEM((rows, vals), jnp.float32),
            pltpu.SemaphoreType.DMA((len(part_tops) - 1,)),
        ],
        compiler_params=params(),
        cost_estimate=pl.CostEstimate(flops=4096 * 128, bytes_accessed=10000000, transcendentals=0),
    )(*operands)[0]


def per_device(edge_field, coupling, owner_map, in_plane, profile_op):
    field = edge_field[0]
    tied = lax.optimization_barrier
    tips = jnp.concatenate([field[:8], field[rows - 8 :]], axis=0)
    near = jnp.concatenate([*around(profile_op[0], first_moves), tips], axis=0)
    slot = rank(owner_map.transpose(0, 2, 1)[0]).reshape(rows)
    near, slot = tied((near, slot))
    plane = jnp.concatenate(around(near, second_moves), axis=0)
    near_rows, *far_rows = sort_rows(slot, field)
    plane, near_rows, *far_rows = tied((plane, near_rows, *far_rows))
    plus, minus = shifted(plane, third_moves), shifted(plane, scaled(third_moves, -1))
    side = shifted(plane, side_moves)
    own_guest, side_guest, pair_guest = [core_swap(part) for part in far_rows]
    weights = coupling.reshape(rows // vals, vals)
    base = stencil(field, weights, in_plane)
    reply = core_swap(replies(own_guest, [plane], (0,)))
    effect = effects(near_rows, [plane], (0,), None)
    minus, plus, effect, reply, base = tied((minus, plus, effect, reply, base))
    returned = [reply]
    returned.append(core_swap(replies(pair_guest, [plus, minus], (0, 1))))
    returned.append(core_swap(replies(side_guest, [side], (0,))))
    effect = effects(near_rows, [side, plus, minus], (1, 2, 3), effect)
    ends = end_terms(plane, plus, minus, weights, in_plane)
    return finish(slot, base, ends, returned, effect)[None]


def solution(mesh):
    placed = (
        P("lam", "sub", None),
        P("lam", "sub"),
        P("lam", "sub", None),
        P(),
        P(("sub", "lam"), None, None),
    )
    return jax.shard_map(
        per_device, mesh=mesh, in_specs=placed, out_specs=P("lam", "sub", None), check_vma=False
    )
```

```python
import functools

import jax
import jax.numpy as jnp
from jax import lax
from jax.experimental import pallas as pl
from jax.experimental.pallas import tpu as pltpu
from jax.sharding import PartitionSpec as P

step_size = 0.25
axes_all = ("sub", "lam")
owners = 128
cap = 48
rows = 4096
vals = 128
slots = owners * cap
half = slots // 2
block = 16 * cap
chunk = 256
unroll = 128
long_unroll = 256
group = 4 * vals
stride = group + 16
vmem_bytes = 20 * 1024 * 1024


in_vmem = pl.BlockSpec(memory_space=pltpu.VMEM)


def params():
    return pltpu.CompilerParams(vmem_limit_bytes=vmem_bytes)


def device(y, x, z, c):
    return ((y % 4) * 4 + (x % 4)) * 8 + (z % 4) * 2 + (c % 2)


def shifted(value, moves):
    pairs = []
    for y in range(4):
        for x in range(4):
            for z in range(4):
                for c in range(2):
                    dy, dx, dz = moves[c]
                    pairs.append((device(y, x, z, c), device(y + dy, x + dx, z + dz, c)))
    return lax.ppermute(value, axes_all, pairs)


def scaled(moves, step):
    return [tuple(step * part for part in move) for move in moves]


def core_swap(value):
    pairs = [(d, d ^ 1) for d in range(owners)]
    return lax.ppermute(value, axes_all, pairs)


first_moves = [(2, 0, 1), (0, 2, 1)]
second_moves = [(0, 1, 0), (1, 0, 0)]
third_moves = [(1, 0, 0), (0, 1, 0)]
side_moves = [(0, 0, 1), (0, 0, -1)]


def around(value, moves):
    return [value] + [shifted(value, scaled(moves, step)) for step in (-1, 1, 2)]


def offset(index):
    return jnp.where(index == 1, 1, jnp.where(index == 2, 3, jnp.where(index == 3, 2, 0)))


def slot_owners():
    sub, lam = lax.axis_index("sub"), lax.axis_index("lam")
    y, x, z, c = sub // 4, sub % 4, lam // 2, lam % 2
    index = lax.broadcasted_iota(jnp.int32, (owners, chunk), 0)
    side, third = index >> 6, (index >> 4) & 3
    second, first = (index >> 2) & 3, index & 3
    core = side ^ c
    turn = offset(first)
    along = 2 * turn + jnp.where(third == 2, 3, jnp.where(third == 3, 1, 0))
    up = turn + jnp.where(third == 1, jnp.where(core == 0, 3, 1), 0)
    dx = jnp.where(core == 0, offset(second), along)
    dy = jnp.where(core == 0, along, offset(second))
    return ((((y + dy) & 3) << 2) + ((x + dx) & 3)) * 8 + ((z + up) & 3) * 2 + core


def rank_kernel(owner_ref, slot_ref):
    table = slot_owners()
    row = lax.broadcasted_iota(jnp.int32, (chunk, chunk + owners), 0)
    col = lax.broadcasted_iota(jnp.int32, (chunk, chunk + owners), 1)
    earlier = jnp.where((row < col) | (col >= chunk), 1.0, 0.0).astype(jnp.bfloat16)
    start = cap * lax.broadcasted_iota(jnp.int32, (owners, owners), 0).astype(jnp.float32)
    for j in range(0, rows, chunk):
        hit = table == owner_ref[:, j : j + chunk]
        count = jnp.dot(
            jnp.where(hit, 1.0, 0.0).astype(jnp.bfloat16), earlier, preferred_element_type=jnp.float32
        )
        place = count[:, :chunk] + jnp.concatenate([start, start], axis=1)
        slot = jnp.sum(jnp.where(hit, place, 0.0), axis=0, keepdims=True)
        slot_ref[:, j : j + chunk] = slot.astype(jnp.int32)
        start = start + count[:, chunk:]


def rank(owner):
    return pl.pallas_call(
        rank_kernel,
        out_shape=jax.ShapeDtypeStruct((1, rows), jnp.int32),
        compiler_params=params(),
        cost_estimate=pl.CostEstimate(flops=2 * 128 * 4096 * 384, bytes_accessed=100000, transcendentals=0),
    )(owner)


def sort_kernel(slot_ref, field_ref, near_ref, own_ref, side_ref, plus_ref, minus_ref, wide, placed):
    wide[...] = field_ref[...].astype(jnp.float32)

    def body(i, carry):
        first = pl.multiple_of(i * unroll, unroll)
        for j in range(unroll):
            placed[pl.ds(slot_ref[first + j], 1), :] = wide[pl.ds(first + j, 1), :]
        return carry

    lax.fori_loop(0, rows // unroll, body, 0)
    near_ref[...] = placed[:half].astype(jnp.bfloat16)
    for third, far_ref in enumerate((own_ref, side_ref, plus_ref, minus_ref)):
        lo = half + third * block
        far_ref[...] = placed[lo : lo + block].astype(jnp.bfloat16)


def sort_rows(slot, field):
    return pl.pallas_call(
        sort_kernel,
        in_specs=[pl.BlockSpec(memory_space=pltpu.SMEM), in_vmem],
        out_specs=[in_vmem] * 5,
        out_shape=[
            jax.ShapeDtypeStruct((count * block, vals), jnp.bfloat16) for count in (4, 1, 1, 1, 1)
        ],
        scratch_shapes=[pltpu.VMEM((rows, vals), jnp.float32), pltpu.VMEM((slots, vals), jnp.float32)],
        compiler_params=params(),
        cost_estimate=pl.CostEstimate(flops=0, bytes_accessed=20000000, transcendentals=0),
    )(slot, field)


def halo(choice, own_ref, next_ref, label):
    def ends(ref, second):
        top = second * stride + group
        return ref[top : top + 16, :].astype(jnp.float32)

    nothing = jnp.zeros((16, vals), jnp.float32)
    across = jnp.where(choice == 2, ends(next_ref, 0), nothing)
    corner = jnp.where(choice == 1, ends(next_ref, label), across)
    return jnp.where(choice == 0, ends(own_ref, label), corner).astype(jnp.bfloat16)


def ends_kernel(own_ref, before_ref, after_ref, coupling_ref, plane_ref, out_ref):
    plane = plane_ref[...]
    sub, lam = lax.axis_index("sub"), lax.axis_index("lam")
    x, inner = sub % 4, jnp.where(lam % 2 == 0, 0, 2)
    choice = jnp.where(sub == 0, 3, jnp.where(x == 0, 1, inner))
    before = halo(choice, own_ref, before_ref, 2)
    choice = jnp.where(sub == 15, 3, jnp.where(x == 3, 1, inner))
    after = halo(choice, own_ref, after_ref, 1)
    before = jnp.dot(before, plane, preferred_element_type=jnp.float32)[15:16]
    after = jnp.dot(after, plane, preferred_element_type=jnp.float32)[0:1]
    out_ref[0:1, :] = step_size * coupling_ref[0:1, 0:1] * before
    out_ref[1:2, :] = step_size * coupling_ref[31:32, 127:128] * after


def end_terms(own, before, after, coupling, plane):
    return pl.pallas_call(
        ends_kernel,
        in_specs=[in_vmem] * 5,
        out_specs=in_vmem,
        out_shape=jax.ShapeDtypeStruct((8, vals), jnp.float32),
        compiler_params=params(),
        cost_estimate=pl.CostEstimate(flops=1000, bytes_accessed=1000, transcendentals=0),
    )(own, before, after, coupling, plane)


def stencil_kernel(field_ref, coupling_ref, plane_ref, base_ref, projected):
    plane = plane_ref[...]
    projected[0:8, :] = jnp.zeros((8, vals), jnp.float32)
    projected[rows + 8 : rows + 16, :] = jnp.zeros((8, vals), jnp.float32)
    for j in range(rows // 512):
        projected[8 + j * 512 : 8 + (j + 1) * 512, :] = jnp.dot(
            field_ref[j * 512 : (j + 1) * 512, :], plane, preferred_element_type=jnp.float32
        )
    for j in range(rows // vals):
        lo = j * vals
        weight = jnp.broadcast_to(coupling_ref[j : j + 1, :], (vals, vals)).T
        here = projected[lo + 8 : lo + 8 + vals, :]
        before = projected[lo + 7 : lo + 7 + vals, :]
        after = projected[lo + 9 : lo + 9 + vals, :]
        field = field_ref[lo : lo + vals, :].astype(jnp.float32)
        base_ref[lo : lo + vals, :] = field - step_size * (weight * (2.0 * here - before - after))


def stencil(field, coupling, plane):
    return pl.pallas_call(
        stencil_kernel,
        in_specs=[in_vmem] * 3,
        out_specs=in_vmem,
        out_shape=jax.ShapeDtypeStruct((rows, vals), jnp.float32),
        scratch_shapes=[pltpu.VMEM((rows + 16, vals), jnp.float32)],
        compiler_params=params(),
        cost_estimate=pl.CostEstimate(flops=1000, bytes_accessed=1000, transcendentals=0),
    )(field, coupling, plane)


def respond(block, operator):
    response = jnp.dot(block, operator, preferred_element_type=jnp.float32)
    square = response * response
    magnitude = square + pltpu.roll(square, vals // 2, 1)
    reluct = 5.0 - 4.0 / (1.0 + magnitude)
    return reluct * response


def effect_kernel(sources, places, *refs):
    operators, out_ref = refs[: len(sources)], refs[-1]
    for (number, source), place, operator_ref in zip(sources, places, operators):
        rows_ref = refs[len(sources) + number]
        for k in range(16):
            top = k // 4 * stride + k % 4 * vals
            lo, out = source * block + k * cap, place * block + k * cap
            effect = respond(rows_ref[lo : lo + cap, :], operator_ref[top : top + vals, :])
            out_ref[out : out + cap, :] = effect.astype(out_ref.dtype)


def effect_call(operands, sources, places, shape, dtype, aliases):
    return pl.pallas_call(
        functools.partial(effect_kernel, sources, places),
        in_specs=[in_vmem] * len(operands),
        out_specs=in_vmem,
        out_shape=jax.ShapeDtypeStruct((shape, vals), dtype),
        input_output_aliases=aliases,
        compiler_params=params(),
        cost_estimate=pl.CostEstimate(flops=1000, bytes_accessed=1000, transcendentals=0),
    )(*operands)


def replies(operators, guests):
    count = len(guests)
    sources = [(number, 0) for number in range(count)]
    return effect_call([*operators, *guests], sources, range(count), count * block, jnp.bfloat16, {})


def effects(near, operators, thirds, previous):
    operands = [*operators, near]
    aliases = {}
    if previous is not None:
        aliases = {len(operands): 0}
        operands.append(previous)
    sources = [(0, third) for third in thirds]
    return effect_call(operands, sources, thirds, slots, jnp.float32, aliases)


part_tops = (0, 1024, 2048, 3072, 3584, 3840, rows)


def final_kernel(
    slot_ref, base_ref, ends_ref, own_ref, plus_ref, minus_ref, side_ref, _, out_ref, effect_ref, result, sent
):
    for returned_ref, third in ((own_ref, 0), (plus_ref, 2), (minus_ref, 3), (side_ref, 1)):
        lo = half + third * block
        effect_ref[lo : lo + block, :] = returned_ref[...].astype(jnp.float32)

    copies = []
    for number, (top, end) in enumerate(zip(part_tops, part_tops[1:])):

        def body(i, carry):
            first = pl.multiple_of(top + i * long_unroll, long_unroll)
            for j in range(long_unroll):
                effect = effect_ref[pl.ds(slot_ref[first + j], 1), :]
                row = pl.ds(first + j, 1)
                result[row, :] = base_ref[row, :] - step_size * effect
            return carry

        lax.fori_loop(0, (end - top) // long_unroll, body, 0)
        if top == 0:
            result[0:1, :] = result[0:1, :] + ends_ref[0:1, :]
        if end == rows:
            result[rows - 1 : rows, :] = result[rows - 1 : rows, :] + ends_ref[1:2, :]
        span = slice(top, end)
        copies.append(pltpu.make_async_copy(result.at[span], out_ref.at[span], sent.at[number]))
        copies[-1].start()
    for copy in copies:
        copy.wait()


def finish(slot, base, ends, returned, effect):
    operands = [slot, base, ends, *returned, effect]
    return pl.pallas_call(
        final_kernel,
        in_specs=[pl.BlockSpec(memory_space=pltpu.SMEM)] + [in_vmem] * (len(operands) - 1),
        out_specs=[pl.BlockSpec(memory_space=pl.ANY), in_vmem],
        out_shape=[
            jax.ShapeDtypeStruct((rows, vals), jnp.float32),
            jax.ShapeDtypeStruct((slots, vals), jnp.float32),
        ],
        input_output_aliases={len(operands) - 1: 1},
        scratch_shapes=[
            pltpu.VMEM((rows, vals), jnp.float32),
            pltpu.SemaphoreType.DMA((len(part_tops) - 1,)),
        ],
        compiler_params=params(),
        cost_estimate=pl.CostEstimate(flops=4096 * 128, bytes_accessed=10000000, transcendentals=0),
    )(*operands)[0]


def per_device(edge_field, coupling, owner_map, in_plane, profile_op):
    field = edge_field[0]
    tied = lax.optimization_barrier
    tips = jnp.concatenate([field[:8], field[rows - 8 :]], axis=0)
    near = jnp.concatenate([*around(profile_op[0], first_moves), tips], axis=0)
    slot = rank(owner_map.transpose(0, 2, 1)[0]).reshape(rows)
    near, slot = tied((near, slot))
    plane = jnp.concatenate(around(near, second_moves), axis=0)
    near_rows, *far_rows = sort_rows(slot, field)
    plane, near_rows, *far_rows = tied((plane, near_rows, *far_rows))
    plus, minus = shifted(plane, third_moves), shifted(plane, scaled(third_moves, -1))
    side = shifted(plane, side_moves)
    own_guest, side_guest, *pair_guests = [core_swap(part) for part in far_rows]
    weights = coupling.reshape(rows // vals, vals)
    base = stencil(field, weights, in_plane)
    effect = effects(near_rows, [plane], (0,), None)
    reply = replies([plane], [own_guest])
    minus, plus, effect, base, reply = tied((minus, plus, effect, base, reply))
    returned = [core_swap(reply)]
    for part, guest in zip((plus, minus), pair_guests):
        returned.append(core_swap(replies([part], [guest])))
    returned.append(core_swap(replies([side], [side_guest])))
    effect = effects(near_rows, [side, plus, minus], (1, 2, 3), effect)
    ends = end_terms(plane, plus, minus, weights, in_plane)
    return finish(slot, base, ends, returned, effect)[None]


def solution(mesh):
    placed = (
        P("lam", "sub", None),
        P("lam", "sub"),
        P("lam", "sub", None),
        P(),
        P(("sub", "lam"), None, None),
    )
    return jax.shard_map(
        per_device, mesh=mesh, in_specs=placed, out_specs=P("lam", "sub", None), check_vma=False
    )
```

```python
import functools

import jax
import jax.numpy as jnp
from jax import lax
from jax.experimental import pallas as pl
from jax.experimental.pallas import tpu as pltpu
from jax.sharding import PartitionSpec as P

step_size = 0.25
axes_all = ("sub", "lam")
owners = 128
cap = 48
rows = 4096
vals = 128
slots = owners * cap
half = slots // 2
block = 16 * cap
chunk = 256
unroll = 128
long_unroll = 256
group = 4 * vals
stride = group + 16
vmem_bytes = 20 * 1024 * 1024


in_vmem = pl.BlockSpec(memory_space=pltpu.VMEM)


def params():
    return pltpu.CompilerParams(vmem_limit_bytes=vmem_bytes)


def device(y, x, z, c):
    return ((y % 4) * 4 + (x % 4)) * 8 + (z % 4) * 2 + (c % 2)


def shifted(value, moves):
    pairs = []
    for y in range(4):
        for x in range(4):
            for z in range(4):
                for c in range(2):
                    dy, dx, dz = moves[c]
                    pairs.append((device(y, x, z, c), device(y + dy, x + dx, z + dz, c)))
    return lax.ppermute(value, axes_all, pairs)


def scaled(moves, step):
    return [tuple(step * part for part in move) for move in moves]


def core_swap(value):
    pairs = [(d, d ^ 1) for d in range(owners)]
    return lax.ppermute(value, axes_all, pairs)


first_moves = [(2, 0, 1), (0, 2, 1)]
second_moves = [(0, 1, 0), (1, 0, 0)]
third_moves = [(1, 0, 0), (0, 1, 0)]
side_moves = [(0, 0, 1), (0, 0, -1)]


def around(value, moves):
    return [value] + [shifted(value, scaled(moves, step)) for step in (-1, 1, 2)]


def offset(index):
    return jnp.where(index == 1, 1, jnp.where(index == 2, 3, jnp.where(index == 3, 2, 0)))


def slot_owners():
    sub, lam = lax.axis_index("sub"), lax.axis_index("lam")
    y, x, z, c = sub // 4, sub % 4, lam // 2, lam % 2
    index = lax.broadcasted_iota(jnp.int32, (owners, chunk), 0)
    side, third = index >> 6, (index >> 4) & 3
    second, first = (index >> 2) & 3, index & 3
    core = side ^ c
    turn = offset(first)
    along = 2 * turn + jnp.where(third == 2, 3, jnp.where(third == 3, 1, 0))
    up = turn + jnp.where(third == 1, jnp.where(core == 0, 3, 1), 0)
    dx = jnp.where(core == 0, offset(second), along)
    dy = jnp.where(core == 0, along, offset(second))
    return ((((y + dy) & 3) << 2) + ((x + dx) & 3)) * 8 + ((z + up) & 3) * 2 + core


def rank_kernel(owner_ref, slot_ref):
    table = slot_owners()
    row = lax.broadcasted_iota(jnp.int32, (chunk, chunk + owners), 0)
    col = lax.broadcasted_iota(jnp.int32, (chunk, chunk + owners), 1)
    earlier = jnp.where((row < col) | (col >= chunk), 1.0, 0.0).astype(jnp.bfloat16)
    start = cap * lax.broadcasted_iota(jnp.int32, (owners, owners), 0).astype(jnp.float32)
    for j in range(0, rows, chunk):
        hit = table == owner_ref[:, j : j + chunk]
        count = jnp.dot(
            jnp.where(hit, 1.0, 0.0).astype(jnp.bfloat16), earlier, preferred_element_type=jnp.float32
        )
        place = count[:, :chunk] + jnp.concatenate([start, start], axis=1)
        slot = jnp.sum(jnp.where(hit, place, 0.0), axis=0, keepdims=True)
        slot_ref[:, j : j + chunk] = slot.astype(jnp.int32)
        start = start + count[:, chunk:]


def rank(owner):
    return pl.pallas_call(
        rank_kernel,
        out_shape=jax.ShapeDtypeStruct((1, rows), jnp.int32),
        compiler_params=params(),
        cost_estimate=pl.CostEstimate(flops=2 * 128 * 4096 * 384, bytes_accessed=100000, transcendentals=0),
    )(owner)


def sort_kernel(slot_ref, field_ref, near_ref, own_ref, side_ref, plus_ref, minus_ref, wide, placed):
    wide[...] = field_ref[...].astype(jnp.float32)

    def body(i, carry):
        first = pl.multiple_of(i * unroll, unroll)
        for j in range(unroll):
            placed[pl.ds(slot_ref[first + j], 1), :] = wide[pl.ds(first + j, 1), :]
        return carry

    lax.fori_loop(0, rows // unroll, body, 0)
    near_ref[...] = placed[:half].astype(jnp.bfloat16)
    for third, far_ref in enumerate((own_ref, side_ref, plus_ref, minus_ref)):
        lo = half + third * block
        far_ref[...] = placed[lo : lo + block].astype(jnp.bfloat16)


def sort_rows(slot, field):
    return pl.pallas_call(
        sort_kernel,
        in_specs=[pl.BlockSpec(memory_space=pltpu.SMEM), in_vmem],
        out_specs=[in_vmem] * 5,
        out_shape=[
            jax.ShapeDtypeStruct((count * block, vals), jnp.bfloat16) for count in (4, 1, 1, 1, 1)
        ],
        scratch_shapes=[pltpu.VMEM((rows, vals), jnp.float32), pltpu.VMEM((slots, vals), jnp.float32)],
        compiler_params=params(),
        cost_estimate=pl.CostEstimate(flops=0, bytes_accessed=20000000, transcendentals=0),
    )(slot, field)


def halo(choice, own_ref, next_ref, label):
    def ends(ref, second):
        top = second * stride + group
        return ref[top : top + 16, :].astype(jnp.float32)

    nothing = jnp.zeros((16, vals), jnp.float32)
    across = jnp.where(choice == 2, ends(next_ref, 0), nothing)
    corner = jnp.where(choice == 1, ends(next_ref, label), across)
    return jnp.where(choice == 0, ends(own_ref, label), corner).astype(jnp.bfloat16)


def ends_kernel(own_ref, before_ref, after_ref, coupling_ref, plane_ref, out_ref):
    plane = plane_ref[...]
    sub, lam = lax.axis_index("sub"), lax.axis_index("lam")
    x, inner = sub % 4, jnp.where(lam % 2 == 0, 0, 2)
    choice = jnp.where(sub == 0, 3, jnp.where(x == 0, 1, inner))
    before = halo(choice, own_ref, before_ref, 2)
    choice = jnp.where(sub == 15, 3, jnp.where(x == 3, 1, inner))
    after = halo(choice, own_ref, after_ref, 1)
    before = jnp.dot(before, plane, preferred_element_type=jnp.float32)[15:16]
    after = jnp.dot(after, plane, preferred_element_type=jnp.float32)[0:1]
    out_ref[0:1, :] = step_size * coupling_ref[0:1, 0:1] * before
    out_ref[1:2, :] = step_size * coupling_ref[31:32, 127:128] * after


def end_terms(own, before, after, coupling, plane):
    return pl.pallas_call(
        ends_kernel,
        in_specs=[in_vmem] * 5,
        out_specs=in_vmem,
        out_shape=jax.ShapeDtypeStruct((8, vals), jnp.float32),
        compiler_params=params(),
        cost_estimate=pl.CostEstimate(flops=1000, bytes_accessed=1000, transcendentals=0),
    )(own, before, after, coupling, plane)


def stencil_kernel(field_ref, coupling_ref, plane_ref, base_ref, projected):
    plane = plane_ref[...]
    projected[0:8, :] = jnp.zeros((8, vals), jnp.float32)
    projected[rows + 8 : rows + 16, :] = jnp.zeros((8, vals), jnp.float32)
    for j in range(rows // 512):
        projected[8 + j * 512 : 8 + (j + 1) * 512, :] = jnp.dot(
            field_ref[j * 512 : (j + 1) * 512, :], plane, preferred_element_type=jnp.float32
        )
    for j in range(rows // vals):
        lo = j * vals
        weight = jnp.broadcast_to(coupling_ref[j : j + 1, :], (vals, vals)).T
        here = projected[lo + 8 : lo + 8 + vals, :]
        before = projected[lo + 7 : lo + 7 + vals, :]
        after = projected[lo + 9 : lo + 9 + vals, :]
        field = field_ref[lo : lo + vals, :].astype(jnp.float32)
        base_ref[lo : lo + vals, :] = field - step_size * (weight * (2.0 * here - before - after))


def stencil(field, coupling, plane):
    return pl.pallas_call(
        stencil_kernel,
        in_specs=[in_vmem] * 3,
        out_specs=in_vmem,
        out_shape=jax.ShapeDtypeStruct((rows, vals), jnp.float32),
        scratch_shapes=[pltpu.VMEM((rows + 16, vals), jnp.float32)],
        compiler_params=params(),
        cost_estimate=pl.CostEstimate(flops=1000, bytes_accessed=1000, transcendentals=0),
    )(field, coupling, plane)


def respond(block, operator):
    response = jnp.dot(block, operator, preferred_element_type=jnp.float32)
    square = response * response
    magnitude = square + pltpu.roll(square, vals // 2, 1)
    reluct = 5.0 - 4.0 / (1.0 + magnitude)
    return reluct * response


def effect_kernel(sources, places, *refs):
    operators, out_ref = refs[: len(sources)], refs[-1]
    for (number, source), place, operator_ref in zip(sources, places, operators):
        rows_ref = refs[len(sources) + number]
        for k in range(16):
            top = k // 4 * stride + k % 4 * vals
            lo, out = source * block + k * cap, place * block + k * cap
            effect = respond(rows_ref[lo : lo + cap, :], operator_ref[top : top + vals, :])
            out_ref[out : out + cap, :] = effect.astype(out_ref.dtype)


def effect_call(operands, sources, places, shape, dtype, aliases):
    return pl.pallas_call(
        functools.partial(effect_kernel, sources, places),
        in_specs=[in_vmem] * len(operands),
        out_specs=in_vmem,
        out_shape=jax.ShapeDtypeStruct((shape, vals), dtype),
        input_output_aliases=aliases,
        compiler_params=params(),
        cost_estimate=pl.CostEstimate(flops=1000, bytes_accessed=1000, transcendentals=0),
    )(*operands)


def replies(operators, guests):
    count = len(guests)
    sources = [(number, 0) for number in range(count)]
    return effect_call([*operators, *guests], sources, range(count), count * block, jnp.bfloat16, {})


def effects(near, operators, thirds, previous):
    operands = [*operators, near]
    aliases = {}
    if previous is not None:
        aliases = {len(operands): 0}
        operands.append(previous)
    sources = [(0, third) for third in thirds]
    return effect_call(operands, sources, thirds, slots, jnp.float32, aliases)


part_tops = (0, 1024, 2048, 3072, 3584, 3840, rows)


def final_kernel(
    slot_ref, base_ref, ends_ref, own_ref, pair_ref, side_ref, _, out_ref, effect_ref, result, sent
):
    for returned_ref, first, third in ((own_ref, 0, 0), (pair_ref, 0, 2), (pair_ref, 1, 3), (side_ref, 0, 1)):
        lo, top = half + third * block, first * block
        effect_ref[lo : lo + block, :] = returned_ref[top : top + block, :].astype(jnp.float32)

    copies = []
    for number, (top, end) in enumerate(zip(part_tops, part_tops[1:])):

        def body(i, carry):
            first = pl.multiple_of(top + i * long_unroll, long_unroll)
            for j in range(long_unroll):
                effect = effect_ref[pl.ds(slot_ref[first + j], 1), :]
                row = pl.ds(first + j, 1)
                result[row, :] = base_ref[row, :] - step_size * effect
            return carry

        lax.fori_loop(0, (end - top) // long_unroll, body, 0)
        if top == 0:
            result[0:1, :] = result[0:1, :] + ends_ref[0:1, :]
        if end == rows:
            result[rows - 1 : rows, :] = result[rows - 1 : rows, :] + ends_ref[1:2, :]
        span = slice(top, end)
        copies.append(pltpu.make_async_copy(result.at[span], out_ref.at[span], sent.at[number]))
        copies[-1].start()
    for copy in copies:
        copy.wait()


def finish(slot, base, ends, returned, effect):
    operands = [slot, base, ends, *returned, effect]
    return pl.pallas_call(
        final_kernel,
        in_specs=[pl.BlockSpec(memory_space=pltpu.SMEM)] + [in_vmem] * (len(operands) - 1),
        out_specs=[pl.BlockSpec(memory_space=pl.ANY), in_vmem],
        out_shape=[
            jax.ShapeDtypeStruct((rows, vals), jnp.float32),
            jax.ShapeDtypeStruct((slots, vals), jnp.float32),
        ],
        input_output_aliases={len(operands) - 1: 1},
        scratch_shapes=[
            pltpu.VMEM((rows, vals), jnp.float32),
            pltpu.SemaphoreType.DMA((len(part_tops) - 1,)),
        ],
        compiler_params=params(),
        cost_estimate=pl.CostEstimate(flops=4096 * 128, bytes_accessed=10000000, transcendentals=0),
    )(*operands)[0]


def per_device(edge_field, coupling, owner_map, in_plane, profile_op):
    field = edge_field[0]
    tied = lax.optimization_barrier
    tips = jnp.concatenate([field[:8], field[rows - 8 :]], axis=0)
    near = jnp.concatenate([*around(profile_op[0], first_moves), tips], axis=0)
    slot = rank(owner_map.transpose(0, 2, 1)[0]).reshape(rows)
    near, slot = tied((near, slot))
    plane = jnp.concatenate(around(near, second_moves), axis=0)
    near_rows, *far_rows = sort_rows(slot, field)
    plane, near_rows, *far_rows = tied((plane, near_rows, *far_rows))
    plus, minus = shifted(plane, third_moves), shifted(plane, scaled(third_moves, -1))
    side = shifted(plane, side_moves)
    own_guest, side_guest, *pair_guests = [core_swap(part) for part in far_rows]
    weights = coupling.reshape(rows // vals, vals)
    base = stencil(field, weights, in_plane)
    effect = effects(near_rows, [plane], (0,), None)
    minus, plus, effect, base = tied((minus, plus, effect, base))
    returned = [core_swap(replies([plane], [own_guest]))]
    returned.append(core_swap(replies([plus, minus], pair_guests)))
    returned.append(core_swap(replies([side], [side_guest])))
    effect = effects(near_rows, [side, plus, minus], (1, 2, 3), effect)
    ends = end_terms(plane, plus, minus, weights, in_plane)
    return finish(slot, base, ends, returned, effect)[None]


def solution(mesh):
    placed = (
        P("lam", "sub", None),
        P("lam", "sub"),
        P("lam", "sub", None),
        P(),
        P(("sub", "lam"), None, None),
    )
    return jax.shard_map(
        per_device, mesh=mesh, in_specs=placed, out_specs=P("lam", "sub", None), check_vma=False
    )
```

```python
import functools

import jax
import jax.numpy as jnp
from jax import lax
from jax.experimental import pallas as pl
from jax.experimental.pallas import tpu as pltpu
from jax.sharding import PartitionSpec as P

step_size = 0.25
axes_all = ("sub", "lam")
owners = 128
cap = 48
rows = 4096
vals = 128
slots = owners * cap
half = slots // 2
block = 16 * cap
chunk = 256
unroll = 128
long_unroll = 256
group = 4 * vals
stride = group + 16
vmem_bytes = 20 * 1024 * 1024


in_vmem = pl.BlockSpec(memory_space=pltpu.VMEM)


def params():
    return pltpu.CompilerParams(vmem_limit_bytes=vmem_bytes)


def device(y, x, z, c):
    return ((y % 4) * 4 + (x % 4)) * 8 + (z % 4) * 2 + (c % 2)


def shifted(value, moves):
    pairs = []
    for y in range(4):
        for x in range(4):
            for z in range(4):
                for c in range(2):
                    dy, dx, dz = moves[c]
                    pairs.append((device(y, x, z, c), device(y + dy, x + dx, z + dz, c)))
    return lax.ppermute(value, axes_all, pairs)


def scaled(moves, step):
    return [tuple(step * part for part in move) for move in moves]


def core_swap(value):
    pairs = [(d, d ^ 1) for d in range(owners)]
    return lax.ppermute(value, axes_all, pairs)


first_moves = [(2, 0, 1), (0, 2, 1)]
second_moves = [(0, 1, 0), (1, 0, 0)]
third_moves = [(1, 0, 0), (0, 1, 0)]
side_moves = [(0, 0, 1), (0, 0, -1)]


def around(value, moves):
    return [value] + [shifted(value, scaled(moves, step)) for step in (-1, 1, 2)]


def offset(index):
    return jnp.where(index == 1, 1, jnp.where(index == 2, 3, jnp.where(index == 3, 2, 0)))


def slot_owners():
    sub, lam = lax.axis_index("sub"), lax.axis_index("lam")
    y, x, z, c = sub // 4, sub % 4, lam // 2, lam % 2
    index = lax.broadcasted_iota(jnp.int32, (owners, chunk), 0)
    side, third = index >> 6, (index >> 4) & 3
    second, first = (index >> 2) & 3, index & 3
    core = side ^ c
    turn = offset(first)
    along = 2 * turn + jnp.where(third == 2, 3, jnp.where(third == 3, 1, 0))
    up = turn + jnp.where(third == 1, jnp.where(core == 0, 3, 1), 0)
    dx = jnp.where(core == 0, offset(second), along)
    dy = jnp.where(core == 0, along, offset(second))
    return ((((y + dy) & 3) << 2) + ((x + dx) & 3)) * 8 + ((z + up) & 3) * 2 + core


def rank_kernel(owner_ref, slot_ref):
    table = slot_owners()
    row = lax.broadcasted_iota(jnp.int32, (chunk, chunk + owners), 0)
    col = lax.broadcasted_iota(jnp.int32, (chunk, chunk + owners), 1)
    earlier = jnp.where((row < col) | (col >= chunk), 1.0, 0.0).astype(jnp.bfloat16)
    start = cap * lax.broadcasted_iota(jnp.int32, (owners, owners), 0).astype(jnp.float32)
    for j in range(0, rows, chunk):
        hit = table == owner_ref[:, j : j + chunk]
        count = jnp.dot(
            jnp.where(hit, 1.0, 0.0).astype(jnp.bfloat16), earlier, preferred_element_type=jnp.float32
        )
        place = count[:, :chunk] + jnp.concatenate([start, start], axis=1)
        slot = jnp.sum(jnp.where(hit, place, 0.0), axis=0, keepdims=True)
        slot_ref[:, j : j + chunk] = slot.astype(jnp.int32)
        start = start + count[:, chunk:]


def rank(owner):
    return pl.pallas_call(
        rank_kernel,
        out_shape=jax.ShapeDtypeStruct((1, rows), jnp.int32),
        compiler_params=params(),
        cost_estimate=pl.CostEstimate(flops=2 * 128 * 4096 * 384, bytes_accessed=100000, transcendentals=0),
    )(owner)


def sort_kernel(slot_ref, field_ref, near_ref, own_ref, side_ref, plus_ref, minus_ref, wide, placed):
    wide[...] = field_ref[...].astype(jnp.float32)

    def body(i, carry):
        first = pl.multiple_of(i * unroll, unroll)
        for j in range(unroll):
            placed[pl.ds(slot_ref[first + j], 1), :] = wide[pl.ds(first + j, 1), :]
        return carry

    lax.fori_loop(0, rows // unroll, body, 0)
    near_ref[...] = placed[:half].astype(jnp.bfloat16)
    for third, far_ref in enumerate((own_ref, side_ref, plus_ref, minus_ref)):
        lo = half + third * block
        far_ref[...] = placed[lo : lo + block].astype(jnp.bfloat16)


def sort_rows(slot, field):
    return pl.pallas_call(
        sort_kernel,
        in_specs=[pl.BlockSpec(memory_space=pltpu.SMEM), in_vmem],
        out_specs=[in_vmem] * 5,
        out_shape=[
            jax.ShapeDtypeStruct((count * block, vals), jnp.bfloat16) for count in (4, 1, 1, 1, 1)
        ],
        scratch_shapes=[pltpu.VMEM((rows, vals), jnp.float32), pltpu.VMEM((slots, vals), jnp.float32)],
        compiler_params=params(),
        cost_estimate=pl.CostEstimate(flops=0, bytes_accessed=20000000, transcendentals=0),
    )(slot, field)


def halo(choice, own_ref, next_ref, label):
    def ends(ref, second):
        top = second * stride + group
        return ref[top : top + 16, :].astype(jnp.float32)

    nothing = jnp.zeros((16, vals), jnp.float32)
    across = jnp.where(choice == 2, ends(next_ref, 0), nothing)
    corner = jnp.where(choice == 1, ends(next_ref, label), across)
    return jnp.where(choice == 0, ends(own_ref, label), corner).astype(jnp.bfloat16)


def ends_kernel(own_ref, before_ref, after_ref, coupling_ref, plane_ref, out_ref):
    plane = plane_ref[...]
    sub, lam = lax.axis_index("sub"), lax.axis_index("lam")
    x, inner = sub % 4, jnp.where(lam % 2 == 0, 0, 2)
    choice = jnp.where(sub == 0, 3, jnp.where(x == 0, 1, inner))
    before = halo(choice, own_ref, before_ref, 2)
    choice = jnp.where(sub == 15, 3, jnp.where(x == 3, 1, inner))
    after = halo(choice, own_ref, after_ref, 1)
    before = jnp.dot(before, plane, preferred_element_type=jnp.float32)[15:16]
    after = jnp.dot(after, plane, preferred_element_type=jnp.float32)[0:1]
    out_ref[0:1, :] = step_size * coupling_ref[0:1, 0:1] * before
    out_ref[1:2, :] = step_size * coupling_ref[31:32, 127:128] * after


def end_terms(own, before, after, coupling, plane):
    return pl.pallas_call(
        ends_kernel,
        in_specs=[in_vmem] * 5,
        out_specs=in_vmem,
        out_shape=jax.ShapeDtypeStruct((8, vals), jnp.float32),
        compiler_params=params(),
        cost_estimate=pl.CostEstimate(flops=1000, bytes_accessed=1000, transcendentals=0),
    )(own, before, after, coupling, plane)


def stencil_kernel(field_ref, coupling_ref, plane_ref, base_ref, projected):
    plane = plane_ref[...]
    projected[0:8, :] = jnp.zeros((8, vals), jnp.float32)
    projected[rows + 8 : rows + 16, :] = jnp.zeros((8, vals), jnp.float32)
    for j in range(rows // 512):
        projected[8 + j * 512 : 8 + (j + 1) * 512, :] = jnp.dot(
            field_ref[j * 512 : (j + 1) * 512, :], plane, preferred_element_type=jnp.float32
        )
    for j in range(rows // vals):
        lo = j * vals
        weight = jnp.broadcast_to(coupling_ref[j : j + 1, :], (vals, vals)).T
        here = projected[lo + 8 : lo + 8 + vals, :]
        before = projected[lo + 7 : lo + 7 + vals, :]
        after = projected[lo + 9 : lo + 9 + vals, :]
        field = field_ref[lo : lo + vals, :].astype(jnp.float32)
        base_ref[lo : lo + vals, :] = field - step_size * (weight * (2.0 * here - before - after))


def stencil(field, coupling, plane):
    return pl.pallas_call(
        stencil_kernel,
        in_specs=[in_vmem] * 3,
        out_specs=in_vmem,
        out_shape=jax.ShapeDtypeStruct((rows, vals), jnp.float32),
        scratch_shapes=[pltpu.VMEM((rows + 16, vals), jnp.float32)],
        compiler_params=params(),
        cost_estimate=pl.CostEstimate(flops=1000, bytes_accessed=1000, transcendentals=0),
    )(field, coupling, plane)


def respond(block, operator):
    response = jnp.dot(block, operator, preferred_element_type=jnp.float32)
    square = response * response
    magnitude = square + pltpu.roll(square, vals // 2, 1)
    reluct = 5.0 - 4.0 / (1.0 + magnitude)
    return reluct * response


def effect_kernel(sources, places, *refs):
    operators, out_ref = refs[: len(sources)], refs[-1]
    for (number, source), place, operator_ref in zip(sources, places, operators):
        rows_ref = refs[len(sources) + number]
        for k in range(16):
            top = k // 4 * stride + k % 4 * vals
            lo, out = source * block + k * cap, place * block + k * cap
            effect = respond(rows_ref[lo : lo + cap, :], operator_ref[top : top + vals, :])
            out_ref[out : out + cap, :] = effect.astype(out_ref.dtype)


def effect_call(operands, sources, places, shape, dtype, aliases):
    return pl.pallas_call(
        functools.partial(effect_kernel, sources, places),
        in_specs=[in_vmem] * len(operands),
        out_specs=in_vmem,
        out_shape=jax.ShapeDtypeStruct((shape, vals), dtype),
        input_output_aliases=aliases,
        compiler_params=params(),
        cost_estimate=pl.CostEstimate(flops=1000, bytes_accessed=1000, transcendentals=0),
    )(*operands)


def replies(operators, guests):
    count = len(guests)
    sources = [(number, 0) for number in range(count)]
    return effect_call([*operators, *guests], sources, range(count), count * block, jnp.bfloat16, {})


def effects(near, operators, thirds, previous):
    operands = [*operators, near]
    aliases = {}
    if previous is not None:
        aliases = {len(operands): 0}
        operands.append(previous)
    sources = [(0, third) for third in thirds]
    return effect_call(operands, sources, thirds, slots, jnp.float32, aliases)


part_tops = (0, 1024, 2048, 3072, 3584, 3840, rows)


def final_kernel(
    slot_ref, base_ref, ends_ref, own_ref, trio_ref, _, out_ref, effect_ref, result, sent
):
    effect_ref[half : half + block, :] = own_ref[...].astype(jnp.float32)
    effect_ref[half + block :, :] = trio_ref[...].astype(jnp.float32)

    copies = []
    for number, (top, end) in enumerate(zip(part_tops, part_tops[1:])):

        def body(i, carry):
            first = pl.multiple_of(top + i * long_unroll, long_unroll)
            for j in range(long_unroll):
                effect = effect_ref[pl.ds(slot_ref[first + j], 1), :]
                row = pl.ds(first + j, 1)
                result[row, :] = base_ref[row, :] - step_size * effect
            return carry

        lax.fori_loop(0, (end - top) // long_unroll, body, 0)
        if top == 0:
            result[0:1, :] = result[0:1, :] + ends_ref[0:1, :]
        if end == rows:
            result[rows - 1 : rows, :] = result[rows - 1 : rows, :] + ends_ref[1:2, :]
        span = slice(top, end)
        copies.append(pltpu.make_async_copy(result.at[span], out_ref.at[span], sent.at[number]))
        copies[-1].start()
    for copy in copies:
        copy.wait()


def finish(slot, base, ends, returned, effect):
    operands = [slot, base, ends, *returned, effect]
    return pl.pallas_call(
        final_kernel,
        in_specs=[pl.BlockSpec(memory_space=pltpu.SMEM)] + [in_vmem] * (len(operands) - 1),
        out_specs=[pl.BlockSpec(memory_space=pl.ANY), in_vmem],
        out_shape=[
            jax.ShapeDtypeStruct((rows, vals), jnp.float32),
            jax.ShapeDtypeStruct((slots, vals), jnp.float32),
        ],
        input_output_aliases={len(operands) - 1: 1},
        scratch_shapes=[
            pltpu.VMEM((rows, vals), jnp.float32),
            pltpu.SemaphoreType.DMA((len(part_tops) - 1,)),
        ],
        compiler_params=params(),
        cost_estimate=pl.CostEstimate(flops=4096 * 128, bytes_accessed=10000000, transcendentals=0),
    )(*operands)[0]


def per_device(edge_field, coupling, owner_map, in_plane, profile_op):
    field = edge_field[0]
    tied = lax.optimization_barrier
    tips = jnp.concatenate([field[:8], field[rows - 8 :]], axis=0)
    near = jnp.concatenate([*around(profile_op[0], first_moves), tips], axis=0)
    slot = rank(owner_map.transpose(0, 2, 1)[0]).reshape(rows)
    near, slot = tied((near, slot))
    plane = jnp.concatenate(around(near, second_moves), axis=0)
    near_rows, *far_rows = sort_rows(slot, field)
    plane, near_rows, *far_rows = tied((plane, near_rows, *far_rows))
    plus, minus = shifted(plane, third_moves), shifted(plane, scaled(third_moves, -1))
    side = shifted(plane, side_moves)
    own_guest, side_guest, *pair_guests = [core_swap(part) for part in far_rows]
    weights = coupling.reshape(rows // vals, vals)
    base = stencil(field, weights, in_plane)
    effect = effects(near_rows, [plane], (0,), None)
    reply = replies([plane], [own_guest])
    effect, base, reply, guests = tied((effect, base, reply, [side_guest, *pair_guests]))
    side_guest, *pair_guests = guests
    minus, plus, side, effect, base, reply = tied((minus, plus, side, effect, base, reply))
    returned = [core_swap(reply)]
    returned.append(core_swap(replies([side, plus, minus], [side_guest, *pair_guests])))
    effect = effects(near_rows, [side, plus, minus], (1, 2, 3), effect)
    ends = end_terms(plane, plus, minus, weights, in_plane)
    return finish(slot, base, ends, returned, effect)[None]


def solution(mesh):
    placed = (
        P("lam", "sub", None),
        P("lam", "sub"),
        P("lam", "sub", None),
        P(),
        P(("sub", "lam"), None, None),
    )
    return jax.shard_map(
        per_device, mesh=mesh, in_specs=placed, out_specs=P("lam", "sub", None), check_vma=False
    )
```

```python
import functools

import jax
import jax.numpy as jnp
from jax import lax
from jax.experimental import pallas as pl
from jax.experimental.pallas import tpu as pltpu
from jax.sharding import PartitionSpec as P

step_size = 0.25
axes_all = ("sub", "lam")
owners = 128
cap = 48
rows = 4096
vals = 128
slots = owners * cap
half = slots // 2
block = 16 * cap
chunk = 256
unroll = 128
long_unroll = 256
group = 4 * vals
stride = group + 16
vmem_bytes = 20 * 1024 * 1024


in_vmem = pl.BlockSpec(memory_space=pltpu.VMEM)


def params():
    return pltpu.CompilerParams(vmem_limit_bytes=vmem_bytes)


def device(y, x, z, c):
    return ((y % 4) * 4 + (x % 4)) * 8 + (z % 4) * 2 + (c % 2)


def shifted(value, moves):
    pairs = []
    for y in range(4):
        for x in range(4):
            for z in range(4):
                for c in range(2):
                    dy, dx, dz = moves[c]
                    pairs.append((device(y, x, z, c), device(y + dy, x + dx, z + dz, c)))
    return lax.ppermute(value, axes_all, pairs)


def scaled(moves, step):
    return [tuple(step * part for part in move) for move in moves]


def core_swap(value):
    pairs = [(d, d ^ 1) for d in range(owners)]
    return lax.ppermute(value, axes_all, pairs)


first_moves = [(2, 0, 1), (0, 2, 1)]
second_moves = [(0, 1, 0), (1, 0, 0)]
third_moves = [(1, 0, 0), (0, 1, 0)]
side_moves = [(0, 0, 1), (0, 0, -1)]


def around(value, moves):
    return [value] + [shifted(value, scaled(moves, step)) for step in (-1, 1, 2)]


def offset(index):
    return jnp.where(index == 1, 1, jnp.where(index == 2, 3, jnp.where(index == 3, 2, 0)))


def slot_owners():
    sub, lam = lax.axis_index("sub"), lax.axis_index("lam")
    y, x, z, c = sub // 4, sub % 4, lam // 2, lam % 2
    index = lax.broadcasted_iota(jnp.int32, (owners, chunk), 0)
    side, third = index >> 6, (index >> 4) & 3
    second, first = (index >> 2) & 3, index & 3
    core = side ^ c
    turn = offset(first)
    along = 2 * turn + jnp.where(third == 2, 3, jnp.where(third == 3, 1, 0))
    up = turn + jnp.where(third == 1, jnp.where(core == 0, 3, 1), 0)
    dx = jnp.where(core == 0, offset(second), along)
    dy = jnp.where(core == 0, along, offset(second))
    return ((((y + dy) & 3) << 2) + ((x + dx) & 3)) * 8 + ((z + up) & 3) * 2 + core


def rank_kernel(owner_ref, slot_ref):
    table = slot_owners()
    row = lax.broadcasted_iota(jnp.int32, (chunk, chunk + owners), 0)
    col = lax.broadcasted_iota(jnp.int32, (chunk, chunk + owners), 1)
    earlier = jnp.where((row < col) | (col >= chunk), 1.0, 0.0).astype(jnp.bfloat16)
    start = cap * lax.broadcasted_iota(jnp.int32, (owners, owners), 0).astype(jnp.float32)
    for j in range(0, rows, chunk):
        hit = table == owner_ref[:, j : j + chunk]
        count = jnp.dot(
            jnp.where(hit, 1.0, 0.0).astype(jnp.bfloat16), earlier, preferred_element_type=jnp.float32
        )
        place = count[:, :chunk] + jnp.concatenate([start, start], axis=1)
        slot = jnp.sum(jnp.where(hit, place, 0.0), axis=0, keepdims=True)
        slot_ref[:, j : j + chunk] = slot.astype(jnp.int32)
        start = start + count[:, chunk:]


def rank(owner):
    return pl.pallas_call(
        rank_kernel,
        out_shape=jax.ShapeDtypeStruct((1, rows), jnp.int32),
        compiler_params=params(),
        cost_estimate=pl.CostEstimate(flops=2 * 128 * 4096 * 384, bytes_accessed=100000, transcendentals=0),
    )(owner)


def sort_kernel(slot_ref, field_ref, near_ref, own_ref, side_ref, plus_ref, minus_ref, wide, placed):
    wide[...] = field_ref[...].astype(jnp.float32)

    def body(i, carry):
        first = pl.multiple_of(i * unroll, unroll)
        for j in range(unroll):
            placed[pl.ds(slot_ref[first + j], 1), :] = wide[pl.ds(first + j, 1), :]
        return carry

    lax.fori_loop(0, rows // unroll, body, 0)
    near_ref[...] = placed[:half].astype(jnp.bfloat16)
    for third, far_ref in enumerate((own_ref, side_ref, plus_ref, minus_ref)):
        lo = half + third * block
        far_ref[...] = placed[lo : lo + block].astype(jnp.bfloat16)


def sort_rows(slot, field):
    return pl.pallas_call(
        sort_kernel,
        in_specs=[pl.BlockSpec(memory_space=pltpu.SMEM), in_vmem],
        out_specs=[in_vmem] * 5,
        out_shape=[
            jax.ShapeDtypeStruct((count * block, vals), jnp.bfloat16) for count in (4, 1, 1, 1, 1)
        ],
        scratch_shapes=[pltpu.VMEM((rows, vals), jnp.float32), pltpu.VMEM((slots, vals), jnp.float32)],
        compiler_params=params(),
        cost_estimate=pl.CostEstimate(flops=0, bytes_accessed=20000000, transcendentals=0),
    )(slot, field)


def halo(choice, own_ref, next_ref, label):
    def ends(ref, second):
        top = second * stride + group
        return ref[top : top + 16, :].astype(jnp.float32)

    nothing = jnp.zeros((16, vals), jnp.float32)
    across = jnp.where(choice == 2, ends(next_ref, 0), nothing)
    corner = jnp.where(choice == 1, ends(next_ref, label), across)
    return jnp.where(choice == 0, ends(own_ref, label), corner).astype(jnp.bfloat16)


def ends_kernel(own_ref, before_ref, after_ref, coupling_ref, plane_ref, out_ref):
    plane = plane_ref[...]
    sub, lam = lax.axis_index("sub"), lax.axis_index("lam")
    x, inner = sub % 4, jnp.where(lam % 2 == 0, 0, 2)
    choice = jnp.where(sub == 0, 3, jnp.where(x == 0, 1, inner))
    before = halo(choice, own_ref, before_ref, 2)
    choice = jnp.where(sub == 15, 3, jnp.where(x == 3, 1, inner))
    after = halo(choice, own_ref, after_ref, 1)
    before = jnp.dot(before, plane, preferred_element_type=jnp.float32)[15:16]
    after = jnp.dot(after, plane, preferred_element_type=jnp.float32)[0:1]
    out_ref[0:1, :] = step_size * coupling_ref[0:1, 0:1] * before
    out_ref[1:2, :] = step_size * coupling_ref[31:32, 127:128] * after


def end_terms(own, before, after, coupling, plane):
    return pl.pallas_call(
        ends_kernel,
        in_specs=[in_vmem] * 5,
        out_specs=in_vmem,
        out_shape=jax.ShapeDtypeStruct((8, vals), jnp.float32),
        compiler_params=params(),
        cost_estimate=pl.CostEstimate(flops=1000, bytes_accessed=1000, transcendentals=0),
    )(own, before, after, coupling, plane)


def stencil_kernel(field_ref, coupling_ref, plane_ref, base_ref, projected):
    plane = plane_ref[...]
    projected[0:8, :] = jnp.zeros((8, vals), jnp.float32)
    projected[rows + 8 : rows + 16, :] = jnp.zeros((8, vals), jnp.float32)
    for j in range(rows // 512):
        projected[8 + j * 512 : 8 + (j + 1) * 512, :] = jnp.dot(
            field_ref[j * 512 : (j + 1) * 512, :], plane, preferred_element_type=jnp.float32
        )
    for j in range(rows // vals):
        lo = j * vals
        weight = jnp.broadcast_to(coupling_ref[j : j + 1, :], (vals, vals)).T
        here = projected[lo + 8 : lo + 8 + vals, :]
        before = projected[lo + 7 : lo + 7 + vals, :]
        after = projected[lo + 9 : lo + 9 + vals, :]
        field = field_ref[lo : lo + vals, :].astype(jnp.float32)
        base_ref[lo : lo + vals, :] = field - step_size * (weight * (2.0 * here - before - after))


def stencil(field, coupling, plane):
    return pl.pallas_call(
        stencil_kernel,
        in_specs=[in_vmem] * 3,
        out_specs=in_vmem,
        out_shape=jax.ShapeDtypeStruct((rows, vals), jnp.float32),
        scratch_shapes=[pltpu.VMEM((rows + 16, vals), jnp.float32)],
        compiler_params=params(),
        cost_estimate=pl.CostEstimate(flops=1000, bytes_accessed=1000, transcendentals=0),
    )(field, coupling, plane)


def respond(block, operator):
    response = jnp.dot(block, operator, preferred_element_type=jnp.float32)
    square = response * response
    magnitude = square + pltpu.roll(square, vals // 2, 1)
    reluct = 5.0 - 4.0 / (1.0 + magnitude)
    return reluct * response


def effect_kernel(sources, places, *refs):
    operators, out_ref = refs[: len(sources)], refs[-1]
    for (number, source), place, operator_ref in zip(sources, places, operators):
        rows_ref = refs[len(sources) + number]
        for k in range(16):
            top = k // 4 * stride + k % 4 * vals
            lo, out = source * block + k * cap, place * block + k * cap
            effect = respond(rows_ref[lo : lo + cap, :], operator_ref[top : top + vals, :])
            out_ref[out : out + cap, :] = effect.astype(out_ref.dtype)


def effect_call(operands, sources, places, shape, dtype, aliases):
    return pl.pallas_call(
        functools.partial(effect_kernel, sources, places),
        in_specs=[in_vmem] * len(operands),
        out_specs=in_vmem,
        out_shape=jax.ShapeDtypeStruct((shape, vals), dtype),
        input_output_aliases=aliases,
        compiler_params=params(),
        cost_estimate=pl.CostEstimate(flops=1000, bytes_accessed=1000, transcendentals=0),
    )(*operands)


def replies(operators, guests):
    count = len(guests)
    sources = [(number, 0) for number in range(count)]
    return effect_call([*operators, *guests], sources, range(count), count * block, jnp.bfloat16, {})


def own_reply_kernel(operator_ref, guest_ref, *out_refs):
    for k in range(16):
        top = k // 4 * stride + k % 4 * vals
        lo, out = k * cap, k % 8 * cap
        effect = respond(guest_ref[lo : lo + cap, :], operator_ref[top : top + vals, :])
        out_refs[k // 8][out : out + cap, :] = effect.astype(jnp.bfloat16)


def own_replies(operator, guest):
    return pl.pallas_call(
        own_reply_kernel,
        in_specs=[in_vmem] * 2,
        out_specs=[in_vmem] * 2,
        out_shape=[jax.ShapeDtypeStruct((block // 2, vals), jnp.bfloat16)] * 2,
        compiler_params=params(),
        cost_estimate=pl.CostEstimate(flops=1000, bytes_accessed=1000, transcendentals=0),
    )(operator, guest)


def effects(near, operators, thirds, previous):
    operands = [*operators, near]
    aliases = {}
    if previous is not None:
        aliases = {len(operands): 0}
        operands.append(previous)
    sources = [(0, third) for third in thirds]
    return effect_call(operands, sources, thirds, slots, jnp.float32, aliases)


part_tops = (0, 1024, 2048, 3072, 3584, 3840, rows)


def final_kernel(
    slot_ref, base_ref, ends_ref, own_ref, rest_ref, trio_ref, _, out_ref, effect_ref, result, sent
):
    effect_ref[half : half + block // 2, :] = own_ref[...].astype(jnp.float32)
    effect_ref[half + block // 2 : half + block, :] = rest_ref[...].astype(jnp.float32)
    effect_ref[half + block :, :] = trio_ref[...].astype(jnp.float32)

    copies = []
    for number, (top, end) in enumerate(zip(part_tops, part_tops[1:])):

        def body(i, carry):
            first = pl.multiple_of(top + i * long_unroll, long_unroll)
            for j in range(long_unroll):
                effect = effect_ref[pl.ds(slot_ref[first + j], 1), :]
                row = pl.ds(first + j, 1)
                result[row, :] = base_ref[row, :] - step_size * effect
            return carry

        lax.fori_loop(0, (end - top) // long_unroll, body, 0)
        if top == 0:
            result[0:1, :] = result[0:1, :] + ends_ref[0:1, :]
        if end == rows:
            result[rows - 1 : rows, :] = result[rows - 1 : rows, :] + ends_ref[1:2, :]
        span = slice(top, end)
        copies.append(pltpu.make_async_copy(result.at[span], out_ref.at[span], sent.at[number]))
        copies[-1].start()
    for copy in copies:
        copy.wait()


def finish(slot, base, ends, returned, effect):
    operands = [slot, base, ends, *returned, effect]
    return pl.pallas_call(
        final_kernel,
        in_specs=[pl.BlockSpec(memory_space=pltpu.SMEM)] + [in_vmem] * (len(operands) - 1),
        out_specs=[pl.BlockSpec(memory_space=pl.ANY), in_vmem],
        out_shape=[
            jax.ShapeDtypeStruct((rows, vals), jnp.float32),
            jax.ShapeDtypeStruct((slots, vals), jnp.float32),
        ],
        input_output_aliases={len(operands) - 1: 1},
        scratch_shapes=[
            pltpu.VMEM((rows, vals), jnp.float32),
            pltpu.SemaphoreType.DMA((len(part_tops) - 1,)),
        ],
        compiler_params=params(),
        cost_estimate=pl.CostEstimate(flops=4096 * 128, bytes_accessed=10000000, transcendentals=0),
    )(*operands)[0]


def per_device(edge_field, coupling, owner_map, in_plane, profile_op):
    field = edge_field[0]
    tied = lax.optimization_barrier
    tips = jnp.concatenate([field[:8], field[rows - 8 :]], axis=0)
    near = jnp.concatenate([*around(profile_op[0], first_moves), tips], axis=0)
    slot = rank(owner_map.transpose(0, 2, 1)[0]).reshape(rows)
    near, slot = tied((near, slot))
    plane = jnp.concatenate(around(near, second_moves), axis=0)
    near_rows, *far_rows = sort_rows(slot, field)
    plane, near_rows, *far_rows = tied((plane, near_rows, *far_rows))
    plus, minus = shifted(plane, third_moves), shifted(plane, scaled(third_moves, -1))
    side = shifted(plane, side_moves)
    own_guest, side_guest, *pair_guests = [core_swap(part) for part in far_rows]
    weights = coupling.reshape(rows // vals, vals)
    base = stencil(field, weights, in_plane)
    effect = effects(near_rows, [plane], (0,), None)
    reply = [core_swap(part) for part in own_replies(plane, own_guest)]
    effect, base, reply, guests = tied((effect, base, reply, [side_guest, *pair_guests]))
    side_guest, *pair_guests = guests
    minus, plus, side, effect, base, reply = tied((minus, plus, side, effect, base, reply))
    returned = [*reply]
    returned.append(core_swap(replies([side, plus, minus], [side_guest, *pair_guests])))
    effect = effects(near_rows, [side, plus, minus], (1, 2, 3), effect)
    ends = end_terms(plane, plus, minus, weights, in_plane)
    return finish(slot, base, ends, returned, effect)[None]


def solution(mesh):
    placed = (
        P("lam", "sub", None),
        P("lam", "sub"),
        P("lam", "sub", None),
        P(),
        P(("sub", "lam"), None, None),
    )
    return jax.shard_map(
        per_device, mesh=mesh, in_specs=placed, out_specs=P("lam", "sub", None), check_vma=False
    )
```

```python
import functools

import jax
import jax.numpy as jnp
from jax import lax
from jax.experimental import pallas as pl
from jax.experimental.pallas import tpu as pltpu
from jax.sharding import PartitionSpec as P

step_size = 0.25
axes_all = ("sub", "lam")
owners = 128
cap = 48
rows = 4096
vals = 128
slots = owners * cap
half = slots // 2
block = 16 * cap
chunk = 256
unroll = 128
long_unroll = 256
group = 4 * vals
stride = group + 16
vmem_bytes = 20 * 1024 * 1024


in_vmem = pl.BlockSpec(memory_space=pltpu.VMEM)


def params():
    return pltpu.CompilerParams(vmem_limit_bytes=vmem_bytes)


def device(y, x, z, c):
    return ((y % 4) * 4 + (x % 4)) * 8 + (z % 4) * 2 + (c % 2)


def shifted(value, moves):
    pairs = []
    for y in range(4):
        for x in range(4):
            for z in range(4):
                for c in range(2):
                    dy, dx, dz = moves[c]
                    pairs.append((device(y, x, z, c), device(y + dy, x + dx, z + dz, c)))
    return lax.ppermute(value, axes_all, pairs)


def scaled(moves, step):
    return [tuple(step * part for part in move) for move in moves]


def core_swap(value):
    pairs = [(d, d ^ 1) for d in range(owners)]
    return lax.ppermute(value, axes_all, pairs)


first_moves = [(2, 0, 1), (0, 2, 1)]
second_moves = [(0, 1, 0), (1, 0, 0)]
third_moves = [(1, 0, 0), (0, 1, 0)]
side_moves = [(0, 0, 1), (0, 0, -1)]


def around(value, moves):
    return [value] + [shifted(value, scaled(moves, step)) for step in (-1, 1, 2)]


def offset(index):
    return jnp.where(index == 1, 1, jnp.where(index == 2, 3, jnp.where(index == 3, 2, 0)))


def slot_owners():
    sub, lam = lax.axis_index("sub"), lax.axis_index("lam")
    y, x, z, c = sub // 4, sub % 4, lam // 2, lam % 2
    index = lax.broadcasted_iota(jnp.int32, (owners, chunk), 0)
    side, third = index >> 6, (index >> 4) & 3
    second, first = (index >> 2) & 3, index & 3
    core = side ^ c
    turn = offset(first)
    along = 2 * turn + jnp.where(third == 2, 3, jnp.where(third == 3, 1, 0))
    up = turn + jnp.where(third == 1, jnp.where(core == 0, 3, 1), 0)
    dx = jnp.where(core == 0, offset(second), along)
    dy = jnp.where(core == 0, along, offset(second))
    return ((((y + dy) & 3) << 2) + ((x + dx) & 3)) * 8 + ((z + up) & 3) * 2 + core


def rank_kernel(owner_ref, slot_ref):
    table = slot_owners()
    row = lax.broadcasted_iota(jnp.int32, (chunk, chunk + owners), 0)
    col = lax.broadcasted_iota(jnp.int32, (chunk, chunk + owners), 1)
    earlier = jnp.where((row < col) | (col >= chunk), 1.0, 0.0).astype(jnp.bfloat16)
    start = cap * lax.broadcasted_iota(jnp.int32, (owners, owners), 0).astype(jnp.float32)
    for j in range(0, rows, chunk):
        hit = table == owner_ref[:, j : j + chunk]
        count = jnp.dot(
            jnp.where(hit, 1.0, 0.0).astype(jnp.bfloat16), earlier, preferred_element_type=jnp.float32
        )
        place = count[:, :chunk] + jnp.concatenate([start, start], axis=1)
        slot = jnp.sum(jnp.where(hit, place, 0.0), axis=0, keepdims=True)
        slot_ref[:, j : j + chunk] = slot.astype(jnp.int32)
        start = start + count[:, chunk:]


def rank(owner):
    return pl.pallas_call(
        rank_kernel,
        out_shape=jax.ShapeDtypeStruct((1, rows), jnp.int32),
        compiler_params=params(),
        cost_estimate=pl.CostEstimate(flops=2 * 128 * 4096 * 384, bytes_accessed=100000, transcendentals=0),
    )(owner)


def sort_kernel(slot_ref, field_ref, near_ref, own_ref, side_ref, plus_ref, minus_ref, wide, placed):
    wide[...] = field_ref[...].astype(jnp.float32)

    def body(i, carry):
        first = pl.multiple_of(i * unroll, unroll)
        for j in range(unroll):
            placed[pl.ds(slot_ref[first + j], 1), :] = wide[pl.ds(first + j, 1), :]
        return carry

    lax.fori_loop(0, rows // unroll, body, 0)
    near_ref[...] = placed[:half].astype(jnp.bfloat16)
    for third, far_ref in enumerate((own_ref, side_ref, plus_ref, minus_ref)):
        lo = half + third * block
        far_ref[...] = placed[lo : lo + block].astype(jnp.bfloat16)


def sort_rows(slot, field):
    return pl.pallas_call(
        sort_kernel,
        in_specs=[pl.BlockSpec(memory_space=pltpu.SMEM), in_vmem],
        out_specs=[in_vmem] * 5,
        out_shape=[
            jax.ShapeDtypeStruct((count * block, vals), jnp.bfloat16) for count in (4, 1, 1, 1, 1)
        ],
        scratch_shapes=[pltpu.VMEM((rows, vals), jnp.float32), pltpu.VMEM((slots, vals), jnp.float32)],
        compiler_params=params(),
        cost_estimate=pl.CostEstimate(flops=0, bytes_accessed=20000000, transcendentals=0),
    )(slot, field)


def halo(choice, own_ref, next_ref, label):
    def ends(ref, second):
        top = second * stride + group
        return ref[top : top + 16, :].astype(jnp.float32)

    nothing = jnp.zeros((16, vals), jnp.float32)
    across = jnp.where(choice == 2, ends(next_ref, 0), nothing)
    corner = jnp.where(choice == 1, ends(next_ref, label), across)
    return jnp.where(choice == 0, ends(own_ref, label), corner).astype(jnp.bfloat16)


def ends_kernel(own_ref, before_ref, after_ref, coupling_ref, plane_ref, out_ref):
    plane = plane_ref[...]
    sub, lam = lax.axis_index("sub"), lax.axis_index("lam")
    x, inner = sub % 4, jnp.where(lam % 2 == 0, 0, 2)
    choice = jnp.where(sub == 0, 3, jnp.where(x == 0, 1, inner))
    before = halo(choice, own_ref, before_ref, 2)
    choice = jnp.where(sub == 15, 3, jnp.where(x == 3, 1, inner))
    after = halo(choice, own_ref, after_ref, 1)
    before = jnp.dot(before, plane, preferred_element_type=jnp.float32)[15:16]
    after = jnp.dot(after, plane, preferred_element_type=jnp.float32)[0:1]
    out_ref[0:1, :] = step_size * coupling_ref[0:1, 0:1] * before
    out_ref[1:2, :] = step_size * coupling_ref[31:32, 127:128] * after


def end_terms(own, before, after, coupling, plane):
    return pl.pallas_call(
        ends_kernel,
        in_specs=[in_vmem] * 5,
        out_specs=in_vmem,
        out_shape=jax.ShapeDtypeStruct((8, vals), jnp.float32),
        compiler_params=params(),
        cost_estimate=pl.CostEstimate(flops=1000, bytes_accessed=1000, transcendentals=0),
    )(own, before, after, coupling, plane)


def stencil_kernel(field_ref, coupling_ref, plane_ref, base_ref, projected):
    plane = plane_ref[...]
    projected[0:8, :] = jnp.zeros((8, vals), jnp.float32)
    projected[rows + 8 : rows + 16, :] = jnp.zeros((8, vals), jnp.float32)
    for j in range(rows // 512):
        projected[8 + j * 512 : 8 + (j + 1) * 512, :] = jnp.dot(
            field_ref[j * 512 : (j + 1) * 512, :], plane, preferred_element_type=jnp.float32
        )
    for j in range(rows // vals):
        lo = j * vals
        weight = jnp.broadcast_to(coupling_ref[j : j + 1, :], (vals, vals)).T
        here = projected[lo + 8 : lo + 8 + vals, :]
        before = projected[lo + 7 : lo + 7 + vals, :]
        after = projected[lo + 9 : lo + 9 + vals, :]
        field = field_ref[lo : lo + vals, :].astype(jnp.float32)
        base_ref[lo : lo + vals, :] = field - step_size * (weight * (2.0 * here - before - after))


def stencil(field, coupling, plane):
    return pl.pallas_call(
        stencil_kernel,
        in_specs=[in_vmem] * 3,
        out_specs=in_vmem,
        out_shape=jax.ShapeDtypeStruct((rows, vals), jnp.float32),
        scratch_shapes=[pltpu.VMEM((rows + 16, vals), jnp.float32)],
        compiler_params=params(),
        cost_estimate=pl.CostEstimate(flops=1000, bytes_accessed=1000, transcendentals=0),
    )(field, coupling, plane)


def respond(block, operator):
    response = jnp.dot(block, operator, preferred_element_type=jnp.float32)
    square = response * response
    magnitude = square + pltpu.roll(square, vals // 2, 1)
    reluct = 5.0 - 4.0 / (1.0 + magnitude)
    return reluct * response


def effect_kernel(sources, places, *refs):
    operators, out_ref = refs[: len(sources)], refs[-1]
    for (number, source), place, operator_ref in zip(sources, places, operators):
        rows_ref = refs[len(sources) + number]
        for k in range(16):
            top = k // 4 * stride + k % 4 * vals
            lo, out = source * block + k * cap, place * block + k * cap
            effect = respond(rows_ref[lo : lo + cap, :], operator_ref[top : top + vals, :])
            out_ref[out : out + cap, :] = effect.astype(out_ref.dtype)


def effect_call(operands, sources, places, shape, dtype, aliases):
    return pl.pallas_call(
        functools.partial(effect_kernel, sources, places),
        in_specs=[in_vmem] * len(operands),
        out_specs=in_vmem,
        out_shape=jax.ShapeDtypeStruct((shape, vals), dtype),
        input_output_aliases=aliases,
        compiler_params=params(),
        cost_estimate=pl.CostEstimate(flops=1000, bytes_accessed=1000, transcendentals=0),
    )(*operands)


def replies(operators, guests):
    count = len(guests)
    sources = [(number, 0) for number in range(count)]
    return effect_call([*operators, *guests], sources, range(count), count * block, jnp.bfloat16, {})


def own_reply_kernel(operator_ref, guest_ref, *out_refs):
    for k in range(16):
        top = k // 4 * stride + k % 4 * vals
        lo, out = k * cap, k % 8 * cap
        effect = respond(guest_ref[lo : lo + cap, :], operator_ref[top : top + vals, :])
        out_refs[k // 8][out : out + cap, :] = effect.astype(jnp.bfloat16)


def own_replies(operator, guest):
    return pl.pallas_call(
        own_reply_kernel,
        in_specs=[in_vmem] * 2,
        out_specs=[in_vmem] * 2,
        out_shape=[jax.ShapeDtypeStruct((block // 2, vals), jnp.bfloat16)] * 2,
        compiler_params=params(),
        cost_estimate=pl.CostEstimate(flops=1000, bytes_accessed=1000, transcendentals=0),
    )(operator, guest)


def effects(near, operators, thirds, previous):
    operands = [*operators, near]
    aliases = {}
    if previous is not None:
        aliases = {len(operands): 0}
        operands.append(previous)
    sources = [(0, third) for third in thirds]
    return effect_call(operands, sources, thirds, slots, jnp.float32, aliases)


part_tops = (0, 1024, 2048, 3072, 3584, 3840, rows)


def final_kernel(
    slot_ref, base_ref, ends_ref, own_ref, rest_ref, trio_ref, _, out_ref, effect_ref, result, sent
):
    effect_ref[half : half + block // 2, :] = own_ref[...].astype(jnp.float32)
    effect_ref[half + block // 2 : half + block, :] = rest_ref[...].astype(jnp.float32)
    effect_ref[half + block : half + 2 * block, :] = trio_ref[:block].astype(jnp.float32)
    effect_ref[half + 2 * block : half + 3 * block, :] = trio_ref[2 * block :].astype(jnp.float32)
    effect_ref[half + 3 * block :, :] = trio_ref[block : 2 * block].astype(jnp.float32)

    copies = []
    for number, (top, end) in enumerate(zip(part_tops, part_tops[1:])):

        def body(i, carry):
            first = pl.multiple_of(top + i * long_unroll, long_unroll)
            for j in range(long_unroll):
                effect = effect_ref[pl.ds(slot_ref[first + j], 1), :]
                row = pl.ds(first + j, 1)
                result[row, :] = base_ref[row, :] - step_size * effect
            return carry

        lax.fori_loop(0, (end - top) // long_unroll, body, 0)
        if top == 0:
            result[0:1, :] = result[0:1, :] + ends_ref[0:1, :]
        if end == rows:
            result[rows - 1 : rows, :] = result[rows - 1 : rows, :] + ends_ref[1:2, :]
        span = slice(top, end)
        copies.append(pltpu.make_async_copy(result.at[span], out_ref.at[span], sent.at[number]))
        copies[-1].start()
    for copy in copies:
        copy.wait()


def finish(slot, base, ends, returned, effect):
    operands = [slot, base, ends, *returned, effect]
    return pl.pallas_call(
        final_kernel,
        in_specs=[pl.BlockSpec(memory_space=pltpu.SMEM)] + [in_vmem] * (len(operands) - 1),
        out_specs=[pl.BlockSpec(memory_space=pl.ANY), in_vmem],
        out_shape=[
            jax.ShapeDtypeStruct((rows, vals), jnp.float32),
            jax.ShapeDtypeStruct((slots, vals), jnp.float32),
        ],
        input_output_aliases={len(operands) - 1: 1},
        scratch_shapes=[
            pltpu.VMEM((rows, vals), jnp.float32),
            pltpu.SemaphoreType.DMA((len(part_tops) - 1,)),
        ],
        compiler_params=params(),
        cost_estimate=pl.CostEstimate(flops=4096 * 128, bytes_accessed=10000000, transcendentals=0),
    )(*operands)[0]


def per_device(edge_field, coupling, owner_map, in_plane, profile_op):
    field = edge_field[0]
    tied = lax.optimization_barrier
    tips = jnp.concatenate([field[:8], field[rows - 8 :]], axis=0)
    near = jnp.concatenate([*around(profile_op[0], first_moves), tips], axis=0)
    slot = rank(owner_map.transpose(0, 2, 1)[0]).reshape(rows)
    near, slot = tied((near, slot))
    plane = jnp.concatenate(around(near, second_moves), axis=0)
    near_rows, *far_rows = sort_rows(slot, field)
    plane, near_rows, *far_rows = tied((plane, near_rows, *far_rows))
    plus, minus = shifted(plane, third_moves), shifted(plane, scaled(third_moves, -1))
    side = shifted(plane, side_moves)
    own_guest, side_guest, *pair_guests = [core_swap(part) for part in far_rows]
    weights = coupling.reshape(rows // vals, vals)
    base = stencil(field, weights, in_plane)
    effect = effects(near_rows, [plane], (0,), None)
    reply = [core_swap(part) for part in own_replies(plane, own_guest)]
    effect, base, reply, guests = tied((effect, base, reply, [side_guest, *pair_guests]))
    side_guest, *pair_guests = guests
    plus, minus, side, effect, base, reply = tied((plus, minus, side, effect, base, reply))
    returned = [*reply]
    returned.append(core_swap(replies([side, minus, plus], [side_guest, *reversed(pair_guests)])))
    effect = effects(near_rows, [side, plus, minus], (1, 2, 3), effect)
    ends = end_terms(plane, plus, minus, weights, in_plane)
    return finish(slot, base, ends, returned, effect)[None]


def solution(mesh):
    placed = (
        P("lam", "sub", None),
        P("lam", "sub"),
        P("lam", "sub", None),
        P(),
        P(("sub", "lam"), None, None),
    )
    return jax.shard_map(
        per_device, mesh=mesh, in_specs=placed, out_specs=P("lam", "sub", None), check_vma=False
    )
```
